32 devices in a mesh: dp: 4 (over y, x), tensor: 8 (over z, core).
Axes of the slice: x: 2, y: 2, z: 4, core: 2. Of those that a mesh axis runs over, the one named last changes fastest.
Arguments:
- tokens: bfloat16 [8, 1024, 2048], P('dp', 'tensor'), may hold values from -6 to 6
- cotangent: bfloat16 [8, 1024, 2048], P('dp', 'tensor'), may hold values from -6 to 6
- segments: int32 [8, 1024], P('dp'), may hold values from 0 to 5, never falling along the last dimension, each value on 1 to 640 neighbouring positions
- valid_mask: int32 [8, 1024], P('dp'), may hold values 0 or 1
- norm_params: float32 [2, 2048], replicated, may hold values from 0.5 to 1.5
- norm_moments: float32 [2, 2, 2048], replicated, may hold values from 0.0001 to 0.01
- heads_weight: float32 [3, 2048, 2048], P(None, 'dp', 'tensor'), may hold values from -0.125 to 0.125
- heads_moments: float32 [2, 3, 2048, 2048], P(None, None, 'dp', 'tensor'), may hold values from 0.0001 to 0.01
- heads_bias: float32 [3, 2048], P(None, 'tensor'), may hold values from -3 to 3
- heads_bias_moments: float32 [2, 3, 2048], P(None, None, 'tensor'), may hold values from 0.0001 to 0.01
- merge_weight: float32 [2048, 2048], P('tensor', 'dp'), may hold values from -0.5 to 0.5
- merge_moments: float32 [2, 2048, 2048], P(None, 'tensor', 'dp'), may hold values from 0.0001 to 0.01
- expand_weight: float32 [2048, 8192], P('dp', 'tensor'), may hold values from -0.125 to 0.125
- expand_moments: float32 [2, 2048, 8192], P(None, 'dp', 'tensor'), may hold values from 0.0001 to 0.01
- expand_bias: float32 [8192], P('tensor'), may hold values from -3 to 3
- expand_bias_moments: float32 [2, 8192], P(None, 'tensor'), may hold values from 0.0001 to 0.01
- shrink_weight: float32 [8192, 2048], P('tensor', 'dp'), may hold values from -0.0625 to 0.0625
- shrink_moments: float32 [2, 8192, 2048], P(None, 'tensor', 'dp'), may hold values from 0.0001 to 0.01
- output_bias: float32 [2, 2048], replicated, may hold values from -2 to 2
- output_bias_moments: float32 [2, 2, 2048], replicated, may hold values from 0.0001 to 0.01
Outputs:
- output: bfloat16 [8, 1024, 2048], P('dp', 'tensor')
- input_grad: bfloat16 [8, 1024, 2048], P('dp', 'tensor')
- norm_params_update: float32 [2, 2048], replicated
- norm_moments_new: float32 [2, 2, 2048], replicated
- heads_weight_update: float32 [3, 2048, 2048], P(None, 'dp', 'tensor')
- heads_moments_new: float32 [2, 3, 2048, 2048], P(None, None, 'dp', 'tensor')
- heads_bias_update: float32 [3, 2048], P(None, 'tensor')
- heads_bias_moments_new: float32 [2, 3, 2048], P(None, None, 'tensor')
- merge_weight_update: float32 [2048, 2048], P('tensor', 'dp')
- merge_moments_new: float32 [2, 2048, 2048], P(None, 'tensor', 'dp')
- expand_weight_update: float32 [2048, 8192], P('dp', 'tensor')
- expand_moments_new: float32 [2, 2048, 8192], P(None, 'dp', 'tensor')
- expand_bias_update: float32 [8192], P('tensor')
- expand_bias_moments_new: float32 [2, 8192], P(None, 'tensor')
- shrink_weight_update: float32 [8192, 2048], P('tensor', 'dp')
- shrink_moments_new: float32 [2, 8192, 2048], P(None, 'tensor', 'dp')
- output_bias_update: float32 [2, 2048], replicated
- output_bias_moments_new: float32 [2, 2, 2048], replicated
The draws below stay inside these ranges and needn't reach their ends.
Inputs may be any that keep to these rules, and one draw needn't show every extreme that they name: In each sequence the segments numbers never fall; a document has at most 640 tokens, and one has exactly that many.
All inputs are finite; a program needn't handle non-finite values. No bound on the sum of `valid_mask` on one device may be relied on, other than what follows from the above.
Results may differ from the reference program's by a relative error of at most 0.02.
Values may be sent and summed in bfloat16 or wider, within the bound.
No kernel may reach another device: no remote copies, remote signals or barrier semaphores. Data moves between devices by JAX's collectives and lax.ppermute only.
A program may use at most 256 MiB of HBM per device.

```python
import math
import jax
import jax.numpy as jnp
import numpy as np
from jax import lax

D = 2048
HEADS = 32
HEAD_DIM = 64
ROT = 32
FF = 8192
SEQ = 1024
STEP = 5
SEQS = 8


def with_ends(values, own_key, low, largest):
    longest = values.shape.index(max(values.shape))
    spots = []
    for shift in (0, 1):
        where = [jax.random.randint(jax.random.fold_in(own_key, axis), (), 0, length) for axis, length in enumerate(values.shape)]
        where[longest] = (where[longest] + shift) % values.shape[longest]
        spots.append(tuple(where))
    return values.at[spots[0]].set(low).at[spots[1]].set(largest)


def steps_of(rng, dims, cuts, smallest, largest):
    def one(axis_at, blocks):
        heights = jax.random.uniform(jax.random.fold_in(jax.random.fold_in(rng, 6), axis_at), (blocks,), jnp.float32, smallest / len(cuts), largest / len(cuts))
        return jnp.repeat(jnp.exp(heights), dims[axis_at] // blocks).reshape((-1,) + (1,) * (len(dims) - axis_at - 1))

    factor_of = one(*cuts[0])
    for cut in cuts[1:]:
        factor_of = factor_of * one(*cut)
    return factor_of


def length_profile(count, total, limit, skew):
    portions = [(1 << 20) // math.isqrt(standing ** skew) + 1 for standing in range(2, count + 1)]
    spare, holding = total - limit - (count - 1), [1] * (count - 1)
    while spare > 0:
        movable = [i for i in range(count - 1) if holding[i] < limit]
        whole, budget = sum([portions[i] for i in movable]), spare
        for i in movable:
            extra = min(limit - holding[i], max(1, budget * portions[i] // whole), spare)
            holding[i] = holding[i] + extra
            spare = spare - extra
    return np.array([limit] + holding)


def uneven_parts(stream_key, number_of, total, most, slope):
    if number_of == 2:
        one = jax.random.randint(stream_key, (), max(1, total - most), min(most, total - 1) + 1)
        return jnp.stack([one, total - one])
    sizes = jnp.asarray(length_profile(number_of, total, most, slope), jnp.int32)
    couples = (number_of - 1) // 2
    donor, taker = sizes[1:1 + 2 * couples:2], sizes[2:2 + 2 * couples:2]
    room = jnp.minimum(donor - 1, most - taker)
    moved = jax.random.randint(jax.random.fold_in(stream_key, 1), (couples,), 0, 1 << 20) % (room + 1)
    sizes = sizes.at[1:1 + 2 * couples:2].set(donor - moved).at[2:2 + 2 * couples:2].set(taker + moved)
    return sizes[jax.random.permutation(jax.random.fold_in(stream_key, 2), number_of)]


def bell_draw(rng, extent, width, limit, split=(), kind=jnp.bfloat16):
    entries = width * jax.random.normal(rng, extent, jnp.float32)
    if split:
        entries = entries * steps_of(rng, extent, split, -0.22, 0.18)
    return jnp.clip(entries, -limit, limit).astype(kind)


def setup_inputs(seed: int = 0) -> dict:
    keys = jax.random.split(jax.random.key(seed), 21)
    return {
        "tokens": bell_draw(keys[0], (SEQS, SEQ, D), 1.0, 6.0, ((0, 4), (1, 8))),
        "cotangent": bell_draw(keys[1], (SEQS, SEQ, D), 1.0, 6.0, ((0, 4), (1, 8))),
        "segments": jax.vmap(lambda own: jnp.searchsorted(jnp.cumsum(uneven_parts(own, SEQ // 256 + 2, SEQ, SEQ // 2 + SEQ // 8, 0)), jnp.arange(SEQ), side="right"))(jax.random.split(keys[2], SEQS)).reshape((SEQS, SEQ)).astype(jnp.int32),
        "valid_mask": with_ends((jax.random.randint(keys[3], (SEQS, SEQ), 0, 20) < 19).astype(jnp.int32), jax.random.fold_in(keys[3], 1), 0, 1),
        "norm_params": jnp.clip(jax.random.uniform(keys[4], (2, D), jnp.float32, 0.5, 1.5), 0.5, 1.5),
        "norm_moments": jnp.clip(jnp.exp(jax.random.uniform(keys[5], (2, 2, D), jnp.float32, math.log(0.0001), math.log(0.01))), 0.0001, 0.01),
        "heads_weight": bell_draw(keys[6], (3, D, D), D ** -0.5, 0.125, ((1, 4), (2, 8)), jnp.float32),
        "heads_moments": jnp.clip(jnp.exp(math.log(0.01) - 4.6051702 * jax.random.uniform(keys[7], (2, 3, D, D), jnp.float32) ** steps_of(keys[7], (2, 3, D, D), ((2, 4), (3, 8)), -0.2, 0.2)), 0.0001, 0.01),
        "heads_bias": bell_draw(keys[8], (3, D), 0.5, 3.0, ((1, 8),), jnp.float32),
        "heads_bias_moments": jnp.clip(jnp.exp(math.log(0.01) - 4.6051702 * jax.random.uniform(keys[9], (2, 3, D), jnp.float32) ** steps_of(keys[9], (2, 3, D), ((2, 8),), -0.2, 0.2)), 0.0001, 0.01),
        "merge_weight": bell_draw(keys[10], (D, D), (D // 16) ** -0.5, 0.5, ((0, 8), (1, 4)), jnp.float32),
        "merge_moments": jnp.clip(jnp.exp(math.log(0.01) - 4.6051702 * jax.random.uniform(keys[11], (2, D, D), jnp.float32) ** steps_of(keys[11], (2, D, D), ((1, 8), (2, 4)), -0.2, 0.2)), 0.0001, 0.01),
        "expand_weight": bell_draw(keys[12], (D, FF), D ** -0.5, 0.125, ((0, 4), (1, 8)), jnp.float32),
        "expand_moments": jnp.clip(jnp.exp(math.log(0.01) - 4.6051702 * jax.random.uniform(keys[13], (2, D, FF), jnp.float32) ** steps_of(keys[13], (2, D, FF), ((1, 4), (2, 8)), -0.2, 0.2)), 0.0001, 0.01),
        "expand_bias": bell_draw(keys[14], (FF,), 0.5, 3.0, ((0, 8),), jnp.float32),
        "expand_bias_moments": jnp.clip(jnp.exp(math.log(0.01) - 4.6051702 * jax.random.uniform(keys[15], (2, FF), jnp.float32) ** steps_of(keys[15], (2, FF), ((1, 8),), -0.2, 0.2)), 0.0001, 0.01),
        "shrink_weight": bell_draw(keys[16], (FF, D), FF ** -0.5, 0.0625, ((0, 8), (1, 4)), jnp.float32),
        "shrink_moments": jnp.clip(jnp.exp(math.log(0.01) - 4.6051702 * jax.random.uniform(keys[17], (2, FF, D), jnp.float32) ** steps_of(keys[17], (2, FF, D), ((1, 8), (2, 4)), -0.2, 0.2)), 0.0001, 0.01),
        "output_bias": bell_draw(keys[18], (2, D), 0.3, 2.0, (), jnp.float32),
        "output_bias_moments": jnp.clip(jnp.exp(jax.random.uniform(keys[19], (2, 2, D), jnp.float32, math.log(0.0001), math.log(0.01))), 0.0001, 0.01),
    }


@jax.custom_vjp
def low(v):
    return lax.optimization_barrier(v.astype(jnp.bfloat16)).astype(jnp.float32)

@jax.custom_vjp
def low_back(v):
    return v

def low_keep(v):
    return (low(v), None)

def low_pass(kept, grad):
    return (grad,)

def back_keep(v):
    return (v, None)

def back_low(kept, grad):
    return (low(grad),)
low.defvjp(low_keep, low_pass)
low_back.defvjp(back_keep, back_low)
norm_eps = 1e-05
beta_first = 0.9
beta_second = 0.95
adam_eps = 1e-08
masked_score = -1000000000.0
highest = lax.Precision.HIGHEST

def rotary_tables(segment):
    token_index = jnp.arange(segment.shape[0], dtype=jnp.int32)
    doc_begins = jnp.concatenate([jnp.ones((1,), dtype=jnp.bool_), segment[1:] != segment[:-1]])
    doc_start = lax.cummax(jnp.where(doc_begins, token_index, 0), axis=0)
    positions = (token_index - doc_start).astype(jnp.float32)
    frequency = jnp.power(10000.0, -2.0 * jnp.arange(ROT // 2, dtype=jnp.float32) / ROT)
    angles = positions[:, None] * frequency[None, :]
    return (jnp.cos(angles), jnp.sin(angles))

def rotate(values, cosine_table, sine_table):
    half_rot = ROT // 2
    leading = values[..., :half_rot]
    trailing = values[..., half_rot:ROT]
    cosine_rows = cosine_table[:, None, :]
    sine_rows = sine_table[:, None, :]
    return jnp.concatenate([leading * cosine_rows - trailing * sine_rows, trailing * cosine_rows + leading * sine_rows, values[..., ROT:]], axis=-1)

def allowed_mask(segment, valid, start, rows_count):
    query_index = start + jnp.arange(rows_count, dtype=jnp.int32)
    key_index = jnp.arange(segment.shape[0], dtype=jnp.int32)
    query_segment = lax.dynamic_slice_in_dim(segment, start, rows_count, 0)
    same_doc = query_segment[:, None] == segment[None, :]
    causal = key_index[None, :] <= query_index[:, None]
    diagonal = key_index[None, :] == query_index[:, None]
    return same_doc & causal & ((valid[None, :] > 0) | diagonal)

def block_forward(params, inputs, segment, valid):
    norm_params, heads_weight, heads_bias, merge_weight, expand_weight, expand_bias, shrink_weight, output_bias = params
    seq_len = inputs.shape[0]
    row_mean = lax.optimization_barrier(jnp.mean(inputs, axis=-1, keepdims=True))
    centred = inputs - row_mean
    variance = lax.optimization_barrier(jnp.mean(centred * centred, axis=-1, keepdims=True))
    normed = low(centred * lax.rsqrt(variance + norm_eps) * norm_params[0] + norm_params[1])
    triple = jnp.einsum('sd,tdf->tsf', normed, low(heads_weight), precision=highest) + heads_bias[:, None, :]
    cosine_table, sine_table = rotary_tables(segment)
    shaped = (seq_len, HEADS, HEAD_DIM)
    queries = low(rotate(low_back(triple[0]).reshape(shaped), cosine_table, sine_table))
    keys_rot = low(rotate(low_back(triple[1]).reshape(shaped), cosine_table, sine_table))
    values_low = low(low_back(triple[2])).reshape(shaped)
    block_rows = min(512, seq_len)
    block_count = seq_len // block_rows
    block_starts = jnp.arange(block_count, dtype=jnp.int32) * block_rows
    query_blocks = queries.reshape(block_count, block_rows, HEADS, HEAD_DIM)

    def attend(block_item):
        query_block, start = block_item
        raw = jnp.einsum('qhd,khd->hqk', query_block, keys_rot, precision=highest)
        scores = HEAD_DIM ** (-0.5) * low_back(raw)
        scores = jnp.where(allowed_mask(segment, valid, start, block_rows)[None], scores, masked_score)
        row_max = lax.optimization_barrier(jnp.max(scores, axis=-1, keepdims=True))
        exponentials = jnp.exp(scores - row_max)
        probs = exponentials / lax.optimization_barrier(jnp.sum(exponentials, axis=-1, keepdims=True))
        return jnp.einsum('hqk,khd->qhd', low(probs), values_low, precision=highest)
    attended = lax.map(jax.checkpoint(attend), (query_blocks, block_starts)).reshape(seq_len, HEADS * HEAD_DIM)
    attended = low(low_back(attended))
    hidden_pre = jnp.dot(normed, low(expand_weight), precision=highest) + expand_bias
    hidden = low(jax.nn.gelu(low_back(hidden_pre), approximate=True))
    branch_attn = jnp.dot(attended, low(merge_weight), precision=highest) + output_bias[0]
    branch_mlp = jnp.dot(hidden, low(shrink_weight), precision=highest) + output_bias[1]
    return inputs + branch_attn + branch_mlp

def adam_update(moments, gradient, first_fix, second_fix):
    moment_one = beta_first * moments[0] + (1.0 - beta_first) * gradient
    moment_two = beta_second * moments[1] + (1.0 - beta_second) * gradient * gradient
    scaled_step = moment_one / first_fix / (jnp.sqrt(moment_two / second_fix) + adam_eps)
    return (scaled_step, jnp.stack([moment_one, moment_two]))

def reference(tokens, cotangent, segments, valid_mask, norm_params, norm_moments, heads_weight, heads_moments, heads_bias, heads_bias_moments, merge_weight, merge_moments, expand_weight, expand_moments, expand_bias, expand_bias_moments, shrink_weight, shrink_moments, output_bias, output_bias_moments):
    params = (norm_params, heads_weight, heads_bias, merge_weight, expand_weight, expand_bias, shrink_weight, output_bias)

    def per_sequence(totals, seq_entry):
        seq_rows, seq_cot, seq_segment, seq_valid = seq_entry

        def forward(weights, inputs):
            return block_forward(weights, inputs, seq_segment, seq_valid)
        result, pullback = jax.vjp(forward, params, seq_rows.astype(jnp.float32))
        gradients, row_grad = pullback(seq_cot.astype(jnp.float32))
        totals = jax.tree.map(jnp.add, totals, gradients)
        return (totals, (result.astype(jnp.bfloat16), row_grad.astype(jnp.bfloat16)))
    zeros_tree = jax.tree.map(jnp.zeros_like, params)
    totals, (output, input_grad) = lax.scan(per_sequence, zeros_tree, (tokens, cotangent, segments, valid_mask))
    scale_back = 1.0 / tokens.shape[1]
    gradients = jax.tree.map(lambda summed: summed * scale_back, totals)
    first_fix = 1.0 - beta_first ** STEP
    second_fix = 1.0 - beta_second ** STEP
    norm_upd, norm_mom = adam_update(norm_moments, gradients[0], first_fix, second_fix)
    heads_upd, heads_mom = adam_update(heads_moments, gradients[1], first_fix, second_fix)
    hbias_upd, hbias_mom = adam_update(heads_bias_moments, gradients[2], first_fix, second_fix)
    merge_upd, merge_mom = adam_update(merge_moments, gradients[3], first_fix, second_fix)
    expand_upd, expand_mom = adam_update(expand_moments, gradients[4], first_fix, second_fix)
    ebias_upd, ebias_mom = adam_update(expand_bias_moments, gradients[5], first_fix, second_fix)
    shrink_upd, shrink_mom = adam_update(shrink_moments, gradients[6], first_fix, second_fix)
    obias_upd, obias_mom = adam_update(output_bias_moments, gradients[7], first_fix, second_fix)
    return (output, input_grad, norm_upd, norm_mom, heads_upd, heads_mom, hbias_upd, hbias_mom, merge_upd, merge_mom, expand_upd, expand_mom, ebias_upd, ebias_mom, shrink_upd, shrink_mom, obias_upd, obias_mom)
```

```python
import jax
import jax.numpy as jnp
from jax import lax
from jax.experimental import pallas as pl
from jax.experimental.pallas import tpu as pltpu
from jax.sharding import PartitionSpec as P

HEAD_DIM = 64
ROT = 32
STEP = 5
LANES = 128

norm_eps = 1e-05
beta_first = 0.9
beta_second = 0.95
adam_eps = 1e-08
masked_score = -1000000000.0
score_scale = HEAD_DIM ** (-0.5)

f32 = jnp.float32
bf16 = jnp.bfloat16


def document_starts(segment):
    token_index = jnp.arange(segment.shape[0], dtype=jnp.int32)
    doc_begins = jnp.concatenate([jnp.ones((1,), dtype=jnp.bool_), segment[1:] != segment[:-1]])
    return lax.cummax(jnp.where(doc_begins, token_index, 0), axis=0)


def rotary_tables(doc_start):
    seq_len = doc_start.shape[0]
    positions = (jnp.arange(seq_len, dtype=jnp.int32) - doc_start).astype(f32)
    frequency = jnp.power(10000.0, -2.0 * jnp.arange(ROT // 2, dtype=f32) / ROT)
    angles = positions[:, None] * frequency[None, :]
    cosine, sine = jnp.cos(angles), jnp.sin(angles)
    rest = HEAD_DIM - ROT
    cosine = jnp.concatenate([cosine, cosine, jnp.ones((seq_len, rest), f32)], axis=1)
    sine = jnp.concatenate([-sine, sine, jnp.zeros((seq_len, rest), f32)], axis=1)
    copies = LANES // HEAD_DIM
    return jnp.tile(cosine, (1, copies)), jnp.tile(sine, (1, copies))


def masks(doc_start, valid):
    index = jnp.arange(doc_start.shape[0], dtype=jnp.int32)

    def build(query, start, key, key_valid):
        allowed = (key >= start) & (key <= query) & ((key_valid > 0) | (key == query))
        return jnp.where(allowed, 0.0, masked_score).astype(bf16)

    rows = build(index[:, None], doc_start[:, None], index[None, :], valid[None, :])
    columns = build(index[None, :], doc_start[None, :], index[:, None], valid[:, None])
    return rows, columns


def rotate(values, cosine, sine):
    half_rot = ROT // 2
    width = values.shape[1]
    lane = lax.broadcasted_iota(jnp.int32, values.shape, 1) % HEAD_DIM
    ahead = pltpu.roll(values, width - half_rot, 1)
    behind = pltpu.roll(values, half_rot, 1)
    partner = jnp.where(lane < half_rot, ahead, behind)
    return values * cosine + partner * sine


def nt(left, right):
    return lax.dot_general(left, right, (((1,), (1,)), ((), ())), preferred_element_type=f32)


def nn(left, right):
    return lax.dot_general(left, right, (((1,), (0,)), ((), ())), preferred_element_type=f32)


def tn(left, right):
    return lax.dot_general(left, right, (((0,), (0,)), ((), ())), preferred_element_type=f32)


def widen(table, width):
    return jnp.concatenate([table] * (width // LANES), axis=1)


def attend_kernel(
    low_ref, triple_ref, bias_ref, cos_ref, sin_ref, mask_ref, qkv_ref, out_ref, lse_ref, k_all, v_all
):
    step = pl.program_id(0)
    rows, width = out_ref.shape
    heads = width // HEAD_DIM
    blocks = k_all.shape[0] // rows
    cosine = widen(cos_ref[...], width)
    sine = widen(sin_ref[...], width)
    query = rotate(triple_ref[:, :width] + bias_ref[0:1, :], cosine, sine).astype(bf16)
    key = rotate(triple_ref[:, width : 2 * width] + bias_ref[1:2, :], cosine, sine).astype(bf16)
    value = (triple_ref[:, 2 * width :] + bias_ref[2:3, :]).astype(bf16)
    qkv_ref[0] = query
    qkv_ref[1] = key
    qkv_ref[2] = value
    own = pl.ds(pl.multiple_of(step * rows, rows), rows)
    k_all[own, :] = key
    v_all[own, :] = value
    scaled = query * jnp.asarray(score_scale, bf16)
    head_of = lax.broadcasted_iota(jnp.int32, (rows, width), 1) // HEAD_DIM
    lane = lax.broadcasted_iota(jnp.int32, (rows, LANES), 1)
    span = step - low_ref[step] + 1
    for count in range(1, blocks + 1):

        @pl.when(span == count)
        def _(count=count):
            begin = pl.multiple_of((step - (count - 1)) * rows, rows)
            keys = k_all[pl.ds(begin, count * rows), :]
            values = v_all[pl.ds(begin, count * rows), :]
            mask = mask_ref[:, pl.ds(begin, count * rows)].astype(f32)
            result = jnp.zeros((rows, width), f32)
            stats = jnp.zeros((rows, LANES), f32)
            for head in range(heads):
                mine = head_of == head
                scores = nt(jnp.where(mine, scaled, jnp.zeros_like(scaled)), keys) + mask
                top = jnp.max(scores, axis=1, keepdims=True)
                weights = jnp.exp(scores - top)
                total = jnp.sum(weights, axis=1, keepdims=True)
                mixed = nn(weights.astype(bf16), values) * (1.0 / total)
                result = jnp.where(mine, mixed, result)
                stats = jnp.where(lane == head, top + jnp.log(total), stats)
            out_ref[...] = result.astype(bf16)
            lse_ref[...] = jnp.transpose(stats)[: lse_ref.shape[0], :]


def attend(triple, bias, cosine, sine, mask, low, rows):
    seq_len = triple.shape[0]
    width = triple.shape[1] // 3
    blocks = seq_len // rows
    stat_rows = 8
    grid_spec = pltpu.PrefetchScalarGridSpec(
        num_scalar_prefetch=1,
        grid=(blocks,),
        in_specs=[
            pl.BlockSpec((rows, 3 * width), lambda i, low: (i, 0)),
            pl.BlockSpec((3, width), lambda i, low: (0, 0)),
            pl.BlockSpec((rows, LANES), lambda i, low: (i, 0)),
            pl.BlockSpec((rows, LANES), lambda i, low: (i, 0)),
            pl.BlockSpec((rows, seq_len), lambda i, low: (i, 0)),
        ],
        out_specs=[
            pl.BlockSpec((3, rows, width), lambda i, low: (0, i, 0)),
            pl.BlockSpec((rows, width), lambda i, low: (i, 0)),
            pl.BlockSpec((stat_rows, rows), lambda i, low: (0, i)),
        ],
        scratch_shapes=[pltpu.VMEM((seq_len, width), bf16), pltpu.VMEM((seq_len, width), bf16)],
    )
    pairs = seq_len * seq_len * width
    return pl.pallas_call(
        attend_kernel,
        grid_spec=grid_spec,
        out_shape=[
            jax.ShapeDtypeStruct((3, seq_len, width), bf16),
            jax.ShapeDtypeStruct((seq_len, width), bf16),
            jax.ShapeDtypeStruct((stat_rows, seq_len), f32),
        ],
        compiler_params=pltpu.CompilerParams(vmem_limit_bytes=24 * 1024 * 1024),
        cost_estimate=pl.CostEstimate(
            flops=4 * pairs, bytes_accessed=8 * seq_len * seq_len, transcendentals=pairs // HEAD_DIM
        ),
        name="attend",
    )(low, triple, bias, cosine, sine, mask)


def attend_back_kernel(
    low_ref, q_ref, k_ref, v_ref, d_ref, lse_ref, mask_ref, cos_ref, sin_ref, out_ref, sum_ref, dk_all, dv_all
):
    step = pl.program_id(0)
    rows, width = d_ref.shape
    heads = width // HEAD_DIM
    seq_len = dk_all.shape[0]
    blocks = seq_len // rows

    @pl.when(step == 0)
    def _():
        dk_all[...] = jnp.zeros_like(dk_all)
        dv_all[...] = jnp.zeros_like(dv_all)
        sum_ref[...] = jnp.zeros_like(sum_ref)

    scaled = q_ref[0] * jnp.asarray(score_scale, bf16)
    d_out = d_ref[...]
    zero = jnp.zeros_like(d_out)
    head_of = lax.broadcasted_iota(jnp.int32, (rows, width), 1) // HEAD_DIM
    own = pl.ds(pl.multiple_of(step * rows, rows), rows)
    span = step - low_ref[step] + 1
    for count in range(1, blocks + 1):

        @pl.when(span == count)
        def _(count=count):
            begin = pl.multiple_of((step - (count - 1)) * rows, rows)
            reach = pl.ds(begin, count * rows)
            keys = k_ref[0, reach, :]
            values = v_ref[0, reach, :]
            mask = mask_ref[reach, :].astype(f32)
            d_query = jnp.zeros((rows, width), f32)
            probs_side, scores_side, queries_down, d_outs_down = [], [], [], []
            for head in range(heads):
                mine = head_of == head
                query = jnp.where(mine, scaled, zero)
                d_mine = jnp.where(mine, d_out, zero)
                scores = nt(keys, query) + mask
                probs = jnp.exp(scores - lse_ref[head : head + 1, :])
                d_probs = nt(values, d_mine)
                delta = jnp.sum(probs * d_probs, axis=0, keepdims=True)
                d_scores = (probs * (d_probs - delta)).astype(bf16)
                d_query = jnp.where(mine, tn(d_scores, keys), d_query)
                probs_side.append(probs.astype(bf16))
                scores_side.append(d_scores)
                queries_down.append(query)
                d_outs_down.append(d_mine)
            dv_all[reach, :] += nn(
                jnp.concatenate(probs_side, axis=1), jnp.concatenate(d_outs_down, axis=0)
            )
            dk_all[reach, :] += nn(
                jnp.concatenate(scores_side, axis=1), jnp.concatenate(queries_down, axis=0)
            )
            cosine = widen(cos_ref[own, :], width)
            sine = widen(sin_ref[own, :], width)
            low_query = rotate(d_query * score_scale, cosine, -sine).astype(bf16)
            out_ref[own, :width] = low_query
            sum_ref[0:1, :] += jnp.sum(low_query.astype(f32), axis=0, keepdims=True)

    @pl.when(step == blocks - 1)
    def _():
        cosine = widen(cos_ref[...], width)
        sine = widen(sin_ref[...], width)
        low_key = rotate(dk_all[...], cosine, -sine).astype(bf16)
        low_value = dv_all[...].astype(bf16)
        out_ref[:, width : 2 * width] = low_key
        out_ref[:, 2 * width :] = low_value
        sum_ref[1:2, :] = jnp.sum(low_key.astype(f32), axis=0, keepdims=True)
        sum_ref[2:3, :] = jnp.sum(low_value.astype(f32), axis=0, keepdims=True)


def attend_back(qkv, d_out, lse, mask, cosine, sine, low, rows):
    seq_len, width = d_out.shape
    blocks = seq_len // rows
    stat_rows = lse.shape[0]
    grid_spec = pltpu.PrefetchScalarGridSpec(
        num_scalar_prefetch=1,
        grid=(blocks,),
        in_specs=[
            pl.BlockSpec((1, rows, width), lambda i, low: (0, i, 0)),
            pl.BlockSpec((1, seq_len, width), lambda i, low: (1, 0, 0)),
            pl.BlockSpec((1, seq_len, width), lambda i, low: (2, 0, 0)),
            pl.BlockSpec((rows, width), lambda i, low: (i, 0)),
            pl.BlockSpec((stat_rows, rows), lambda i, low: (0, i)),
            pl.BlockSpec((seq_len, rows), lambda i, low: (0, i)),
            pl.BlockSpec((seq_len, LANES), lambda i, low: (0, 0)),
            pl.BlockSpec((seq_len, LANES), lambda i, low: (0, 0)),
        ],
        out_specs=[
            pl.BlockSpec((seq_len, 3 * width), lambda i, low: (0, 0)),
            pl.BlockSpec((8, width), lambda i, low: (0, 0)),
        ],
        scratch_shapes=[pltpu.VMEM((seq_len, width), f32), pltpu.VMEM((seq_len, width), f32)],
    )
    pairs = seq_len * seq_len * width
    return pl.pallas_call(
        attend_back_kernel,
        grid_spec=grid_spec,
        out_shape=[
            jax.ShapeDtypeStruct((seq_len, 3 * width), bf16),
            jax.ShapeDtypeStruct((8, width), f32),
        ],
        compiler_params=pltpu.CompilerParams(vmem_limit_bytes=32 * 1024 * 1024),
        cost_estimate=pl.CostEstimate(
            flops=10 * pairs, bytes_accessed=8 * seq_len * seq_len, transcendentals=pairs // HEAD_DIM
        ),
        name="attend_back",
    )(low, qkv, qkv, qkv, d_out, lse, mask, cosine, sine)


def adam_update(moments, gradient):
    first_fix = 1.0 - beta_first**STEP
    second_fix = 1.0 - beta_second**STEP
    moment_one = beta_first * moments[0] + (1.0 - beta_first) * gradient
    moment_two = beta_second * moments[1] + (1.0 - beta_second) * gradient * gradient
    scaled_step = moment_one / first_fix / (jnp.sqrt(moment_two / second_fix) + adam_eps)
    return (scaled_step, jnp.stack([moment_one, moment_two]))


def swap(array, distance):
    size = lax.axis_size("dp")
    return lax.ppermute(array, "dp", [(i, i ^ distance) for i in range(size)])


def after(array, *others):
    return lax.optimization_barrier((array, *others))[0]


def gather_pieces(own):
    size = lax.axis_size("dp")
    if size != 4:
        return [own] + [swap(own, j) for j in range(1, size)]
    half = own.shape[0] // 2
    near, far = swap(own, 1), swap(own, 2)
    top = swap(near[:half], 2)
    bottom = swap(far[half:], 1)
    return [own, near, far, jnp.concatenate([top, bottom], axis=0)]


def scatter_pieces(pieces):
    size = len(pieces)
    if size != 4:
        total = pieces[0].astype(f32)
        for j in range(1, size):
            total = total + swap(pieces[j], j).astype(f32)
        return total
    half = pieces[0].shape[0] // 2
    top = swap(pieces[3][:half], 1)
    bottom = swap(pieces[3][half:], 2)

    def plus(left, right):
        return (left.astype(f32) + right.astype(f32)).astype(bf16)

    near = swap(jnp.concatenate([pieces[1][:half], plus(pieces[1][half:], bottom)], axis=0), 1)
    far = swap(jnp.concatenate([plus(pieces[2][:half], top), pieces[2][half:]], axis=0), 2)
    return pieces[0].astype(f32) + near.astype(f32) + far.astype(f32)


def body(
    tokens,
    cotangent,
    segments,
    valid_mask,
    norm_params,
    norm_moments,
    heads_weight,
    heads_moments,
    heads_bias,
    heads_bias_moments,
    merge_weight,
    merge_moments,
    expand_weight,
    expand_moments,
    expand_bias,
    expand_bias_moments,
    shrink_weight,
    shrink_moments,
    output_bias,
    output_bias_moments,
):
    ranks = lax.axis_size("dp")
    rank = lax.axis_index("dp")
    count, _, model_width = tokens.shape
    seq_len = segments.shape[1]
    width = heads_weight.shape[2]
    piece = model_width // ranks
    rows = min(256, seq_len)

    def relative(array):
        parts = [
            lax.dynamic_slice_in_dim(array, (rank ^ j) * piece, piece, array.ndim - 1) for j in range(ranks)
        ]
        return jnp.concatenate(parts, axis=-1)

    heads_own = jnp.concatenate([heads_weight[c] for c in range(3)], axis=1).astype(bf16)
    heads_pieces = gather_pieces(heads_own)
    expand_pieces = gather_pieces(after(expand_weight.astype(bf16), heads_pieces[1], heads_pieces[2]))
    merge_pieces = gather_pieces(after(merge_weight.astype(bf16), expand_pieces[1], expand_pieces[2]))
    shrink_pieces = gather_pieces(after(shrink_weight.astype(bf16), merge_pieces[1], merge_pieces[2]))
    heads_full = jnp.concatenate(heads_pieces, axis=0)
    expand_full = jnp.concatenate(expand_pieces, axis=0)
    merge_full = jnp.concatenate(merge_pieces, axis=1)
    shrink_full = jnp.concatenate(shrink_pieces, axis=1)

    norm_rel = relative(norm_params)
    norm_gain, norm_shift = norm_rel[0], norm_rel[1]
    inputs = relative(tokens).astype(f32)
    cot_rows = relative(cotangent)
    row_mean = jnp.mean(inputs, axis=-1, keepdims=True)
    centred = inputs - row_mean
    variance = jnp.mean(centred * centred, axis=-1, keepdims=True)
    inv_std = lax.rsqrt(variance + norm_eps)
    unit = centred * inv_std
    normed_rows = (unit * norm_gain + norm_shift).astype(bf16)

    def gather_rows(array):
        return lax.all_gather(array, "tensor", axis=0, tiled=True)

    def scatter_rows(array):
        return lax.psum_scatter(array, "tensor", scatter_dimension=0, tiled=True)

    normed = [gather_rows(normed_rows[s]) for s in range(count)]
    cot = [gather_rows(after(cot_rows[s], normed_rows)) for s in range(count)]

    starts = [document_starts(segments[s]) for s in range(count)]
    tables = [rotary_tables(start) for start in starts]
    masked = [masks(starts[s], valid_mask[s]) for s in range(count)]
    lows = [start[::rows] // rows for start in starts]

    outs, kept = [], []
    for s in range(count):
        triple = nn(normed[s], heads_full)
        qkv, attended, lse = attend(triple, heads_bias, *tables[s], masked[s][0], lows[s], rows)
        pre = nn(normed[s], expand_full) + expand_bias
        inner = jnp.sqrt(2.0 / jnp.pi).astype(f32) * (pre + 0.044715 * pre * pre * pre)
        tanh = jnp.tanh(inner)
        hidden = (0.5 * pre * (1.0 + tanh)).astype(bf16)
        slope = 0.5 * (1.0 + tanh) + 0.5 * pre * (1.0 - tanh * tanh) * (
            jnp.sqrt(2.0 / jnp.pi).astype(f32) * (1.0 + 3 * 0.044715 * pre * pre)
        )
        hidden, slope = lax.optimization_barrier((hidden, slope.astype(bf16)))
        partial = (nn(attended, merge_full) + nn(hidden, shrink_full)).astype(bf16)
        outs.append(scatter_rows(partial))
        kept.append((qkv, attended, lse, hidden, slope))

    d_cats, d_hiddens, grads, bias_sums, hidden_sums = [], [], [], [], []
    for s in range(count):
        qkv, attended, lse, hidden, slope = kept[s]
        d_attended = nt(cot[s], merge_full).astype(bf16)
        d_cat, sums = attend_back(qkv, d_attended, lse, masked[s][1], *tables[s], lows[s], rows)
        d_hidden = (nt(cot[s], shrink_full) * slope.astype(f32)).astype(bf16)
        hidden_sums.append(jnp.sum(d_hidden.astype(f32), axis=0))
        partial = (nt(d_cat, heads_full) + nt(d_hidden, expand_full)).astype(bf16)
        grads.append(scatter_rows(partial))
        d_cats.append(d_cat)
        d_hiddens.append(d_hidden)
        bias_sums.append(sums[:3])

    normed_all = jnp.concatenate(normed, axis=0)
    cot_all = jnp.concatenate(cot, axis=0)
    d_cat_all = jnp.concatenate(d_cats, axis=0)
    d_hidden_all = jnp.concatenate(d_hiddens, axis=0)
    attended_all = jnp.concatenate([k[1] for k in kept], axis=0)
    hidden_all = jnp.concatenate([k[3] for k in kept], axis=0)

    def columns(array, j):
        return array[:, j * piece : (j + 1) * piece]

    order = list(range(ranks))[::-1]

    def spread(make):
        made = {j: make(j) for j in order}
        return scatter_pieces([made[j] for j in range(ranks)])

    shrink_grad = spread(lambda j: tn(hidden_all, columns(cot_all, j)).astype(bf16))
    merge_grad = spread(lambda j: tn(attended_all, columns(cot_all, j)).astype(bf16))
    expand_grad = spread(lambda j: tn(columns(normed_all, j), d_hidden_all).astype(bf16))
    heads_cat = spread(lambda j: tn(columns(normed_all, j), d_cat_all).astype(bf16))
    heads_grad = jnp.stack([heads_cat[:, c * width : (c + 1) * width] for c in range(3)])

    branches = jnp.stack(outs).astype(f32)
    bias_row = relative(output_bias[0] + output_bias[1])
    output = relative((inputs + branches + bias_row).astype(bf16))

    d_normed = jnp.stack(grads).astype(f32)
    cot_float = cot_rows.astype(f32)
    d_unit = d_normed * norm_gain
    mean_unit = jnp.mean(d_unit, axis=-1, keepdims=True)
    mean_cross = jnp.mean(d_unit * unit, axis=-1, keepdims=True)
    input_grad = relative((cot_float + inv_std * (d_unit - mean_unit - unit * mean_cross)).astype(bf16))

    norm_step = relative(
        jnp.stack([jnp.sum(d_normed * unit, axis=(0, 1)), jnp.sum(d_normed, axis=(0, 1))])
    )
    output_bias_step = relative(jnp.sum(cot_float, axis=(0, 1)))
    heads_bias_total, expand_bias_total = lax.psum((sum(bias_sums), sum(hidden_sums)), "dp")
    norm_total, output_bias_total = lax.psum((norm_step, output_bias_step), ("dp", "tensor"))

    scale_back = 1.0 / seq_len
    norm_upd, norm_mom = adam_update(norm_moments, norm_total * scale_back)
    heads_upd, heads_mom = adam_update(heads_moments, heads_grad * scale_back)
    hbias_upd, hbias_mom = adam_update(heads_bias_moments, heads_bias_total * scale_back)
    merge_upd, merge_mom = adam_update(merge_moments, merge_grad * scale_back)
    expand_upd, expand_mom = adam_update(expand_moments, expand_grad * scale_back)
    ebias_upd, ebias_mom = adam_update(expand_bias_moments, expand_bias_total * scale_back)
    shrink_upd, shrink_mom = adam_update(shrink_moments, shrink_grad * scale_back)
    output_bias_grad = jnp.stack([output_bias_total, output_bias_total]) * scale_back
    obias_upd, obias_mom = adam_update(output_bias_moments, output_bias_grad)
    return (
        output,
        input_grad,
        norm_upd,
        norm_mom,
        heads_upd,
        heads_mom,
        hbias_upd,
        hbias_mom,
        merge_upd,
        merge_mom,
        expand_upd,
        expand_mom,
        ebias_upd,
        ebias_mom,
        shrink_upd,
        shrink_mom,
        obias_upd,
        obias_mom,
    )


def solution(mesh):
    placed = (
        P("dp", "tensor", None),
        P("dp", "tensor", None),
        P("dp", None),
        P("dp", None),
        P(),
        P(),
        P(None, "dp", "tensor"),
        P(None, None, "dp", "tensor"),
        P(None, "tensor"),
        P(None, None, "tensor"),
        P("tensor", "dp"),
        P(None, "tensor", "dp"),
        P("dp", "tensor"),
        P(None, "dp", "tensor"),
        P("tensor"),
        P(None, "tensor"),
        P("tensor", "dp"),
        P(None, "tensor", "dp"),
        P(),
        P(),
    )
    return jax.shard_map(
        body,
        mesh=mesh,
        in_specs=placed,
        out_specs=(placed[0], placed[0], P(), P(), *placed[6:18], P(), P()),
        check_vma=False,
    )
```

```python
import math
from functools import partial

import jax
import jax.numpy as jnp
from jax import lax
from jax.experimental import pallas as pl
from jax.experimental.pallas import tpu as pltpu
from jax.sharding import PartitionSpec as P

HEAD_DIM = 64
ROT = 32
STEP = 5
LANES = 128

norm_eps = 1e-05
beta_first = 0.9
beta_second = 0.95
adam_eps = 1e-08
masked_score = -1000000000.0
score_scale = HEAD_DIM ** (-0.5)
VMEM = 60

f32 = jnp.float32
bf16 = jnp.bfloat16


def document_starts(segment):
    token_index = jnp.arange(segment.shape[0], dtype=jnp.int32)
    doc_begins = jnp.concatenate([jnp.ones((1,), dtype=jnp.bool_), segment[1:] != segment[:-1]])
    return lax.cummax(jnp.where(doc_begins, token_index, 0), axis=0)


def rotary_tables(doc_start):
    seq_len = doc_start.shape[0]
    positions = (jnp.arange(seq_len, dtype=jnp.int32) - doc_start).astype(f32)
    half_rot = ROT // 2
    frequency = jnp.power(10000.0, -2.0 * jnp.arange(half_rot, dtype=f32) / ROT)
    flat = jnp.zeros((HEAD_DIM - ROT,), f32)
    copies = LANES // HEAD_DIM
    by_lane = jnp.tile(jnp.concatenate([frequency, frequency, flat]), copies)
    sign = jnp.where(jnp.arange(LANES) % HEAD_DIM < half_rot, -1.0, 1.0)
    angles = positions[:, None] * by_lane[None, :]
    return jnp.cos(angles), jnp.sin(angles) * sign[None, :]


def masks(doc_start, valid):
    index = jnp.arange(doc_start.shape[0], dtype=jnp.int32)

    def build(query, start, key, key_valid):
        allowed = (key >= start) & (key <= query) & ((key_valid > 0) | (key == query))
        return jnp.where(allowed, 0.0, masked_score).astype(bf16)

    rows = build(index[:, None], doc_start[:, None], index[None, :], valid[None, :])
    columns = build(index[None, :], doc_start[None, :], index[:, None], valid[:, None])
    return rows, columns


def rotate(values, cosine, sine):
    half_rot = ROT // 2
    width = values.shape[1]
    lane = lax.broadcasted_iota(jnp.int32, values.shape, 1) % HEAD_DIM
    ahead = pltpu.roll(values, width - half_rot, 1)
    behind = pltpu.roll(values, half_rot, 1)
    partner = jnp.where(lane < half_rot, ahead, behind)
    return values * cosine + partner * sine


def nt(left, right):
    return lax.dot_general(left, right, (((1,), (1,)), ((), ())), preferred_element_type=f32)


def nn(left, right):
    return lax.dot_general(left, right, (((1,), (0,)), ((), ())), preferred_element_type=f32)


def tn(left, right):
    return lax.dot_general(left, right, (((0,), (0,)), ((), ())), preferred_element_type=f32)


def widen(table, width):
    return jnp.concatenate([table] * (width // LANES), axis=1)


def params(megabytes):
    return pltpu.CompilerParams(vmem_limit_bytes=megabytes * 1024 * 1024)


def steady():
    return pl.CostEstimate(flops=10**10, bytes_accessed=10**7, transcendentals=0)


one = pl.Buffered(1)


def resident(array):
    zeros = (0,) * array.ndim
    return pl.BlockSpec(array.shape, lambda *_: zeros, pipeline_mode=one)


def block_of(array, shape, place):
    return pl.BlockSpec(shape, lambda *_: place, pipeline_mode=one)


def attend_kernel(lows, first, low_ref, x_ref, bias_ref, cos_ref, sin_ref, mask_ref, *refs):
    *weights, qkv_ref, out_ref, lse_ref, k_all, v_all = refs
    seq, step = pl.program_id(0), pl.program_id(1)
    rows, width = out_ref.shape
    heads = width // HEAD_DIM
    blocks = k_all.shape[0] // rows
    cosine = widen(cos_ref[...], width)
    sine = widen(sin_ref[...], width)
    triple = []
    for which in range(3):
        total = None
        for low, ref in zip(lows, weights[which::3]):
            term = nn(x_ref[:, low : low + ref.shape[0]], ref[...])
            total = term if total is None else total + term
        triple.append(total + bias_ref[which : which + 1, :])
    query = rotate(triple[0], cosine, sine).astype(bf16)
    key = rotate(triple[1], cosine, sine).astype(bf16)
    value = triple[2].astype(bf16)
    qkv_ref[0] = query
    qkv_ref[1] = key
    qkv_ref[2] = value
    own = pl.ds(pl.multiple_of(step * rows, rows), rows)
    k_all[own, :] = key
    v_all[own, :] = value
    scaled = query * jnp.asarray(score_scale, bf16)
    head_of = lax.broadcasted_iota(jnp.int32, (rows, width), 1) // HEAD_DIM
    lane = lax.broadcasted_iota(jnp.int32, (rows, LANES), 1)
    span = step - low_ref[first + seq, step] + 1
    for count in range(1, blocks + 1):

        @pl.when(span == count)
        def _(count=count):
            begin = pl.multiple_of((step - (count - 1)) * rows, rows)
            keys = k_all[pl.ds(begin, count * rows), :]
            values = v_all[pl.ds(begin, count * rows), :]
            mask = mask_ref[:, pl.ds(begin, count * rows)].astype(f32)
            result = jnp.zeros((rows, width), f32)
            stats = jnp.zeros((rows, LANES), f32)
            for head in range(heads):
                mine = head_of == head
                scores = nt(jnp.where(mine, scaled, jnp.zeros_like(scaled)), keys) + mask
                top = jnp.max(scores, axis=1, keepdims=True)
                weights = jnp.exp(scores - top)
                total = jnp.sum(weights, axis=1, keepdims=True)
                mixed = nn(weights.astype(bf16), values) * (1.0 / total)
                result = jnp.where(mine, mixed, result)
                stats = jnp.where(lane == head, top + jnp.log(total), stats)
            out_ref[...] = result.astype(bf16)
            lse_ref[...] = jnp.transpose(stats)[: lse_ref.shape[0], :]


def attend(normed, first, count, entry, bias, cosine, sine, mask, low, rows):
    pieces, lows = entry
    _, seq_len, model_width = normed.shape
    width = bias.shape[1]
    blocks = seq_len // rows
    stat_rows = 8
    side = (pieces[0].shape[1] - 3 * width) // width

    def rows_of(columns):
        return pl.BlockSpec((None, rows, columns), lambda s, i, low: (first + s, i, 0))

    grid_spec = pltpu.PrefetchScalarGridSpec(
        num_scalar_prefetch=1,
        grid=(count, blocks),
        in_specs=[
            rows_of(model_width),
            resident(bias),
            rows_of(LANES),
            rows_of(LANES),
            rows_of(seq_len),
            *[
                block_of(piece, (piece.shape[0], width), (0, side + which))
                for piece in pieces
                for which in range(3)
            ],
        ],
        out_specs=[
            pl.BlockSpec((3, None, rows, width), lambda s, i, low: (0, s, i, 0)),
            pl.BlockSpec((None, rows, width), lambda s, i, low: (s, i, 0)),
            pl.BlockSpec((None, stat_rows, rows), lambda s, i, low: (s, 0, i)),
        ],
        scratch_shapes=[pltpu.VMEM((seq_len, width), bf16), pltpu.VMEM((seq_len, width), bf16)],
    )
    return pl.pallas_call(
        partial(attend_kernel, lows, first),
        grid_spec=grid_spec,
        out_shape=[
            jax.ShapeDtypeStruct((3, count, seq_len, width), bf16),
            jax.ShapeDtypeStruct((count, seq_len, width), bf16),
            jax.ShapeDtypeStruct((count, stat_rows, seq_len), f32),
        ],
        compiler_params=params(VMEM),
        cost_estimate=steady(),
        name="attend",
    )(low, normed, bias, cosine, sine, mask, *[piece for piece in pieces for _ in range(3)])


def attend_back_kernel(
    lows, first, low_ref, q_ref, k_ref, v_ref, g_ref, lse_ref, mask_ref, cos_ref, sin_ref, *refs
):
    *weights, out_ref, sum_ref, dk_all, dv_all = refs
    seq, step = pl.program_id(0), pl.program_id(1)
    rows, width = q_ref.shape
    heads = width // HEAD_DIM
    seq_len = dk_all.shape[0]
    blocks = seq_len // rows

    @pl.when(step == 0)
    def _():
        dk_all[...] = jnp.zeros_like(dk_all)
        dv_all[...] = jnp.zeros_like(dv_all)

    @pl.when((step == 0) & (seq == 0))
    def _():
        sum_ref[...] = jnp.zeros_like(sum_ref)

    scaled = q_ref[...] * jnp.asarray(score_scale, bf16)
    d_out = None
    for low, ref in zip(lows, weights):
        term = nt(g_ref[:, low : low + ref.shape[1]], ref[...])
        d_out = term if d_out is None else d_out + term
    d_out = d_out.astype(bf16)
    zero = jnp.zeros_like(d_out)
    head_of = lax.broadcasted_iota(jnp.int32, (rows, width), 1) // HEAD_DIM
    own = pl.ds(pl.multiple_of(step * rows, rows), rows)
    span = step - low_ref[first + seq, step] + 1
    for count in range(1, blocks + 1):

        @pl.when(span == count)
        def _(count=count):
            begin = pl.multiple_of((step - (count - 1)) * rows, rows)
            reach = pl.ds(begin, count * rows)
            keys = k_ref[reach, :]
            values = v_ref[reach, :]
            mask = mask_ref[reach, :].astype(f32)
            d_query = jnp.zeros((rows, width), f32)
            probs_side, scores_side, queries_down, d_outs_down = [], [], [], []
            for head in range(heads):
                mine = head_of == head
                query = jnp.where(mine, scaled, zero)
                d_mine = jnp.where(mine, d_out, zero)
                scores = nt(keys, query) + mask
                probs = jnp.exp(scores - lse_ref[head : head + 1, :])
                d_probs = nt(values, d_mine)
                delta = jnp.sum(probs * d_probs, axis=0, keepdims=True)
                d_scores = (probs * (d_probs - delta)).astype(bf16)
                d_query = jnp.where(mine, tn(d_scores, keys), d_query)
                probs_side.append(probs.astype(bf16))
                scores_side.append(d_scores)
                queries_down.append(query)
                d_outs_down.append(d_mine)
            dv_all[reach, :] += nn(
                jnp.concatenate(probs_side, axis=1), jnp.concatenate(d_outs_down, axis=0)
            )
            dk_all[reach, :] += nn(
                jnp.concatenate(scores_side, axis=1), jnp.concatenate(queries_down, axis=0)
            )
            cosine = widen(cos_ref[own, :], width)
            sine = widen(sin_ref[own, :], width)
            low_query = rotate(d_query * score_scale, cosine, -sine).astype(bf16)
            out_ref[own, :width] = low_query
            sum_ref[0:1, :] += jnp.sum(low_query.astype(f32), axis=0, keepdims=True)

    @pl.when(step == blocks - 1)
    def _():
        cosine = widen(cos_ref[...], width)
        sine = widen(sin_ref[...], width)
        low_key = rotate(dk_all[...], cosine, -sine).astype(bf16)
        low_value = dv_all[...].astype(bf16)
        out_ref[:, width : 2 * width] = low_key
        out_ref[:, 2 * width :] = low_value
        sum_ref[1:2, :] += jnp.sum(low_key.astype(f32), axis=0, keepdims=True)
        sum_ref[2:3, :] += jnp.sum(low_value.astype(f32), axis=0, keepdims=True)


def attend_back(qkv, cot, first, count, exits, lse, mask, cosine, sine, low, rows):
    pieces, lows = exits
    _, seq_len, model_width = cot.shape
    width = qkv.shape[3]
    blocks = seq_len // rows
    stat_rows = lse.shape[1]
    units = pieces[0].shape[0] - width

    def whole_of(columns):
        return pl.BlockSpec((None, seq_len, columns), lambda s, i, low: (first + s, 0, 0))

    grid_spec = pltpu.PrefetchScalarGridSpec(
        num_scalar_prefetch=1,
        grid=(count, blocks),
        in_specs=[
            pl.BlockSpec((None, None, rows, width), lambda s, i, low: (0, first + s, i, 0)),
            pl.BlockSpec((None, None, seq_len, width), lambda s, i, low: (1, first + s, 0, 0)),
            pl.BlockSpec((None, None, seq_len, width), lambda s, i, low: (2, first + s, 0, 0)),
            pl.BlockSpec((None, rows, model_width), lambda s, i, low: (first + s, i, 0)),
            pl.BlockSpec((None, stat_rows, rows), lambda s, i, low: (first + s, 0, i)),
            pl.BlockSpec((None, seq_len, rows), lambda s, i, low: (first + s, 0, i)),
            whole_of(LANES),
            whole_of(LANES),
            *[block_of(piece, (width, piece.shape[1]), (units // width, 0)) for piece in pieces],
        ],
        out_specs=[
            pl.BlockSpec((None, seq_len, 3 * width), lambda s, i, low: (s, 0, 0)),
            pl.BlockSpec((8, width), lambda s, i, low: (0, 0)),
        ],
        scratch_shapes=[pltpu.VMEM((seq_len, width), f32), pltpu.VMEM((seq_len, width), f32)],
    )
    return pl.pallas_call(
        partial(attend_back_kernel, lows, first),
        grid_spec=grid_spec,
        out_shape=[
            jax.ShapeDtypeStruct((count, seq_len, 3 * width), bf16),
            jax.ShapeDtypeStruct((8, width), f32),
        ],
        compiler_params=params(VMEM),
        cost_estimate=steady(),
        name="attend_back",
    )(low, qkv, qkv, qkv, cot, lse, mask, cosine, sine, *pieces)


def gelu_kernel(lows, tick_ref, x_ref, bias_ref, *refs):
    *weights, hidden_ref, slope_ref = refs
    pre = bias_ref[...]
    for low, ref in zip(lows, weights):
        pre = pre + nn(x_ref[:, low : low + ref.shape[0]], ref[...])
    scale = (2.0 / math.pi) ** 0.5
    square = pre * pre
    tanh = jnp.tanh(scale * pre * (1.0 + 0.044715 * square))
    half = 0.5 * (1.0 + tanh)
    hidden_ref[...] = (pre * half).astype(bf16)
    slope = half + 0.5 * pre * (1.0 - tanh * tanh) * (scale * (1.0 + 3 * 0.044715 * square))
    slope_ref[...] = slope.astype(bf16)


def gelu_units(tick, normed, entry, bias, rows):
    pieces, lows = entry
    count, seq_len, model_width = normed.shape
    units = bias.shape[1]
    block = pl.BlockSpec((None, rows, units), lambda s, i, _: (s, i, 0))
    return pl.pallas_call(
        partial(gelu_kernel, lows),
        grid_spec=pltpu.PrefetchScalarGridSpec(
            num_scalar_prefetch=1,
            grid=(count, seq_len // rows),
            in_specs=[
                pl.BlockSpec((None, rows, model_width), lambda s, i, _: (s, i, 0)),
                resident(bias),
                *[block_of(piece, (piece.shape[0], units), (0, 0)) for piece in pieces],
            ],
            out_specs=[block, block],
        ),
        out_shape=[jax.ShapeDtypeStruct((count, seq_len, units), bf16)] * 2,
        compiler_params=params(VMEM),
        cost_estimate=steady(),
        name="gelu_units",
    )(tick, normed, bias, *pieces)


def out_kernel(lows, tick_ref, a_ref, h_ref, *refs):
    weights, outs = refs[: len(lows)], refs[len(lows) :]
    units = h_ref.shape[1]
    seq = pl.program_id(0)
    for which, out_ref in enumerate(outs):

        @pl.when(seq == which)
        def _(out_ref=out_ref):
            for low, ref in zip(lows, weights):
                term = nn(h_ref[...], ref[:units, :]) + nn(a_ref[...], ref[units:, :])
                out_ref[:, low : low + ref.shape[1]] = term.astype(bf16)


def out_sums(tick, attended, hidden, exits, rows):
    pieces, lows = exits
    count, seq_len, width = attended.shape
    units = hidden.shape[2]
    model_width = sum(piece.shape[1] for piece in pieces)
    blocks = seq_len // rows

    def rows_of(columns):
        return pl.BlockSpec((None, rows, columns), lambda s, i, _: (s, i, 0))

    def own_rows(which):
        return pl.BlockSpec(
            (rows, model_width), lambda s, i, _: (jnp.clip(i + (s - which) * blocks, 0, blocks - 1), 0)
        )

    return pl.pallas_call(
        partial(out_kernel, lows),
        grid_spec=pltpu.PrefetchScalarGridSpec(
            num_scalar_prefetch=1,
            grid=(count, blocks),
            in_specs=[rows_of(width), rows_of(units), *[resident(piece) for piece in pieces]],
            out_specs=[own_rows(which) for which in range(count)],
        ),
        out_shape=[jax.ShapeDtypeStruct((seq_len, model_width), bf16)] * count,
        compiler_params=params(VMEM),
        cost_estimate=steady(),
        name="out_sums",
    )(tick, attended, hidden, *pieces)


def back_rows_kernel(entry_lows, exit_lows, tick_ref, g_ref, slope_ref, c_ref, *refs):
    entry, exits = refs[: len(entry_lows)], refs[len(entry_lows) : len(entry_lows) + len(exit_lows)]
    hidden_ref, normed_ref, sum_ref = refs[-3:]
    units = slope_ref.shape[1]

    @pl.when(pl.program_id(0) == 0)
    def _():
        sum_ref[...] = jnp.zeros_like(sum_ref)

    total = None
    for low, ref in zip(exit_lows, exits):
        term = nt(g_ref[:, low : low + ref.shape[1]], ref[...])
        total = term if total is None else total + term
    d_hidden = (total * slope_ref[...].astype(f32)).astype(bf16)
    hidden_ref[...] = d_hidden
    sum_ref[0:1, :] += jnp.sum(d_hidden.astype(f32), axis=0, keepdims=True)
    for low, ref in zip(entry_lows, entry):
        term = nt(d_hidden, ref[:, :units]) + nt(c_ref[...], ref[:, units:])
        normed_ref[:, low : low + ref.shape[0]] = term.astype(bf16)


def back_rows(tick, cot, which, slope, d_cat, entry, exits, rows):
    pieces, lows = entry
    exit_pieces, exit_lows = exits
    _, seq_len, model_width = cot.shape
    units = slope.shape[2]

    def rows_of(columns):
        return pl.BlockSpec((None, rows, columns), lambda i, _: (which, i, 0))

    def own_rows(columns):
        return pl.BlockSpec((None, rows, columns), lambda i, _: (0, i, 0))

    return pl.pallas_call(
        partial(back_rows_kernel, lows, exit_lows),
        grid_spec=pltpu.PrefetchScalarGridSpec(
            num_scalar_prefetch=1,
            grid=(seq_len // rows,),
            in_specs=[
                rows_of(model_width),
                rows_of(units),
                own_rows(d_cat.shape[2]),
                *[resident(piece) for piece in pieces],
                *[block_of(piece, (units, piece.shape[1]), (0, 0)) for piece in exit_pieces],
            ],
            out_specs=[
                own_rows(units),
                own_rows(model_width),
                pl.BlockSpec((8, units), lambda i, _: (0, 0)),
            ],
        ),
        out_shape=[
            jax.ShapeDtypeStruct((1, seq_len, units), bf16),
            jax.ShapeDtypeStruct((1, seq_len, model_width), bf16),
            jax.ShapeDtypeStruct((8, units), f32),
        ],
        compiler_params=params(VMEM),
        cost_estimate=steady(),
        name="back_rows",
    )(tick, cot, slope, d_cat, *pieces, *exit_pieces)


def targets(ranks, parts):
    if ranks == 4:
        half = parts // 2
        return [(0, half), (half, parts)] + [(at * parts, (at + 1) * parts) for at in range(1, ranks)]
    return [(at * parts, (at + 1) * parts) for at in range(ranks)]


def rows_grad_kernel(seqs, spans, tick_ref, *refs):
    left, right, outs = refs[:seqs], refs[seqs : 2 * seqs], refs[2 * seqs :]
    step = pl.program_id(0)
    for (begin, end), out_ref in zip(spans, outs):

        @pl.when((step >= begin) & (step < end))
        def _(out_ref=out_ref):
            total = tn(left[0][...], right[0][...])
            for s in range(1, seqs):
                total += tn(left[s][...], right[s][...])
            out_ref[...] = total.astype(bf16)


def rows_grad(tick, left, right, ranks, name):
    seqs, seq_len, model_width = left.shape
    columns = right[0].shape[2]
    piece = model_width // ranks
    parts = max(2, piece // 256)
    block = piece // parts
    spans = targets(ranks, parts)

    def column_block(s):
        return lambda i, _: (s, 0, (ranks - 1 - i // parts) * parts + i % parts)

    def target_block(begin, end):
        return lambda i, _: (jnp.clip(i - begin, 0, end - begin - 1), 0)

    return pl.pallas_call(
        partial(rows_grad_kernel, seqs, spans),
        grid_spec=pltpu.PrefetchScalarGridSpec(
            num_scalar_prefetch=1,
            grid=(ranks * parts,),
            in_specs=[
                *[pl.BlockSpec((None, seq_len, block), column_block(s)) for s in range(seqs)],
                *[block_of(array, (None, seq_len, columns), (0, 0, 0)) for array in right],
            ],
            out_specs=[pl.BlockSpec((block, columns), target_block(*span)) for span in spans],
        ),
        out_shape=[jax.ShapeDtypeStruct(((end - begin) * block, columns), bf16) for begin, end in spans],
        compiler_params=params(VMEM),
        cost_estimate=steady(),
        name=name,
    )(tick, *([left] * seqs), *right)


def columns_grad_kernel(spans, tick_ref, *refs):
    kinds = (len(refs) - 1 - len(spans)) // 2
    left, right, outs, turned = refs[:kinds], refs[kinds], refs[kinds + 1 : -kinds], refs[-kinds:]
    step = pl.program_id(0)

    @pl.when(step == 0)
    def _():
        for source, target in zip(left, turned):
            target[...] = jnp.transpose(source[...])

    for (begin, end), out_ref in zip(spans, outs):

        @pl.when((step >= begin) & (step < end))
        def _(out_ref=out_ref):
            first = 0
            for kind in range(kinds):
                total = nn(turned[kind][...], right[...])
                out_ref[first : first + total.shape[0], :] = total.astype(bf16)
                first += total.shape[0]


def columns_grad(tick, lefts, right, ranks, name):
    tokens, model_width = right.shape
    piece = model_width // ranks
    parts = 2
    block = piece // parts
    spans = targets(ranks, parts)
    height = sum(left.shape[1] for left in lefts)

    def column_block(i, _):
        return (0, (ranks - 1 - i // parts) * parts + i % parts)

    def target_block(begin, end):
        return lambda i, _: (0, jnp.clip(i - begin, 0, end - begin - 1))

    return pl.pallas_call(
        partial(columns_grad_kernel, spans),
        grid_spec=pltpu.PrefetchScalarGridSpec(
            num_scalar_prefetch=1,
            grid=(ranks * parts,),
            in_specs=[*[resident(left) for left in lefts], pl.BlockSpec((tokens, block), column_block)],
            out_specs=[pl.BlockSpec((height, block), target_block(*span)) for span in spans],
            scratch_shapes=[pltpu.VMEM((left.shape[1], tokens), bf16) for left in lefts],
        ),
        out_shape=[jax.ShapeDtypeStruct((height, (end - begin) * block), bf16) for begin, end in spans],
        compiler_params=params(VMEM),
        cost_estimate=steady(),
        name=name,
    )(tick, *lefts, right)


def adam_step(moment_one, moment_two, gradient):
    moment_one = beta_first * moment_one + (1.0 - beta_first) * gradient
    moment_two = beta_second * moment_two + (1.0 - beta_second) * gradient * gradient
    first_fix = 1.0 - beta_first**STEP
    second_fix = 1.0 - beta_second**STEP
    update = moment_one / first_fix / (jnp.sqrt(moment_two / second_fix) + adam_eps)
    return update, moment_one, moment_two


def adam_update(moments, gradient):
    update, moment_one, moment_two = adam_step(moments[0], moments[1], gradient)
    return update, jnp.stack([moment_one, moment_two])


def adam_kernel(scale, tick_ref, moments_ref, *refs):
    *terms, update_ref, new_ref = refs
    gradient = terms[0][...].astype(f32)
    for term in terms[1:]:
        gradient = gradient + term[...].astype(f32)
    update, moment_one, moment_two = adam_step(moments_ref[0], moments_ref[1], gradient * scale)
    update_ref[...] = update
    new_ref[0] = moment_one
    new_ref[1] = moment_two


def adam_sum(tick, moments, terms, scale, row, column, parts):
    groups = parts if parts else 1
    height, width = moments.shape[-2:]
    rows = min(256, height)
    steps = height // rows
    if parts:
        moment_block = pl.BlockSpec((2, None, rows, width), lambda p, i, _: (0, p, i, 0))
        update_block = pl.BlockSpec((None, rows, width), lambda p, i, _: (p, i, 0))
    else:
        moment_block = pl.BlockSpec((2, rows, width), lambda p, i, _: (0, i, 0))
        update_block = pl.BlockSpec((rows, width), lambda p, i, _: (i, 0))
    term_block = pl.BlockSpec((rows, width), lambda p, i, _: (row // rows + i, column // width + p))
    return pl.pallas_call(
        partial(adam_kernel, scale),
        grid_spec=pltpu.PrefetchScalarGridSpec(
            num_scalar_prefetch=1,
            grid=(groups, steps),
            in_specs=[moment_block, *[term_block] * len(terms)],
            out_specs=[update_block, moment_block],
        ),
        out_shape=[
            jax.ShapeDtypeStruct(moments.shape[1:], f32),
            jax.ShapeDtypeStruct(moments.shape, f32),
        ],
        compiler_params=params(VMEM),
        cost_estimate=steady(),
        name="adam_sum",
    )(tick, moments, *terms)


def from_relative(ref, rank, ranks, piece):
    return jnp.concatenate(
        [ref[:, pl.ds(pl.multiple_of((rank ^ j) * piece, piece), piece)] for j in range(ranks)], axis=1
    )


def input_grad_kernel(ranks, rank_ref, x_ref, g_ref, norm_ref, *refs):
    *d_refs, out_ref, sum_ref = refs
    rank = rank_ref[0]
    seq = pl.program_id(0)
    piece = x_ref.shape[1] // ranks
    inputs = x_ref[...].astype(f32)
    centred = inputs - jnp.mean(inputs, axis=1, keepdims=True)
    variance = jnp.mean(centred * centred, axis=1, keepdims=True)
    inv_std = lax.rsqrt(variance + norm_eps)
    unit = centred * inv_std
    cot = g_ref[...].astype(f32)

    @pl.when(seq == 0)
    def _():
        sum_ref[...] = jnp.zeros_like(sum_ref)

    for which, d_ref in enumerate(d_refs):

        @pl.when(seq == which)
        def _(d_ref=d_ref):
            d_normed = from_relative(d_ref, rank, ranks, piece).astype(f32)
            d_unit = d_normed * norm_ref[0:1, :]
            mean_unit = jnp.mean(d_unit, axis=1, keepdims=True)
            mean_cross = jnp.mean(d_unit * unit, axis=1, keepdims=True)
            out_ref[...] = (cot + inv_std * (d_unit - mean_unit - unit * mean_cross)).astype(bf16)
            sum_ref[0:1, :] += jnp.sum(d_normed * unit, axis=0, keepdims=True)
            sum_ref[1:2, :] += jnp.sum(d_normed, axis=0, keepdims=True)
            sum_ref[2:3, :] += jnp.sum(cot, axis=0, keepdims=True)


def input_gradient(rank, tokens, cot_rows, norm_params, grads, ranks):
    count, rows, model_width = tokens.shape
    block = pl.BlockSpec((None, rows, model_width), lambda s, _: (s, 0, 0))
    return pl.pallas_call(
        partial(input_grad_kernel, ranks),
        grid_spec=pltpu.PrefetchScalarGridSpec(
            num_scalar_prefetch=1,
            grid=(count,),
            in_specs=[
                block,
                block,
                resident(norm_params),
                *[block_of(grad, (None, rows, model_width), (0, 0, 0)) for grad in grads],
            ],
            out_specs=[block, pl.BlockSpec((8, model_width), lambda s, _: (0, 0))],
        ),
        out_shape=[
            jax.ShapeDtypeStruct(tokens.shape, bf16),
            jax.ShapeDtypeStruct((8, model_width), f32),
        ],
        compiler_params=params(VMEM),
        cost_estimate=steady(),
        name="input_grad",
    )(rank, tokens, cot_rows, norm_params, *grads)


def output_kernel(ranks, rank_ref, x_ref, bias_ref, *refs):
    *o_refs, out_ref = refs
    rank = rank_ref[0]
    piece = x_ref.shape[1] // ranks
    for which, o_ref in enumerate(o_refs):

        @pl.when(pl.program_id(0) == which)
        def _(o_ref=o_ref):
            branches = from_relative(o_ref, rank, ranks, piece).astype(f32)
            total = x_ref[...].astype(f32) + branches + bias_ref[0:1, :] + bias_ref[1:2, :]
            out_ref[...] = total.astype(bf16)


def layer_output(rank, tokens, output_bias, outs, ranks):
    count, rows, model_width = tokens.shape
    block = pl.BlockSpec((None, rows, model_width), lambda s, _: (s, 0, 0))
    return pl.pallas_call(
        partial(output_kernel, ranks),
        grid_spec=pltpu.PrefetchScalarGridSpec(
            num_scalar_prefetch=1,
            grid=(count,),
            in_specs=[
                block,
                resident(output_bias),
                *[block_of(out, (None, rows, model_width), (0, 0, 0)) for out in outs],
            ],
            out_specs=block,
        ),
        out_shape=jax.ShapeDtypeStruct(tokens.shape, bf16),
        compiler_params=params(VMEM),
        cost_estimate=steady(),
        name="layer_output",
    )(rank, tokens, output_bias, *outs)


def swap(array, distance):
    size = lax.axis_size("dp")
    return lax.ppermute(array, "dp", [(i, i ^ distance) for i in range(size)])


def plus(left, right):
    return (left.astype(f32) + right.astype(f32)).astype(bf16)


class Line:
    def __init__(self, first):
        self.last = first

    def then(self, *arrays):
        found = lax.optimization_barrier((*arrays, self.last))[:-1]
        return found[0] if len(arrays) == 1 else found

    def tick(self):
        return self.then(jnp.zeros((1,), jnp.int32))

    def did(self, array):
        self.last = lax.optimization_barrier((array, self.last))[0]

    def wait(self, *arrays):
        self.last = lax.optimization_barrier((*arrays, self.last))[-1]


class Gather:
    def __init__(self, line, own, axis):
        self.size = lax.axis_size("dp")
        self.own, self.axis = own, axis
        own = line.then(own)
        self.sent = [swap(own, j) for j in ((1, 2) if self.size == 4 else range(1, self.size))]

    def forward(self, line):
        line.wait(*self.sent)
        if self.size == 4:
            half = self.own.shape[self.axis] // 2
            near, far = self.sent
            top = lax.slice_in_dim(near, 0, half, axis=self.axis)
            bottom = lax.slice_in_dim(far, half, 2 * half, axis=self.axis)
            top, bottom = line.then(top, bottom)
            self.rest = [swap(top, 2), swap(bottom, 1)]

    def finish(self, line):
        pieces = [self.own, *self.sent]
        if self.size == 4:
            line.wait(*self.rest)
            pieces += self.rest
        lows, low = [], 0
        for piece in pieces:
            lows.append(low)
            low += piece.shape[self.axis]
        return pieces, tuple(lows)


class Scatter:
    def __init__(self, line, pieces, axis):
        self.axis = axis
        self.size = lax.axis_size("dp")
        if self.size == 4:
            top, bottom, self.far, self.near, self.own = pieces
            top, bottom = line.then(top, bottom)
            self.sent = [swap(top, 1), swap(bottom, 2)]
        else:
            self.own = pieces[-1]
            rest = line.then(*pieces[:-1])
            self.sent = [swap(piece, self.size - 1 - at) for at, piece in enumerate(rest)]
            self.parts = [self.sent]

    def halves(self, array):
        half = array.shape[self.axis] // 2
        return [lax.slice_in_dim(array, at, at + half, axis=self.axis) for at in (0, half)]

    def forward(self, line):
        if self.size == 4:
            line.wait(*self.sent)
            top, bottom = self.sent
            near, far = self.halves(self.near), self.halves(self.far)
            self.second = [plus(near[1], bottom), far[1]]
            first = line.then(near[0], plus(far[0], top))
            self.parts = [[swap(first[0], 1), swap(first[1], 2)]]

    def forward_whole(self, line):
        if self.size == 4:
            line.wait(*self.sent)
            top, bottom = self.sent
            near, far = self.halves(self.near), self.halves(self.far)
            near = jnp.concatenate([near[0], plus(near[1], bottom)], axis=self.axis)
            far = jnp.concatenate([plus(far[0], top), far[1]], axis=self.axis)
            near, far = line.then(near, far)
            self.parts = [[swap(near, 1), swap(far, 2)]]

    def again(self, line):
        if self.size == 4:
            line.wait(*self.parts[0])
            second = line.then(*self.second)
            self.parts.append([swap(second[0], 1), swap(second[1], 2)])

    def finish(self, line):
        line.wait(*self.parts[-1])
        if self.size != 4:
            return [self.own, *self.sent]
        if len(self.parts) == 1:
            return [self.own, *self.parts[0]]
        return [
            self.own,
            *[jnp.concatenate([part[at] for part in self.parts], axis=self.axis) for at in range(2)],
        ]


def sum_axis(array, axis):
    size = lax.axis_size(axis)
    distance = 1
    while distance < size:
        array = array + lax.ppermute(array, axis, [(i, i ^ distance) for i in range(size)])
        distance *= 2
    return array


def body(
    tokens,
    cotangent,
    segments,
    valid_mask,
    norm_params,
    norm_moments,
    heads_weight,
    heads_moments,
    heads_bias,
    heads_bias_moments,
    merge_weight,
    merge_moments,
    expand_weight,
    expand_moments,
    expand_bias,
    expand_bias_moments,
    shrink_weight,
    shrink_moments,
    output_bias,
    output_bias_moments,
):
    ranks = lax.axis_size("dp")
    rank = lax.axis_index("dp")
    count, _, model_width = tokens.shape
    seq_len = segments.shape[1]
    width = heads_weight.shape[2]
    piece = model_width // ranks
    rows = min(256, seq_len)

    def relative(array):
        parts = [
            lax.dynamic_slice_in_dim(array, (rank ^ j) * piece, piece, array.ndim - 1) for j in range(ranks)
        ]
        return jnp.concatenate(parts, axis=-1)

    norm_rel = relative(norm_params)
    norm_gain, norm_shift = norm_rel[0], norm_rel[1]
    inputs = relative(tokens).astype(f32)
    cot_rows = relative(cotangent)
    row_mean = jnp.mean(inputs, axis=-1, keepdims=True)
    centred = inputs - row_mean
    variance = jnp.mean(centred * centred, axis=-1, keepdims=True)
    inv_std = lax.rsqrt(variance + norm_eps)
    unit = centred * inv_std
    normed_rows = (unit * norm_gain + norm_shift).astype(bf16)

    def gather_rows(array):
        return lax.all_gather(array, "tensor", axis=1, tiled=True)

    def scatter_rows(array):
        return lax.psum_scatter(array, "tensor", scatter_dimension=1, tiled=True)

    line = Line(normed_rows)
    rank_here = rank.reshape(1).astype(jnp.int32)
    normed = gather_rows(normed_rows)
    cot = gather_rows(line.then(cot_rows))

    entry_own = jnp.concatenate([expand_weight, *[heads_weight[c] for c in range(3)]], axis=1).astype(bf16)
    entry_gather = Gather(line, entry_own, 0)
    exit_own = jnp.concatenate([shrink_weight, merge_weight], axis=0).astype(bf16)
    starts = jnp.stack([document_starts(segments[s]) for s in range(count)])
    cosine, sine = jax.vmap(rotary_tables)(starts)
    mask_rows, mask_columns = jax.vmap(masks)(starts, valid_mask)
    lows = starts[:, ::rows] // rows
    expand_row = expand_bias.reshape(1, -1)
    line.wait(exit_own, cosine, sine, mask_rows, mask_columns)
    entry_gather.forward(line)
    entry = entry_gather.finish(line)
    line.wait(normed)
    exit_gather = Gather(line, exit_own, 1)
    big = min(512, seq_len)
    units_local = expand_weight.shape[1]

    qkv, attended, lse = attend(
        normed, 0, count, entry, heads_bias, cosine, sine, mask_rows, line.then(lows), rows
    )
    line.did(attended)
    exit_gather.forward(line)
    hidden, slope = gelu_units(line.tick(), normed, entry, expand_row, big)
    line.did(hidden)
    exits = exit_gather.finish(line)
    partials = out_sums(line.tick(), attended, hidden, exits, big)
    line.did(partials[0])

    def adam(moments, terms, row=0, column=0, parts=0):
        update, moments_new = adam_sum(line.tick(), moments, terms, 1.0 / seq_len, row, column, parts)
        line.did(update)
        return update, moments_new

    d_cats, d_hiddens, grads, bias_sums, hidden_sums = ([None] * count for _ in range(5))

    def attention_back(s):
        d_cats[s], bias_sums[s] = attend_back(
            qkv, cot, s, 1, exits, lse, mask_columns, cosine, sine, line.then(lows), rows
        )
        line.did(d_cats[s])

    def rows_back(s):
        d_hiddens[s], sums, hidden_sums[s] = back_rows(
            line.tick(), cot, s, slope, d_cats[s], entry, exits, big
        )
        line.did(d_hiddens[s])
        return sums

    def tokens_of(array):
        return array.reshape(-1, array.shape[-1])

    last = count - 1
    outs = [scatter_rows(partials[s][None]) for s in range(last)]
    for s in range(last):
        attention_back(s)
        grads[s] = scatter_rows(rows_back(s))
    exit_parts = columns_grad(
        line.tick(), [tokens_of(hidden), tokens_of(attended)], tokens_of(cot), ranks, "exit_grad"
    )
    line.did(exit_parts[0])
    line.wait(*outs)
    exit_scatter = Scatter(line, exit_parts, 1)
    attention_back(last)
    exit_scatter.forward(line)
    sums = rows_back(last)
    exit_scatter.again(line)
    grads[last] = scatter_rows(line.then(sums))
    outs.append(scatter_rows(line.then(partials[last])[None]))
    expand_parts = rows_grad(line.tick(), normed, d_hiddens, ranks, "expand_grad")
    line.did(expand_parts[0])
    exit_terms = exit_scatter.finish(line)
    expand_scatter = Scatter(line, expand_parts, 0)
    heads_parts = rows_grad(line.tick(), normed, d_cats, ranks, "heads_grad")
    line.did(heads_parts[0])
    expand_scatter.forward_whole(line)
    heads_scatter = Scatter(line, heads_parts, 0)
    shrink_upd, shrink_mom = adam(shrink_moments, exit_terms)
    merge_upd, merge_mom = adam(merge_moments, exit_terms, row=units_local)
    line.wait(*grads)
    heads_scatter.forward_whole(line)
    input_grad, column_sums = input_gradient(
        line.then(rank_here), tokens, cotangent, norm_params, grads, ranks
    )
    line.did(input_grad)
    expand_terms = expand_scatter.finish(line)
    expand_upd, expand_mom = adam(expand_moments, expand_terms)
    column_sums = sum_axis(line.then(column_sums), "tensor")
    bias_sums = jnp.concatenate([sum(b[:3] for b in bias_sums).reshape(-1), sum(h[0] for h in hidden_sums)])
    totals = sum_axis(jnp.concatenate([column_sums[:3].reshape(-1), bias_sums]), "dp")
    line.did(totals)
    heads_terms = heads_scatter.finish(line)
    heads_upd, heads_mom = adam(heads_moments, heads_terms, parts=3)
    line.wait(*outs)
    output = layer_output(line.then(rank_here), tokens, output_bias, outs, ranks)
    norm_total = totals[: 2 * model_width].reshape(2, model_width)
    output_bias_total = totals[2 * model_width : 3 * model_width]
    bias_total = totals[3 * model_width :]
    heads_bias_total = bias_total[: 3 * width].reshape(3, width)
    expand_bias_total = bias_total[3 * width :]

    scale_back = 1.0 / seq_len
    norm_upd, norm_mom = adam_update(norm_moments, norm_total * scale_back)
    hbias_upd, hbias_mom = adam_update(heads_bias_moments, heads_bias_total * scale_back)
    ebias_upd, ebias_mom = adam_update(expand_bias_moments, expand_bias_total * scale_back)
    output_bias_grad = jnp.stack([output_bias_total, output_bias_total]) * scale_back
    obias_upd, obias_mom = adam_update(output_bias_moments, output_bias_grad)
    return (
        output,
        input_grad,
        norm_upd,
        norm_mom,
        heads_upd,
        heads_mom,
        hbias_upd,
        hbias_mom,
        merge_upd,
        merge_mom,
        expand_upd,
        expand_mom,
        ebias_upd,
        ebias_mom,
        shrink_upd,
        shrink_mom,
        obias_upd,
        obias_mom,
    )


def solution(mesh):
    placed = (
        P("dp", "tensor", None),
        P("dp", "tensor", None),
        P("dp", None),
        P("dp", None),
        P(),
        P(),
        P(None, "dp", "tensor"),
        P(None, None, "dp", "tensor"),
        P(None, "tensor"),
        P(None, None, "tensor"),
        P("tensor", "dp"),
        P(None, "tensor", "dp"),
        P("dp", "tensor"),
        P(None, "dp", "tensor"),
        P("tensor"),
        P(None, "tensor"),
        P("tensor", "dp"),
        P(None, "tensor", "dp"),
        P(),
        P(),
    )
    return jax.shard_map(
        body,
        mesh=mesh,
        in_specs=placed,
        out_specs=(placed[0], placed[0], P(), P(), *placed[6:18], P(), P()),
        check_vma=False,
    )
```

```python
import math
from functools import partial

import jax
import jax.numpy as jnp
from jax import lax
from jax.experimental import pallas as pl
from jax.experimental.pallas import tpu as pltpu
from jax.sharding import PartitionSpec as P

HEAD_DIM = 64
ROT = 32
STEP = 5
LANES = 128

norm_eps = 1e-05
beta_first = 0.9
beta_second = 0.95
adam_eps = 1e-08
masked_score = -1000000000.0
score_scale = HEAD_DIM ** (-0.5)
VMEM = 60

f32 = jnp.float32
bf16 = jnp.bfloat16


def document_starts(segment):
    token_index = jnp.arange(segment.shape[0], dtype=jnp.int32)
    doc_begins = jnp.concatenate([jnp.ones((1,), dtype=jnp.bool_), segment[1:] != segment[:-1]])
    return lax.cummax(jnp.where(doc_begins, token_index, 0), axis=0)


def rotary_tables(doc_start):
    seq_len = doc_start.shape[0]
    positions = (jnp.arange(seq_len, dtype=jnp.int32) - doc_start).astype(f32)
    half_rot = ROT // 2
    frequency = jnp.power(10000.0, -2.0 * jnp.arange(half_rot, dtype=f32) / ROT)
    flat = jnp.zeros((HEAD_DIM - ROT,), f32)
    copies = LANES // HEAD_DIM
    by_lane = jnp.tile(jnp.concatenate([frequency, frequency, flat]), copies)
    sign = jnp.where(jnp.arange(LANES) % HEAD_DIM < half_rot, -1.0, 1.0)
    angles = positions[:, None] * by_lane[None, :]
    return jnp.cos(angles), jnp.sin(angles) * sign[None, :]


def masks(doc_start, valid):
    index = jnp.arange(doc_start.shape[0], dtype=jnp.int32)

    def build(query, start, key, key_valid):
        allowed = (key >= start) & (key <= query) & ((key_valid > 0) | (key == query))
        return jnp.where(allowed, 0.0, masked_score).astype(bf16)

    rows = build(index[:, None], doc_start[:, None], index[None, :], valid[None, :])
    columns = build(index[None, :], doc_start[None, :], index[:, None], valid[:, None])
    return rows, columns


def rotate(values, cosine, sine):
    half_rot = ROT // 2
    width = values.shape[1]
    lane = lax.broadcasted_iota(jnp.int32, values.shape, 1) % HEAD_DIM
    ahead = pltpu.roll(values, width - half_rot, 1)
    behind = pltpu.roll(values, half_rot, 1)
    partner = jnp.where(lane < half_rot, ahead, behind)
    return values * cosine + partner * sine


def nt(left, right):
    return lax.dot_general(left, right, (((1,), (1,)), ((), ())), preferred_element_type=f32)


def nn(left, right):
    return lax.dot_general(left, right, (((1,), (0,)), ((), ())), preferred_element_type=f32)


def tn(left, right):
    return lax.dot_general(left, right, (((0,), (0,)), ((), ())), preferred_element_type=f32)


def widen(table, width):
    return jnp.concatenate([table] * (width // LANES), axis=1)


one = pl.Buffered(1)


def resident(array):
    zeros = (0,) * array.ndim
    return pl.BlockSpec(array.shape, lambda *_: zeros, pipeline_mode=one)


def block_of(array, shape, place):
    return pl.BlockSpec(shape, lambda *_: place, pipeline_mode=one)


def staged(kernel, after, first, inputs, out_shape, name, grid, in_specs, out_specs, scratch_shapes=()):
    def without(first_ref, *refs):
        kernel(first_ref, *refs[len(after) :])

    return pl.pallas_call(
        without,
        grid_spec=pltpu.PrefetchScalarGridSpec(
            num_scalar_prefetch=1,
            grid=grid,
            in_specs=[*[pl.BlockSpec(memory_space=pl.ANY)] * len(after), *in_specs],
            out_specs=out_specs,
            scratch_shapes=scratch_shapes,
        ),
        out_shape=out_shape,
        compiler_params=pltpu.CompilerParams(vmem_limit_bytes=VMEM * 1024 * 1024),
        cost_estimate=pl.CostEstimate(flops=10**10, bytes_accessed=10**7, transcendentals=0),
        name=name,
    )(first, *after, *inputs)


def hold(arrays, after):
    def kernel(*refs):
        pass

    anywhere = pl.BlockSpec(memory_space=pl.ANY)
    return pl.pallas_call(
        kernel,
        in_specs=[anywhere] * (len(arrays) + len(after)),
        out_specs=[anywhere] * len(arrays),
        out_shape=[jax.ShapeDtypeStruct(array.shape, array.dtype) for array in arrays],
        input_output_aliases={at: at for at in range(len(arrays))},
        cost_estimate=pl.CostEstimate(flops=1000, bytes_accessed=1000, transcendentals=0),
        name="hold",
    )(*arrays, *after)


def attend_kernel(lows, first, low_ref, x_ref, bias_ref, cos_ref, sin_ref, mask_ref, *refs):
    *weights, qkv_ref, out_ref, lse_ref, k_all, v_all = refs
    seq, step = pl.program_id(0), pl.program_id(1)
    rows, width = out_ref.shape
    heads = width // HEAD_DIM
    blocks = k_all.shape[0] // rows
    cosine = widen(cos_ref[...], width)
    sine = widen(sin_ref[...], width)
    triple = []
    for which in range(3):
        total = None
        for low, ref in zip(lows, weights[which::3]):
            term = nn(x_ref[:, low : low + ref.shape[0]], ref[...])
            total = term if total is None else total + term
        triple.append(total + bias_ref[which : which + 1, :])
    query = rotate(triple[0], cosine, sine).astype(bf16)
    key = rotate(triple[1], cosine, sine).astype(bf16)
    value = triple[2].astype(bf16)
    qkv_ref[0] = query
    qkv_ref[1] = key
    qkv_ref[2] = value
    own = pl.ds(pl.multiple_of(step * rows, rows), rows)
    k_all[own, :] = key
    v_all[own, :] = value
    scaled = query * jnp.asarray(score_scale, bf16)
    head_of = lax.broadcasted_iota(jnp.int32, (rows, width), 1) // HEAD_DIM
    lane = lax.broadcasted_iota(jnp.int32, (rows, LANES), 1)
    span = step - low_ref[first + seq, step] + 1
    for count in range(1, blocks + 1):

        @pl.when(span == count)
        def _(count=count):
            begin = pl.multiple_of((step - (count - 1)) * rows, rows)
            keys = k_all[pl.ds(begin, count * rows), :]
            values = v_all[pl.ds(begin, count * rows), :]
            mask = mask_ref[:, pl.ds(begin, count * rows)].astype(f32)
            result = jnp.zeros((rows, width), f32)
            stats = jnp.zeros((rows, LANES), f32)
            for head in range(heads):
                mine = head_of == head
                scores = nt(jnp.where(mine, scaled, jnp.zeros_like(scaled)), keys) + mask
                top = jnp.max(scores, axis=1, keepdims=True)
                weights = jnp.exp(scores - top)
                total = jnp.sum(weights, axis=1, keepdims=True)
                mixed = nn(weights.astype(bf16), values) * (1.0 / total)
                result = jnp.where(mine, mixed, result)
                stats = jnp.where(lane == head, top + jnp.log(total), stats)
            out_ref[...] = result.astype(bf16)
            lse_ref[...] = jnp.transpose(stats)[: lse_ref.shape[0], :]


def attend(after, normed, first, count, entry, bias, cosine, sine, mask, low, rows):
    pieces, lows = entry
    _, seq_len, model_width = normed.shape
    width = bias.shape[1]
    blocks = seq_len // rows
    stat_rows = 8
    side = (pieces[0].shape[1] - 3 * width) // width

    def rows_of(columns):
        return pl.BlockSpec((None, rows, columns), lambda s, i, low: (first + s, i, 0))

    return staged(
        partial(attend_kernel, lows, first),
        after,
        low,
        [normed, bias, cosine, sine, mask, *[piece for piece in pieces for _ in range(3)]],
        [
            jax.ShapeDtypeStruct((3, count, seq_len, width), bf16),
            jax.ShapeDtypeStruct((count, seq_len, width), bf16),
            jax.ShapeDtypeStruct((count, stat_rows, seq_len), f32),
        ],
        "attend",
        grid=(count, blocks),
        in_specs=[
            rows_of(model_width),
            resident(bias),
            rows_of(LANES),
            rows_of(LANES),
            rows_of(seq_len),
            *[
                block_of(piece, (piece.shape[0], width), (0, side + which))
                for piece in pieces
                for which in range(3)
            ],
        ],
        out_specs=[
            pl.BlockSpec((3, None, rows, width), lambda s, i, low: (0, s, i, 0)),
            pl.BlockSpec((None, rows, width), lambda s, i, low: (s, i, 0)),
            pl.BlockSpec((None, stat_rows, rows), lambda s, i, low: (s, 0, i)),
        ],
        scratch_shapes=[pltpu.VMEM((seq_len, width), bf16), pltpu.VMEM((seq_len, width), bf16)],
    )


def attend_back_kernel(
    lows, first, low_ref, q_ref, k_ref, v_ref, o_ref, g_ref, lse_ref, mask_ref, cos_ref, sin_ref, *refs
):
    *weights, out_ref, sum_ref, dk_all, dv_all, k_turned = refs
    seq, step = pl.program_id(0), pl.program_id(1)
    rows, width = q_ref.shape
    heads = width // HEAD_DIM
    seq_len = dk_all.shape[0]
    blocks = seq_len // rows

    @pl.when(step == 0)
    def _():
        dk_all[...] = jnp.zeros_like(dk_all)
        dv_all[...] = jnp.zeros_like(dv_all)
        k_turned[...] = jnp.transpose(k_ref[...])

    @pl.when((step == 0) & (seq == 0))
    def _():
        sum_ref[...] = jnp.zeros_like(sum_ref)

    scaled = q_ref[...] * jnp.asarray(score_scale, bf16)
    d_out = None
    for low, ref in zip(lows, weights):
        term = nt(g_ref[:, low : low + ref.shape[1]], ref[...])
        d_out = term if d_out is None else d_out + term
    d_out = d_out.astype(bf16)
    zero = jnp.zeros_like(d_out)
    head_of = lax.broadcasted_iota(jnp.int32, (rows, width), 1) // HEAD_DIM
    product = d_out.astype(f32) * o_ref[...].astype(f32)
    high = product.astype(bf16)
    rest = (product - high.astype(f32)).astype(bf16)
    row_of = lax.broadcasted_iota(jnp.int32, (8, width), 0)
    by_head = (lax.broadcasted_iota(jnp.int32, (8, width), 1) // HEAD_DIM == row_of).astype(bf16)
    delta = nt(by_head, high) + nt(by_head, rest)
    own = pl.ds(pl.multiple_of(step * rows, rows), rows)
    span = step - low_ref[first + seq, step] + 1
    for count in range(1, blocks + 1):

        @pl.when(span == count)
        def _(count=count):
            begin = pl.multiple_of((step - (count - 1)) * rows, rows)
            reach = pl.ds(begin, count * rows)
            keys = k_ref[reach, :]
            values = v_ref[reach, :]
            mask = mask_ref[reach, :].astype(f32)
            probs_side, scores_side, queries_down, d_outs_down, d_query = [], [], [], [], []
            for head in range(heads):
                mine = head_of == head
                query = jnp.where(mine, scaled, zero)
                d_mine = jnp.where(mine, d_out, zero)
                scores = nt(keys, query) + mask
                probs = jnp.exp(scores - lse_ref[head : head + 1, :])
                d_probs = nt(values, d_mine)
                d_scores = (probs * (d_probs - delta[head : head + 1, :])).astype(bf16)
                d_query.append(nn(k_turned[head * HEAD_DIM : (head + 1) * HEAD_DIM, reach], d_scores))
                probs_side.append(probs.astype(bf16))
                scores_side.append(d_scores)
                queries_down.append(query)
                d_outs_down.append(d_mine)
            dv_all[reach, :] += nn(
                jnp.concatenate(probs_side, axis=1), jnp.concatenate(d_outs_down, axis=0)
            )
            dk_all[reach, :] += nn(
                jnp.concatenate(scores_side, axis=1), jnp.concatenate(queries_down, axis=0)
            )
            cosine = widen(cos_ref[own, :], width)
            sine = widen(sin_ref[own, :], width)
            d_rot = jnp.transpose(jnp.concatenate(d_query, axis=0)) * score_scale
            low_query = rotate(d_rot, cosine, -sine).astype(bf16)
            out_ref[own, :width] = low_query
            sum_ref[0:1, :] += jnp.sum(low_query.astype(f32), axis=0, keepdims=True)

    @pl.when(step == blocks - 1)
    def _():
        cosine = widen(cos_ref[...], width)
        sine = widen(sin_ref[...], width)
        low_key = rotate(dk_all[...], cosine, -sine).astype(bf16)
        low_value = dv_all[...].astype(bf16)
        out_ref[:, width : 2 * width] = low_key
        out_ref[:, 2 * width :] = low_value
        sum_ref[1:2, :] += jnp.sum(low_key.astype(f32), axis=0, keepdims=True)
        sum_ref[2:3, :] += jnp.sum(low_value.astype(f32), axis=0, keepdims=True)


def attend_back(after, qkv, attended, cot, first, count, exits, lse, mask, cosine, sine, low, rows):
    pieces, lows = exits
    _, seq_len, model_width = cot.shape
    width = qkv.shape[3]
    blocks = seq_len // rows
    stat_rows = lse.shape[1]
    units = pieces[0].shape[0] - width

    def whole_of(columns):
        return pl.BlockSpec((None, seq_len, columns), lambda s, i, low: (first + s, 0, 0))

    def rows_of(columns):
        return pl.BlockSpec((None, rows, columns), lambda s, i, low: (first + s, i, 0))

    return staged(
        partial(attend_back_kernel, lows, first),
        after,
        low,
        [qkv, qkv, qkv, attended, cot, lse, mask, cosine, sine, *pieces],
        [
            jax.ShapeDtypeStruct((count, seq_len, 3 * width), bf16),
            jax.ShapeDtypeStruct((8, width), f32),
        ],
        "attend_back",
        grid=(count, blocks),
        in_specs=[
            pl.BlockSpec((None, None, rows, width), lambda s, i, low: (0, first + s, i, 0)),
            pl.BlockSpec((None, None, seq_len, width), lambda s, i, low: (1, first + s, 0, 0)),
            pl.BlockSpec((None, None, seq_len, width), lambda s, i, low: (2, first + s, 0, 0)),
            rows_of(width),
            rows_of(model_width),
            pl.BlockSpec((None, stat_rows, rows), lambda s, i, low: (first + s, 0, i)),
            pl.BlockSpec((None, seq_len, rows), lambda s, i, low: (first + s, 0, i)),
            whole_of(LANES),
            whole_of(LANES),
            *[block_of(piece, (width, piece.shape[1]), (units // width, 0)) for piece in pieces],
        ],
        out_specs=[
            pl.BlockSpec((None, seq_len, 3 * width), lambda s, i, low: (s, 0, 0)),
            pl.BlockSpec((8, width), lambda s, i, low: (0, 0)),
        ],
        scratch_shapes=[
            pltpu.VMEM((seq_len, width), f32),
            pltpu.VMEM((seq_len, width), f32),
            pltpu.VMEM((width, seq_len), bf16),
        ],
    )


def gelu_kernel(lows, tick_ref, x_ref, bias_ref, *refs):
    *weights, hidden_ref, slope_ref = refs
    pre = bias_ref[...]
    for low, ref in zip(lows, weights):
        pre = pre + nn(x_ref[:, low : low + ref.shape[0]], ref[...])
    scale = (2.0 / math.pi) ** 0.5
    square = pre * pre
    half = 0.5 + 0.5 * jnp.tanh(pre * (scale + (scale * 0.044715) * square))
    hidden = pre * half
    hidden_ref[...] = hidden.astype(bf16)
    slope = half + hidden * (1.0 - half) * (2.0 * scale + (6.0 * scale * 0.044715) * square)
    slope_ref[...] = slope.astype(bf16)


def gelu_units(after, tick, normed, entry, bias, rows):
    pieces, lows = entry
    count, seq_len, model_width = normed.shape
    units = bias.shape[1]
    block = pl.BlockSpec((None, rows, units), lambda s, i, _: (s, i, 0))
    return staged(
        partial(gelu_kernel, lows),
        after,
        tick,
        [normed, bias, *pieces],
        [jax.ShapeDtypeStruct((count, seq_len, units), bf16)] * 2,
        "gelu_units",
        grid=(count, seq_len // rows),
        in_specs=[
                pl.BlockSpec((None, rows, model_width), lambda s, i, _: (s, i, 0)),
                resident(bias),
                *[block_of(piece, (piece.shape[0], units), (0, 0)) for piece in pieces],
            ],
        out_specs=[block, block],
    )


def out_kernel(lows, tick_ref, a_ref, h_ref, *refs):
    *weights, out_ref = refs
    units = h_ref.shape[1]
    for low, ref in zip(lows, weights):
        term = nn(h_ref[...], ref[:units, :]) + nn(a_ref[...], ref[units:, :])
        out_ref[:, low : low + ref.shape[1]] = term.astype(bf16)


def out_sums(after, tick, attended, hidden, exits, rows):
    pieces, lows = exits
    count, seq_len, width = attended.shape
    units = hidden.shape[2]
    model_width = sum(piece.shape[1] for piece in pieces)

    def rows_of(columns):
        return pl.BlockSpec((None, rows, columns), lambda s, i, _: (s, i, 0))

    return staged(
        partial(out_kernel, lows),
        after,
        tick,
        [attended, hidden, *pieces],
        jax.ShapeDtypeStruct((count, seq_len, model_width), bf16),
        "out_sums",
        grid=(count, seq_len // rows),
        in_specs=[rows_of(width), rows_of(units), *[resident(piece) for piece in pieces]],
        out_specs=rows_of(model_width),
    )


def back_rows_kernel(entry_lows, exit_lows, tick_ref, g_ref, slope_ref, c_ref, *refs):
    entry, exits = refs[: len(entry_lows)], refs[len(entry_lows) : len(entry_lows) + len(exit_lows)]
    hidden_ref, normed_ref, sum_ref = refs[-3:]
    units = slope_ref.shape[1]

    @pl.when((pl.program_id(0) == 0) & (pl.program_id(1) == 0))
    def _():
        sum_ref[...] = jnp.zeros_like(sum_ref)

    total = None
    for low, ref in zip(exit_lows, exits):
        term = nt(g_ref[:, low : low + ref.shape[1]], ref[...])
        total = term if total is None else total + term
    d_hidden = (total * slope_ref[...].astype(f32)).astype(bf16)
    hidden_ref[...] = d_hidden
    sum_ref[0:1, :] += jnp.sum(d_hidden.astype(f32), axis=0, keepdims=True)
    for low, ref in zip(entry_lows, entry):
        term = nt(d_hidden, ref[:, :units]) + nt(c_ref[...], ref[:, units:])
        normed_ref[:, low : low + ref.shape[0]] = term.astype(bf16)


def back_rows(after, tick, cot, slope, d_cat, entry, exits, rows):
    pieces, lows = entry
    exit_pieces, exit_lows = exits
    count, seq_len, model_width = cot.shape
    units = slope.shape[2]

    def rows_of(columns):
        return pl.BlockSpec((None, rows, columns), lambda s, i, _: (s, i, 0))

    return staged(
        partial(back_rows_kernel, lows, exit_lows),
        after,
        tick,
        [cot, slope, d_cat, *pieces, *exit_pieces],
        [
            jax.ShapeDtypeStruct((count, seq_len, units), bf16),
            jax.ShapeDtypeStruct((count, seq_len, model_width), bf16),
            jax.ShapeDtypeStruct((8, units), f32),
        ],
        "back_rows",
        grid=(count, seq_len // rows),
        in_specs=[
            rows_of(model_width),
            rows_of(units),
            rows_of(d_cat.shape[2]),
            *[resident(piece) for piece in pieces],
            *[block_of(piece, (units, piece.shape[1]), (0, 0)) for piece in exit_pieces],
        ],
        out_specs=[
            rows_of(units),
            rows_of(model_width),
            pl.BlockSpec((8, units), lambda s, i, _: (0, 0)),
        ],
    )


def targets(ranks, parts):
    if ranks == 4:
        half = parts // 2
        return [(0, half), (half, parts)] + [(at * parts, (at + 1) * parts) for at in range(1, ranks)]
    return [(at * parts, (at + 1) * parts) for at in range(ranks)]


def rows_grad_kernel(spans, tick_ref, left, right, *outs):
    step = pl.program_id(0)
    for (begin, end), out_ref in zip(spans, outs):

        @pl.when((step >= begin) & (step < end))
        def _(out_ref=out_ref):
            out_ref[...] = tn(left[...], right[...]).astype(bf16)


def rows_grad(after, tick, left, right, ranks, name):
    tokens, model_width = left.shape
    columns = right.shape[1]
    piece = model_width // ranks
    parts = max(2, piece // 256)
    block = piece // parts
    spans = targets(ranks, parts)

    def column_block(i, _):
        return (0, (ranks - 1 - i // parts) * parts + i % parts)

    def target_block(begin, end):
        return lambda i, _: (jnp.clip(i - begin, 0, end - begin - 1), 0)

    return staged(
        partial(rows_grad_kernel, spans),
        after,
        tick,
        [left, right],
        [jax.ShapeDtypeStruct(((end - begin) * block, columns), bf16) for begin, end in spans],
        name,
        grid=(ranks * parts,),
        in_specs=[pl.BlockSpec((tokens, block), column_block), resident(right)],
        out_specs=[pl.BlockSpec((block, columns), target_block(*span)) for span in spans],
    )


def columns_grad_kernel(spans, tick_ref, *refs):
    kinds = (len(refs) - 1 - len(spans)) // 2
    left, right, outs, turned = refs[:kinds], refs[kinds], refs[kinds + 1 : -kinds], refs[-kinds:]
    step = pl.program_id(0)

    @pl.when(step == 0)
    def _():
        for source, target in zip(left, turned):
            target[...] = jnp.transpose(source[...])

    for (begin, end), out_ref in zip(spans, outs):

        @pl.when((step >= begin) & (step < end))
        def _(out_ref=out_ref):
            first = 0
            for kind in range(kinds):
                total = nn(turned[kind][...], right[...])
                out_ref[first : first + total.shape[0], :] = total.astype(bf16)
                first += total.shape[0]


def columns_grad(after, tick, lefts, right, ranks, name):
    tokens, model_width = right.shape
    piece = model_width // ranks
    parts = 2
    block = piece // parts
    spans = targets(ranks, parts)
    height = sum(left.shape[1] for left in lefts)

    def column_block(i, _):
        return (0, (ranks - 1 - i // parts) * parts + i % parts)

    def target_block(begin, end):
        return lambda i, _: (0, jnp.clip(i - begin, 0, end - begin - 1))

    return staged(
        partial(columns_grad_kernel, spans),
        after,
        tick,
        [*lefts, right],
        [jax.ShapeDtypeStruct((height, (end - begin) * block), bf16) for begin, end in spans],
        name,
        grid=(ranks * parts,),
        in_specs=[*[resident(left) for left in lefts], pl.BlockSpec((tokens, block), column_block)],
        out_specs=[pl.BlockSpec((height, block), target_block(*span)) for span in spans],
        scratch_shapes=[pltpu.VMEM((left.shape[1], tokens), bf16) for left in lefts],
    )


def adam_step(moment_one, moment_two, gradient):
    moment_one = beta_first * moment_one + (1.0 - beta_first) * gradient
    moment_two = beta_second * moment_two + (1.0 - beta_second) * gradient * gradient
    first_fix = 1.0 - beta_first**STEP
    second_fix = 1.0 - beta_second**STEP
    update = moment_one / first_fix / (jnp.sqrt(moment_two / second_fix) + adam_eps)
    return update, moment_one, moment_two


def adam_update(moments, gradient):
    update, moment_one, moment_two = adam_step(moments[0], moments[1], gradient)
    return update, jnp.stack([moment_one, moment_two])


def adam_kernel(scale, tick_ref, moments_ref, *refs):
    *terms, update_ref, new_ref = refs
    gradient = terms[0][...].astype(f32)
    for term in terms[1:]:
        gradient = gradient + term[...].astype(f32)
    update, moment_one, moment_two = adam_step(moments_ref[0], moments_ref[1], gradient * scale)
    update_ref[...] = update
    new_ref[0] = moment_one
    new_ref[1] = moment_two


def adam_sum(after, tick, moments, terms, scale, row, column, parts):
    groups = parts if parts else 1
    height, width = moments.shape[-2:]
    rows = min(256, height)
    steps = height // rows
    if parts:
        moment_block = pl.BlockSpec((2, None, rows, width), lambda p, i, _: (0, p, i, 0))
        update_block = pl.BlockSpec((None, rows, width), lambda p, i, _: (p, i, 0))
    else:
        moment_block = pl.BlockSpec((2, rows, width), lambda p, i, _: (0, i, 0))
        update_block = pl.BlockSpec((rows, width), lambda p, i, _: (i, 0))
    term_block = pl.BlockSpec((rows, width), lambda p, i, _: (row // rows + i, column // width + p))
    return staged(
        partial(adam_kernel, scale),
        after,
        tick,
        [moments, *terms],
        [
            jax.ShapeDtypeStruct(moments.shape[1:], f32),
            jax.ShapeDtypeStruct(moments.shape, f32),
        ],
        "adam_sum",
        grid=(groups, steps),
        in_specs=[moment_block, *[term_block] * len(terms)],
        out_specs=[update_block, moment_block],
    )


def from_relative(ref, rank, ranks, piece):
    return jnp.concatenate(
        [ref[:, pl.ds(pl.multiple_of((rank ^ j) * piece, piece), piece)] for j in range(ranks)], axis=1
    )


def input_grad_kernel(ranks, rank_ref, x_ref, g_ref, norm_ref, d_ref, out_ref, sum_ref):
    piece = x_ref.shape[1] // ranks
    inputs = x_ref[...].astype(f32)
    centred = inputs - jnp.mean(inputs, axis=1, keepdims=True)
    variance = jnp.mean(centred * centred, axis=1, keepdims=True)
    inv_std = lax.rsqrt(variance + norm_eps)
    unit = centred * inv_std
    cot = g_ref[...].astype(f32)

    @pl.when(pl.program_id(0) == 0)
    def _():
        sum_ref[...] = jnp.zeros_like(sum_ref)

    d_normed = from_relative(d_ref, rank_ref[0], ranks, piece).astype(f32)
    d_unit = d_normed * norm_ref[0:1, :]
    mean_unit = jnp.mean(d_unit, axis=1, keepdims=True)
    mean_cross = jnp.mean(d_unit * unit, axis=1, keepdims=True)
    out_ref[...] = (cot + inv_std * (d_unit - mean_unit - unit * mean_cross)).astype(bf16)
    sum_ref[0:1, :] += jnp.sum(d_normed * unit, axis=0, keepdims=True)
    sum_ref[1:2, :] += jnp.sum(d_normed, axis=0, keepdims=True)
    sum_ref[2:3, :] += jnp.sum(cot, axis=0, keepdims=True)


def input_gradient(after, rank, tokens, cot_rows, norm_params, grads, ranks):
    count, rows, model_width = tokens.shape
    block = pl.BlockSpec((None, rows, model_width), lambda s, _: (s, 0, 0))
    return staged(
        partial(input_grad_kernel, ranks),
        after,
        rank,
        [tokens, cot_rows, norm_params, grads],
        [
            jax.ShapeDtypeStruct(tokens.shape, bf16),
            jax.ShapeDtypeStruct((8, model_width), f32),
        ],
        "input_grad",
        grid=(count,),
        in_specs=[block, block, resident(norm_params), block],
        out_specs=[block, pl.BlockSpec((8, model_width), lambda s, _: (0, 0))],
    )


def output_kernel(ranks, rank_ref, x_ref, bias_ref, o_ref, out_ref):
    piece = x_ref.shape[1] // ranks
    branches = from_relative(o_ref, rank_ref[0], ranks, piece).astype(f32)
    total = x_ref[...].astype(f32) + branches + bias_ref[0:1, :] + bias_ref[1:2, :]
    out_ref[...] = total.astype(bf16)


def layer_output(after, rank, tokens, output_bias, outs, ranks):
    count, rows, model_width = tokens.shape
    block = pl.BlockSpec((None, rows, model_width), lambda s, _: (s, 0, 0))
    return staged(
        partial(output_kernel, ranks),
        after,
        rank,
        [tokens, output_bias, outs],
        jax.ShapeDtypeStruct(tokens.shape, bf16),
        "layer_output",
        grid=(count,),
        in_specs=[block, resident(output_bias), block],
        out_specs=block,
    )


def swap(array, distance):
    size = lax.axis_size("dp")
    return lax.ppermute(array, "dp", [(i, i ^ distance) for i in range(size)])


def plus(left, right):
    return (left.astype(f32) + right.astype(f32)).astype(bf16)


class Line:
    def __init__(self, tick):
        self.tick, self.pending = tick, []

    def wait(self, *arrays):
        self.pending += arrays

    def run(self, stage, *arguments):
        result = stage(self.pending, *arguments)
        self.pending = [jax.tree.leaves(result)[0]]
        return result


class Gather:
    def __init__(self, own, axis):
        self.size = lax.axis_size("dp")
        self.own, self.axis = own, axis
        self.sent = [swap(own, j) for j in ((1, 2) if self.size == 4 else range(1, self.size))]
        self.rest = []

    def forward(self, after):
        if self.size == 4:
            if after:
                self.sent = hold(self.sent, after)
            half = self.own.shape[self.axis] // 2
            near, far = self.sent
            top = lax.slice_in_dim(near, 0, half, axis=self.axis)
            bottom = lax.slice_in_dim(far, half, 2 * half, axis=self.axis)
            self.rest = [swap(top, 2), swap(bottom, 1)]

    def pieces(self):
        pieces = [self.own, *self.sent, *self.rest]
        lows, low = [], 0
        for piece in pieces:
            lows.append(low)
            low += piece.shape[self.axis]
        return pieces, tuple(lows)


class Scatter:
    def __init__(self, pieces, axis, after=()):
        self.size = lax.axis_size("dp")
        self.axis = axis
        if self.size == 4:
            *ends, self.far, self.near, self.own = pieces
            top, bottom = hold(ends, after) if after else ends
            self.ends = [top, bottom]
            self.first = [swap(top, 1), swap(bottom, 2)]
        else:
            self.ends = []
            self.own = pieces[-1]
            self.first = [swap(piece, self.size - 1 - at) for at, piece in enumerate(pieces[:-1])]

    def forward(self, after=()):
        if self.size != 4:
            return [self.own, *self.first]
        top, bottom = hold(self.first, after) if after else self.first
        half = self.near.shape[self.axis] // 2

        def halves(array):
            return [lax.slice_in_dim(array, at, at + half, axis=self.axis) for at in (0, half)]

        near, far = halves(self.near), halves(self.far)
        near = jnp.concatenate([near[0], plus(near[1], bottom)], axis=self.axis)
        far = jnp.concatenate([plus(far[0], top), far[1]], axis=self.axis)
        return [self.own, swap(near, 1), swap(far, 2)]


def sum_axis(array, axis, distances):
    size = lax.axis_size(axis)
    offsets = [0]
    for distance in distances:
        offsets += [offset + distance for offset in offsets]
    terms = [lax.ppermute(array, axis, [(i, i ^ offset) for i in range(size)]) for offset in offsets[1:]]
    terms = [array, *terms]
    while len(terms) > 1:
        terms = [left + right for left, right in zip(terms[::2], terms[1::2])]
    return terms[0]


def sum_over(array, axis):
    distances = [1 << bit for bit in range((lax.axis_size(axis) - 1).bit_length())]
    first = len(distances) % 2
    if first:
        array = sum_axis(array, axis, distances[:1])
    for at in range(first, len(distances), 2):
        array = sum_axis(array, axis, distances[at : at + 2])
    return array


def body(
    tokens,
    cotangent,
    segments,
    valid_mask,
    norm_params,
    norm_moments,
    heads_weight,
    heads_moments,
    heads_bias,
    heads_bias_moments,
    merge_weight,
    merge_moments,
    expand_weight,
    expand_moments,
    expand_bias,
    expand_bias_moments,
    shrink_weight,
    shrink_moments,
    output_bias,
    output_bias_moments,
):
    ranks = lax.axis_size("dp")
    rank = lax.axis_index("dp")
    count, _, model_width = tokens.shape
    seq_len = segments.shape[1]
    width = heads_weight.shape[2]
    piece = model_width // ranks
    rows = min(256, seq_len)

    def relative(array):
        parts = [
            lax.dynamic_slice_in_dim(array, (rank ^ j) * piece, piece, array.ndim - 1) for j in range(ranks)
        ]
        return jnp.concatenate(parts, axis=-1)

    norm_rel = relative(norm_params)
    norm_gain, norm_shift = norm_rel[0], norm_rel[1]
    inputs = relative(tokens).astype(f32)
    cot_rows = relative(cotangent)
    row_mean = jnp.mean(inputs, axis=-1, keepdims=True)
    centred = inputs - row_mean
    variance = jnp.mean(centred * centred, axis=-1, keepdims=True)
    inv_std = lax.rsqrt(variance + norm_eps)
    unit = centred * inv_std
    normed_rows = (unit * norm_gain + norm_shift).astype(bf16)

    def gather_rows(array):
        return lax.all_gather(array, "tensor", axis=1, tiled=True)

    def scatter_rows(array):
        return lax.psum_scatter(array, "tensor", scatter_dimension=1, tiled=True)

    tick = segments[0, :1]
    line = Line(tick)
    rank_here = rank.reshape(1).astype(jnp.int32)
    normed = gather_rows(normed_rows)
    cot = gather_rows(cot_rows)

    entry_own = jnp.concatenate([expand_weight, *[heads_weight[c] for c in range(3)]], axis=1).astype(bf16)
    entry_gather = Gather(entry_own, 0)
    entry_gather.forward(())
    entry = entry_gather.pieces()
    exit_own = jnp.concatenate([shrink_weight, merge_weight], axis=0).astype(bf16)
    exit_gather = Gather(hold([exit_own], entry_gather.rest or entry_gather.sent)[0], 1)
    starts = jnp.stack([document_starts(segments[s]) for s in range(count)])
    cosine, sine = jax.vmap(rotary_tables)(starts)
    mask_rows, mask_columns = jax.vmap(masks)(starts, valid_mask)
    lows = starts[:, ::rows] // rows
    expand_row = expand_bias.reshape(1, -1)
    big = min(512, seq_len)
    units_local = expand_weight.shape[1]

    line.wait(mask_columns)
    qkv, attended, lse = line.run(
        attend, normed, 0, count, entry, heads_bias, cosine, sine, mask_rows, lows, rows
    )
    exit_gather.forward([attended])
    exits = exit_gather.pieces()
    hidden, slope = line.run(gelu_units, tick, normed, entry, expand_row, big)
    partials = line.run(out_sums, tick, attended, hidden, exits, big)

    outs = scatter_rows(partials)

    def tokens_of(array):
        return array.reshape(-1, array.shape[-1])

    def adam(moments, terms, row=0, column=0, parts=0):
        return line.run(adam_sum, tick, moments, terms, 1.0 / seq_len, row, column, parts)

    exit_parts = line.run(
        columns_grad, tick, [tokens_of(hidden), tokens_of(attended)], tokens_of(cot), ranks, "exit_grad"
    )
    exit_scatter = Scatter(exit_parts, 1)
    d_cat, bias_sums = line.run(
        attend_back, qkv, attended, cot, 0, count, exits, lse, mask_columns, cosine, sine, lows, rows
    )
    exit_terms = exit_scatter.forward([d_cat])
    d_hidden, sums, hidden_sums = line.run(back_rows, tick, cot, slope, d_cat, entry, exits, big)
    grads = scatter_rows(hold([sums], exit_terms[1:])[0])
    line.wait(outs)
    expand_parts = line.run(rows_grad, tick, tokens_of(normed), tokens_of(d_hidden), ranks, "expand_grad")
    expand_scatter = Scatter(expand_parts, 0)
    expand_terms = expand_scatter.forward()
    heads_parts = line.run(rows_grad, tick, tokens_of(normed), tokens_of(d_cat), ranks, "heads_grad")
    heads_scatter = Scatter(heads_parts, 0, expand_scatter.first)
    heads_terms = heads_scatter.forward()
    line.wait(*heads_scatter.ends)
    shrink_upd, shrink_mom = adam(shrink_moments, exit_terms)
    merge_upd, merge_mom = adam(merge_moments, exit_terms, row=units_local)
    line.wait(*heads_scatter.first)
    output = line.run(layer_output, rank_here, tokens, output_bias, outs, ranks)
    expand_upd, expand_mom = adam(expand_moments, expand_terms)
    line.wait(*heads_terms[1:])
    input_grad, column_sums = line.run(
        input_gradient, rank_here, tokens, cotangent, norm_params, grads, ranks
    )
    heads_upd, heads_mom = adam(heads_moments, heads_terms, parts=3)
    column_sums = sum_over(column_sums, "tensor")
    bias_sums = jnp.concatenate([bias_sums[:3].reshape(-1), hidden_sums[0]])
    totals = sum_over(jnp.concatenate([column_sums[:3].reshape(-1), bias_sums]), "dp")
    norm_total = totals[: 2 * model_width].reshape(2, model_width)
    output_bias_total = totals[2 * model_width : 3 * model_width]
    bias_total = totals[3 * model_width :]
    heads_bias_total = bias_total[: 3 * width].reshape(3, width)
    expand_bias_total = bias_total[3 * width :]

    scale_back = 1.0 / seq_len
    norm_upd, norm_mom = adam_update(norm_moments, norm_total * scale_back)
    hbias_upd, hbias_mom = adam_update(heads_bias_moments, heads_bias_total * scale_back)
    ebias_upd, ebias_mom = adam_update(expand_bias_moments, expand_bias_total * scale_back)
    output_bias_grad = jnp.stack([output_bias_total, output_bias_total]) * scale_back
    obias_upd, obias_mom = adam_update(output_bias_moments, output_bias_grad)
    return (
        output,
        input_grad,
        norm_upd,
        norm_mom,
        heads_upd,
        heads_mom,
        hbias_upd,
        hbias_mom,
        merge_upd,
        merge_mom,
        expand_upd,
        expand_mom,
        ebias_upd,
        ebias_mom,
        shrink_upd,
        shrink_mom,
        obias_upd,
        obias_mom,
    )


def solution(mesh):
    placed = (
        P("dp", "tensor", None),
        P("dp", "tensor", None),
        P("dp", None),
        P("dp", None),
        P(),
        P(),
        P(None, "dp", "tensor"),
        P(None, None, "dp", "tensor"),
        P(None, "tensor"),
        P(None, None, "tensor"),
        P("tensor", "dp"),
        P(None, "tensor", "dp"),
        P("dp", "tensor"),
        P(None, "dp", "tensor"),
        P("tensor"),
        P(None, "tensor"),
        P("tensor", "dp"),
        P(None, "tensor", "dp"),
        P(),
        P(),
    )
    return jax.shard_map(
        body,
        mesh=mesh,
        in_specs=placed,
        out_specs=(placed[0], placed[0], P(), P(), *placed[6:18], P(), P()),
        check_vma=False,
    )
```

```python
import math
from functools import partial

import jax
import jax.numpy as jnp
from jax import lax
from jax.experimental import pallas as pl
from jax.experimental.pallas import tpu as pltpu
from jax.sharding import PartitionSpec as P

HEAD_DIM = 64
ROT = 32
STEP = 5
LANES = 128

norm_eps = 1e-05
beta_first = 0.9
beta_second = 0.95
adam_eps = 1e-08
masked_score = -1000000000.0
score_scale = HEAD_DIM ** (-0.5)
VMEM = 60

f32 = jnp.float32
bf16 = jnp.bfloat16


def document_starts(segment):
    token_index = jnp.arange(segment.shape[0], dtype=jnp.int32)
    doc_begins = jnp.concatenate([jnp.ones((1,), dtype=jnp.bool_), segment[1:] != segment[:-1]])
    return lax.cummax(jnp.where(doc_begins, token_index, 0), axis=0)


def rotary_tables(doc_start):
    seq_len = doc_start.shape[0]
    positions = (jnp.arange(seq_len, dtype=jnp.int32) - doc_start).astype(f32)
    half_rot = ROT // 2
    frequency = jnp.power(10000.0, -2.0 * jnp.arange(half_rot, dtype=f32) / ROT)
    flat = jnp.zeros((HEAD_DIM - ROT,), f32)
    copies = LANES // HEAD_DIM
    by_lane = jnp.tile(jnp.concatenate([frequency, frequency, flat]), copies)
    sign = jnp.where(jnp.arange(LANES) % HEAD_DIM < half_rot, -1.0, 1.0)
    angles = positions[:, None] * by_lane[None, :]
    return jnp.cos(angles), jnp.sin(angles) * sign[None, :]


def masks(doc_start, valid):
    index = jnp.arange(doc_start.shape[0], dtype=jnp.int32)

    def build(query, start, key, key_valid):
        allowed = (key >= start) & (key <= query) & ((key_valid > 0) | (key == query))
        return jnp.where(allowed, 0.0, masked_score).astype(bf16)

    rows = build(index[:, None], doc_start[:, None], index[None, :], valid[None, :])
    columns = build(index[None, :], doc_start[None, :], index[:, None], valid[:, None])
    return rows, columns


def rotate(values, cosine, sine):
    half_rot = ROT // 2
    width = values.shape[1]
    lane = lax.broadcasted_iota(jnp.int32, values.shape, 1) % HEAD_DIM
    ahead = pltpu.roll(values, width - half_rot, 1)
    behind = pltpu.roll(values, half_rot, 1)
    partner = jnp.where(lane < half_rot, ahead, behind)
    return values * cosine + partner * sine


def nt(left, right):
    return lax.dot_general(left, right, (((1,), (1,)), ((), ())), preferred_element_type=f32)


def nn(left, right):
    return lax.dot_general(left, right, (((1,), (0,)), ((), ())), preferred_element_type=f32)


def tn(left, right):
    return lax.dot_general(left, right, (((0,), (0,)), ((), ())), preferred_element_type=f32)


def widen(table, width):
    return jnp.concatenate([table] * (width // LANES), axis=1)


one = pl.Buffered(1)


def resident(array):
    zeros = (0,) * array.ndim
    return pl.BlockSpec(array.shape, lambda *_: zeros, pipeline_mode=one)


def block_of(array, shape, place):
    return pl.BlockSpec(shape, lambda *_: place, pipeline_mode=one)


def staged(
    kernel, after, first, inputs, out_shape, name, grid, in_specs, out_specs, scratch_shapes=(), flops=10**10
):
    def without(first_ref, *refs):
        kernel(first_ref, *refs[len(after) :])

    return pl.pallas_call(
        without,
        grid_spec=pltpu.PrefetchScalarGridSpec(
            num_scalar_prefetch=1,
            grid=grid,
            in_specs=[*[pl.BlockSpec(memory_space=pl.ANY)] * len(after), *in_specs],
            out_specs=out_specs,
            scratch_shapes=scratch_shapes,
        ),
        out_shape=out_shape,
        compiler_params=pltpu.CompilerParams(vmem_limit_bytes=VMEM * 1024 * 1024),
        cost_estimate=pl.CostEstimate(flops=flops, bytes_accessed=flops // 1000, transcendentals=0),
        name=name,
    )(first, *after, *inputs)


def hold(arrays, after):
    def kernel(*refs):
        pass

    anywhere = pl.BlockSpec(memory_space=pl.ANY)
    return pl.pallas_call(
        kernel,
        in_specs=[anywhere] * (len(arrays) + len(after)),
        out_specs=[anywhere] * len(arrays),
        out_shape=[jax.ShapeDtypeStruct(array.shape, array.dtype) for array in arrays],
        input_output_aliases={at: at for at in range(len(arrays))},
        cost_estimate=pl.CostEstimate(flops=1000, bytes_accessed=1000, transcendentals=0),
        name="hold",
    )(*arrays, *after)


def attend_kernel(lows, first, low_ref, x_ref, bias_ref, cos_ref, sin_ref, mask_ref, *refs):
    *weights, qkv_ref, out_ref, rest_ref, lse_ref, k_all, v_all = refs
    seq, step = pl.program_id(0), pl.program_id(1)
    rows, width = out_ref.shape
    heads = width // HEAD_DIM
    blocks = k_all.shape[0] // rows
    cosine = widen(cos_ref[...], width)
    sine = widen(sin_ref[...], width)
    triple = []
    for which in range(3):
        total = None
        for low, ref in zip(lows, weights[which::3]):
            term = nn(x_ref[:, low : low + ref.shape[0]], ref[...])
            total = term if total is None else total + term
        triple.append(total + bias_ref[which : which + 1, :])
    query = rotate(triple[0], cosine, sine).astype(bf16)
    key = rotate(triple[1], cosine, sine).astype(bf16)
    value = triple[2].astype(bf16)
    qkv_ref[0] = query
    qkv_ref[1] = key
    qkv_ref[2] = value
    own = pl.ds(pl.multiple_of(step * rows, rows), rows)
    k_all[own, :] = key
    v_all[own, :] = value
    scaled = query * jnp.asarray(score_scale, bf16)
    head_of = lax.broadcasted_iota(jnp.int32, (rows, width), 1) // HEAD_DIM
    lane = lax.broadcasted_iota(jnp.int32, (rows, LANES), 1)
    span = step - low_ref[first + seq, step] + 1
    for count in range(1, blocks + 1):

        @pl.when(span == count)
        def _(count=count):
            begin = pl.multiple_of((step - (count - 1)) * rows, rows)
            keys = k_all[pl.ds(begin, count * rows), :]
            values = v_all[pl.ds(begin, count * rows), :]
            mask = mask_ref[:, pl.ds(begin, count * rows)].astype(f32)
            result = jnp.zeros((rows, width), f32)
            stats = jnp.zeros((rows, LANES), f32)
            for head in range(heads):
                mine = head_of == head
                scores = nt(jnp.where(mine, scaled, jnp.zeros_like(scaled)), keys) + mask
                top = jnp.max(scores, axis=1, keepdims=True)
                weights = jnp.exp(scores - top)
                total = jnp.sum(weights, axis=1, keepdims=True)
                mixed = nn(weights.astype(bf16), values) * (1.0 / total)
                result = jnp.where(mine, mixed, result)
                stats = jnp.where(lane == head, top + jnp.log(total), stats)
            low_result = result.astype(bf16)
            out_ref[...] = low_result
            rest_ref[...] = (result - low_result.astype(f32)).astype(bf16)
            lse_ref[...] = jnp.transpose(stats)[: lse_ref.shape[0], :]


def attend(after, normed, first, count, entry, bias, cosine, sine, mask, low, rows):
    pieces, lows = entry
    _, seq_len, model_width = normed.shape
    width = bias.shape[1]
    blocks = seq_len // rows
    stat_rows = 8
    side = (pieces[0].shape[1] - 3 * width) // width

    def rows_of(columns):
        return pl.BlockSpec((None, rows, columns), lambda s, i, low: (first + s, i, 0))

    return staged(
        partial(attend_kernel, lows, first),
        after,
        low,
        [normed, bias, cosine, sine, mask, *[piece for piece in pieces for _ in range(3)]],
        [
            jax.ShapeDtypeStruct((3, count, seq_len, width), bf16),
            jax.ShapeDtypeStruct((count, seq_len, width), bf16),
            jax.ShapeDtypeStruct((count, seq_len, width), bf16),
            jax.ShapeDtypeStruct((count, stat_rows, seq_len), f32),
        ],
        "attend",
        grid=(count, blocks),
        in_specs=[
            rows_of(model_width),
            resident(bias),
            rows_of(LANES),
            rows_of(LANES),
            rows_of(seq_len),
            *[
                block_of(piece, (piece.shape[0], width), (0, side + which))
                for piece in pieces
                for which in range(3)
            ],
        ],
        out_specs=[
            pl.BlockSpec((3, None, rows, width), lambda s, i, low: (0, s, i, 0)),
            pl.BlockSpec((None, rows, width), lambda s, i, low: (s, i, 0)),
            pl.BlockSpec((None, rows, width), lambda s, i, low: (s, i, 0)),
            pl.BlockSpec((None, stat_rows, rows), lambda s, i, low: (s, 0, i)),
        ],
        scratch_shapes=[pltpu.VMEM((seq_len, width), bf16), pltpu.VMEM((seq_len, width), bf16)],
    )


def attend_back_kernel(
    lows, first, low_ref, q_ref, k_ref, v_ref, o_ref, rest_ref, g_ref, lse_ref, mask_ref, cos_ref, sin_ref, *refs
):
    *weights, out_ref, sum_ref, dk_all, dv_all, k_turned = refs
    seq, step = pl.program_id(0), pl.program_id(1)
    rows, width = q_ref.shape
    heads = width // HEAD_DIM
    seq_len = dk_all.shape[0]
    blocks = seq_len // rows

    @pl.when(step == 0)
    def _():
        dk_all[...] = jnp.zeros_like(dk_all)
        dv_all[...] = jnp.zeros_like(dv_all)
        k_turned[...] = jnp.transpose(k_ref[...])

    @pl.when((step == 0) & (seq == 0))
    def _():
        sum_ref[...] = jnp.zeros_like(sum_ref)

    scaled = q_ref[...] * jnp.asarray(score_scale, bf16)
    d_out = None
    for low, ref in zip(lows, weights):
        term = nt(g_ref[:, low : low + ref.shape[1]], ref[...])
        d_out = term if d_out is None else d_out + term
    d_out = d_out.astype(bf16)
    zero = jnp.zeros_like(d_out)
    head_of = lax.broadcasted_iota(jnp.int32, (rows, width), 1) // HEAD_DIM
    product = d_out.astype(f32) * (o_ref[...].astype(f32) + rest_ref[...].astype(f32))
    high = product.astype(bf16)
    rest = (product - high.astype(f32)).astype(bf16)
    row_of = lax.broadcasted_iota(jnp.int32, (8, width), 0)
    by_head = (lax.broadcasted_iota(jnp.int32, (8, width), 1) // HEAD_DIM == row_of).astype(bf16)
    delta = nt(by_head, high) + nt(by_head, rest)
    own = pl.ds(pl.multiple_of(step * rows, rows), rows)
    span = step - low_ref[first + seq, step] + 1
    for count in range(1, blocks + 1):

        @pl.when(span == count)
        def _(count=count):
            begin = pl.multiple_of((step - (count - 1)) * rows, rows)
            reach = pl.ds(begin, count * rows)
            keys = k_ref[reach, :]
            values = v_ref[reach, :]
            mask = mask_ref[reach, :].astype(f32)
            probs_side, scores_side, queries_down, d_outs_down, d_query = [], [], [], [], []
            for head in range(heads):
                mine = head_of == head
                query = jnp.where(mine, scaled, zero)
                d_mine = jnp.where(mine, d_out, zero)
                scores = nt(keys, query) + mask
                probs = jnp.exp(scores - lse_ref[head : head + 1, :])
                d_probs = nt(values, d_mine)
                d_scores = (probs * (d_probs - delta[head : head + 1, :])).astype(bf16)
                d_query.append(nn(k_turned[head * HEAD_DIM : (head + 1) * HEAD_DIM, reach], d_scores))
                probs_side.append(probs.astype(bf16))
                scores_side.append(d_scores)
                queries_down.append(query)
                d_outs_down.append(d_mine)
            dv_all[reach, :] += nn(
                jnp.concatenate(probs_side, axis=1), jnp.concatenate(d_outs_down, axis=0)
            )
            dk_all[reach, :] += nn(
                jnp.concatenate(scores_side, axis=1), jnp.concatenate(queries_down, axis=0)
            )
            cosine = widen(cos_ref[own, :], width)
            sine = widen(sin_ref[own, :], width)
            d_rot = jnp.transpose(jnp.concatenate(d_query, axis=0)) * score_scale
            low_query = rotate(d_rot, cosine, -sine).astype(bf16)
            out_ref[own, :width] = low_query
            sum_ref[0:1, :] += jnp.sum(low_query.astype(f32), axis=0, keepdims=True)

    @pl.when(step == blocks - 1)
    def _():
        cosine = widen(cos_ref[...], width)
        sine = widen(sin_ref[...], width)
        low_key = rotate(dk_all[...], cosine, -sine).astype(bf16)
        low_value = dv_all[...].astype(bf16)
        out_ref[:, width : 2 * width] = low_key
        out_ref[:, 2 * width :] = low_value
        sum_ref[1:2, :] += jnp.sum(low_key.astype(f32), axis=0, keepdims=True)
        sum_ref[2:3, :] += jnp.sum(low_value.astype(f32), axis=0, keepdims=True)


def attend_back(after, qkv, attended, rest, cot, first, count, exits, lse, mask, cosine, sine, low, rows):
    pieces, lows = exits
    _, seq_len, model_width = cot.shape
    width = qkv.shape[3]
    blocks = seq_len // rows
    stat_rows = lse.shape[1]
    units = pieces[0].shape[0] - width

    def whole_of(columns):
        return pl.BlockSpec((None, seq_len, columns), lambda s, i, low: (first + s, 0, 0))

    def rows_of(columns):
        return pl.BlockSpec((None, rows, columns), lambda s, i, low: (first + s, i, 0))

    return staged(
        partial(attend_back_kernel, lows, first),
        after,
        low,
        [qkv, qkv, qkv, attended, rest, cot, lse, mask, cosine, sine, *pieces],
        [
            jax.ShapeDtypeStruct((count, seq_len, 3 * width), bf16),
            jax.ShapeDtypeStruct((8, width), f32),
        ],
        "attend_back",
        grid=(count, blocks),
        in_specs=[
            pl.BlockSpec((None, None, rows, width), lambda s, i, low: (0, first + s, i, 0)),
            pl.BlockSpec((None, None, seq_len, width), lambda s, i, low: (1, first + s, 0, 0)),
            pl.BlockSpec((None, None, seq_len, width), lambda s, i, low: (2, first + s, 0, 0)),
            rows_of(width),
            rows_of(width),
            rows_of(model_width),
            pl.BlockSpec((None, stat_rows, rows), lambda s, i, low: (first + s, 0, i)),
            pl.BlockSpec((None, seq_len, rows), lambda s, i, low: (first + s, 0, i)),
            whole_of(LANES),
            whole_of(LANES),
            *[block_of(piece, (width, piece.shape[1]), (units // width, 0)) for piece in pieces],
        ],
        out_specs=[
            pl.BlockSpec((None, seq_len, 3 * width), lambda s, i, low: (s, 0, 0)),
            pl.BlockSpec((8, width), lambda s, i, low: (0, 0)),
        ],
        scratch_shapes=[
            pltpu.VMEM((seq_len, width), f32),
            pltpu.VMEM((seq_len, width), f32),
            pltpu.VMEM((width, seq_len), bf16),
        ],
    )


def gelu_kernel(lows, tick_ref, x_ref, bias_ref, *refs):
    *weights, hidden_ref, slope_ref = refs
    pre = bias_ref[...]
    for low, ref in zip(lows, weights):
        pre = pre + nn(x_ref[:, low : low + ref.shape[0]], ref[...])
    scale = (2.0 / math.pi) ** 0.5
    square = pre * pre
    half = 0.5 + 0.5 * jnp.tanh(pre * (scale + (scale * 0.044715) * square))
    hidden = pre * half
    hidden_ref[...] = hidden.astype(bf16)
    slope = half + hidden * (1.0 - half) * (2.0 * scale + (6.0 * scale * 0.044715) * square)
    slope_ref[...] = slope.astype(bf16)


def gelu_units(after, tick, normed, entry, bias, rows):
    pieces, lows = entry
    count, seq_len, model_width = normed.shape
    units = bias.shape[1]
    block = pl.BlockSpec((None, rows, units), lambda s, i, _: (s, i, 0))
    return staged(
        partial(gelu_kernel, lows),
        after,
        tick,
        [normed, bias, *pieces],
        [jax.ShapeDtypeStruct((count, seq_len, units), bf16)] * 2,
        "gelu_units",
        grid=(count, seq_len // rows),
        in_specs=[
                pl.BlockSpec((None, rows, model_width), lambda s, i, _: (s, i, 0)),
                resident(bias),
                *[block_of(piece, (piece.shape[0], units), (0, 0)) for piece in pieces],
            ],
        out_specs=[block, block],
    )


def out_kernel(lows, tick_ref, a_ref, h_ref, *refs):
    *weights, out_ref = refs
    units = h_ref.shape[1]
    for low, ref in zip(lows, weights):
        term = nn(h_ref[...], ref[:units, :]) + nn(a_ref[...], ref[units:, :])
        out_ref[:, low : low + ref.shape[1]] = term.astype(bf16)


def out_sums(after, tick, attended, hidden, exits, rows):
    pieces, lows = exits
    count, seq_len, width = attended.shape
    units = hidden.shape[2]
    model_width = sum(piece.shape[1] for piece in pieces)

    def rows_of(columns):
        return pl.BlockSpec((None, rows, columns), lambda s, i, _: (s, i, 0))

    return staged(
        partial(out_kernel, lows),
        after,
        tick,
        [attended, hidden, *pieces],
        jax.ShapeDtypeStruct((count, seq_len, model_width), bf16),
        "out_sums",
        grid=(count, seq_len // rows),
        in_specs=[rows_of(width), rows_of(units), *[resident(piece) for piece in pieces]],
        out_specs=rows_of(model_width),
    )


def from_relative(ref, rank, ranks, piece):
    return jnp.concatenate(
        [ref[:, pl.ds(pl.multiple_of((rank ^ j) * piece, piece), piece)] for j in range(ranks)], axis=1
    )


def back_rows_kernel(
    entry_lows, exit_lows, ranks, rank_ref, g_ref, slope_ref, c_ref, x_ref, norm_ref, *refs
):
    entry, exits = refs[: len(entry_lows)], refs[len(entry_lows) : len(entry_lows) + len(exit_lows)]
    hidden_ref, normed_ref, sum_ref, norm_sum_ref, norm_total = refs[-5:]
    units = slope_ref.shape[1]
    first = (pl.program_id(0) == 0) & (pl.program_id(1) == 0)
    final = (pl.program_id(0) == pl.num_programs(0) - 1) & (pl.program_id(1) == pl.num_programs(1) - 1)

    @pl.when(first)
    def _():
        sum_ref[...] = jnp.zeros_like(sum_ref)
        norm_total[...] = jnp.zeros_like(norm_total)

    total = None
    for low, ref in zip(exit_lows, exits):
        term = nt(g_ref[:, low : low + ref.shape[1]], ref[...])
        total = term if total is None else total + term
    d_hidden = (total * slope_ref[...].astype(f32)).astype(bf16)
    hidden_ref[...] = d_hidden
    sum_ref[0:1, :] += jnp.sum(d_hidden.astype(f32), axis=0, keepdims=True)
    for low, ref in zip(entry_lows, entry):
        here = slice(low, low + ref.shape[0])
        term = nt(d_hidden, ref[:, :units]) + nt(c_ref[...], ref[:, units:])
        normed_ref[:, here] = term.astype(bf16)
        unit = (x_ref[:, here].astype(f32) - norm_ref[1:2, here]) * (1.0 / norm_ref[0:1, here])
        norm_total[0:1, here] += jnp.sum(term * unit, axis=0, keepdims=True)
        norm_total[1:2, here] += jnp.sum(term, axis=0, keepdims=True)

    @pl.when(final)
    def _():
        norm_sum_ref[...] = from_relative(norm_total, rank_ref[0], ranks, norm_total.shape[1] // ranks)


def back_rows(after, rank, cot, slope, d_cat, normed, norm_rel, entry, exits, ranks, rows):
    pieces, lows = entry
    exit_pieces, exit_lows = exits
    count, seq_len, model_width = cot.shape
    units = slope.shape[2]

    def rows_of(columns):
        return pl.BlockSpec((None, rows, columns), lambda s, i, _: (s, i, 0))

    return staged(
        partial(back_rows_kernel, lows, exit_lows, ranks),
        after,
        rank,
        [cot, slope, d_cat, normed, norm_rel, *pieces, *exit_pieces],
        [
            jax.ShapeDtypeStruct((count, seq_len, units), bf16),
            jax.ShapeDtypeStruct((count, seq_len, model_width), bf16),
            jax.ShapeDtypeStruct((8, units), f32),
            jax.ShapeDtypeStruct((8, model_width), f32),
        ],
        "back_rows",
        grid=(count, seq_len // rows),
        in_specs=[
            rows_of(model_width),
            rows_of(units),
            rows_of(d_cat.shape[2]),
            rows_of(model_width),
            resident(norm_rel),
            *[resident(piece) for piece in pieces],
            *[block_of(piece, (units, piece.shape[1]), (0, 0)) for piece in exit_pieces],
        ],
        out_specs=[
            rows_of(units),
            rows_of(model_width),
            pl.BlockSpec((8, units), lambda s, i, _: (0, 0)),
            pl.BlockSpec((8, model_width), lambda s, i, _: (0, 0)),
        ],
        scratch_shapes=[pltpu.VMEM((8, model_width), f32)],
    )


def targets(ranks, parts):
    if ranks == 4:
        half = parts // 2
        return [(0, half), (half, parts)] + [(at * parts, (at + 1) * parts) for at in range(1, ranks)]
    return [(at * parts, (at + 1) * parts) for at in range(ranks)]


def turn_kernel(tick_ref, x_ref, h_ref, a_ref, normed_ref, exit_ref):
    units = h_ref.shape[1]
    normed_ref[...] = jnp.transpose(x_ref[...])
    exit_ref[:units, :] = jnp.transpose(h_ref[...])
    exit_ref[units:, :] = jnp.transpose(a_ref[...])


def turn(after, tick, normed, hidden, attended, rows):
    tokens, model_width = normed.shape
    units, width = hidden.shape[1], attended.shape[1]

    def rows_of(columns):
        return pl.BlockSpec((rows, columns), lambda i, _: (i, 0))

    def columns_of(height):
        return pl.BlockSpec((height, rows), lambda i, _: (0, i))

    return staged(
        turn_kernel,
        after,
        tick,
        [normed, hidden, attended],
        [
            jax.ShapeDtypeStruct((model_width, tokens), bf16),
            jax.ShapeDtypeStruct((units + width, tokens), bf16),
        ],
        "turn",
        grid=(tokens // rows,),
        in_specs=[rows_of(model_width), rows_of(units), rows_of(width)],
        out_specs=[columns_of(model_width), columns_of(units + width)],
    )


def grad_kernel(spans, tick_ref, left, right, *outs):
    step = pl.program_id(0)
    for (begin, end), out_ref in zip(spans, outs):

        @pl.when((step >= begin) & (step < end))
        def _(out_ref=out_ref):
            out_ref[...] = nn(left[...], right[...]).astype(bf16)


def rows_grad(after, tick, left, right, ranks, name):
    model_width, tokens = left.shape
    columns = right.shape[1]
    piece = model_width // ranks
    parts = max(2, piece // 256)
    block = piece // parts
    spans = targets(ranks, parts)

    def row_block(i, _):
        return ((ranks - 1 - i // parts) * parts + i % parts, 0)

    def target_block(begin, end):
        return lambda i, _: (jnp.clip(i - begin, 0, end - begin - 1), 0)

    return staged(
        partial(grad_kernel, spans),
        after,
        tick,
        [left, right],
        [jax.ShapeDtypeStruct(((end - begin) * block, columns), bf16) for begin, end in spans],
        name,
        grid=(ranks * parts,),
        in_specs=[pl.BlockSpec((block, tokens), row_block), resident(right)],
        out_specs=[pl.BlockSpec((block, columns), target_block(*span)) for span in spans],
    )


def columns_grad(after, tick, left, right, ranks, name):
    height = left.shape[0]
    tokens, model_width = right.shape
    piece = model_width // ranks
    parts = 2
    block = piece // parts
    spans = targets(ranks, parts)

    def column_block(i, _):
        return (0, (ranks - 1 - i // parts) * parts + i % parts)

    def target_block(begin, end):
        return lambda i, _: (0, jnp.clip(i - begin, 0, end - begin - 1))

    return staged(
        partial(grad_kernel, spans),
        after,
        tick,
        [left, right],
        [jax.ShapeDtypeStruct((height, (end - begin) * block), bf16) for begin, end in spans],
        name,
        grid=(ranks * parts,),
        in_specs=[resident(left), pl.BlockSpec((tokens, block), column_block)],
        out_specs=[pl.BlockSpec((height, block), target_block(*span)) for span in spans],
    )


def adam_step(moment_one, moment_two, gradient):
    moment_one = beta_first * moment_one + (1.0 - beta_first) * gradient
    moment_two = beta_second * moment_two + (1.0 - beta_second) * gradient * gradient
    first_fix = 1.0 - beta_first**STEP
    second_fix = 1.0 - beta_second**STEP
    update = moment_one / first_fix / (jnp.sqrt(moment_two / second_fix) + adam_eps)
    return update, moment_one, moment_two


def adam_update(moments, gradient):
    update, moment_one, moment_two = adam_step(moments[0], moments[1], gradient)
    return update, jnp.stack([moment_one, moment_two])


def adam_kernel(scale, tick_ref, moments_ref, *refs):
    *terms, update_ref, new_ref = refs
    gradient = terms[0][...].astype(f32)
    for term in terms[1:]:
        gradient = gradient + term[...].astype(f32)
    update, moment_one, moment_two = adam_step(moments_ref[0], moments_ref[1], gradient * scale)
    update_ref[...] = update
    new_ref[0] = moment_one
    new_ref[1] = moment_two


def adam_sum(after, tick, moments, terms, scale, row, column, parts):
    groups = parts if parts else 1
    height, width = moments.shape[-2:]
    rows = min(256, height)
    steps = height // rows
    if parts:
        moment_block = pl.BlockSpec((2, None, rows, width), lambda p, i, _: (0, p, i, 0))
        update_block = pl.BlockSpec((None, rows, width), lambda p, i, _: (p, i, 0))
    else:
        moment_block = pl.BlockSpec((2, rows, width), lambda p, i, _: (0, i, 0))
        update_block = pl.BlockSpec((rows, width), lambda p, i, _: (i, 0))
    term_block = pl.BlockSpec((rows, width), lambda p, i, _: (row // rows + i, column // width + p))
    return staged(
        partial(adam_kernel, scale),
        after,
        tick,
        [moments, *terms],
        [
            jax.ShapeDtypeStruct(moments.shape[1:], f32),
            jax.ShapeDtypeStruct(moments.shape, f32),
        ],
        "adam_sum",
        grid=(groups, steps),
        in_specs=[moment_block, *[term_block] * len(terms)],
        out_specs=[update_block, moment_block],
    )


def input_grad_kernel(ranks, rank_ref, x_ref, g_ref, norm_ref, d_ref, out_ref):
    piece = x_ref.shape[1] // ranks
    inputs = x_ref[...].astype(f32)
    centred = inputs - jnp.mean(inputs, axis=1, keepdims=True)
    variance = jnp.mean(centred * centred, axis=1, keepdims=True)
    inv_std = lax.rsqrt(variance + norm_eps)
    unit = centred * inv_std
    d_unit = from_relative(d_ref, rank_ref[0], ranks, piece).astype(f32) * norm_ref[0:1, :]
    mean_unit = jnp.mean(d_unit, axis=1, keepdims=True)
    mean_cross = jnp.mean(d_unit * unit, axis=1, keepdims=True)
    cot = g_ref[...].astype(f32)
    out_ref[...] = (cot + inv_std * (d_unit - mean_unit - unit * mean_cross)).astype(bf16)


def input_gradient(after, rank, tokens, cot_rows, norm_params, grads, ranks):
    count, rows, model_width = tokens.shape
    part = rows // 2
    block = pl.BlockSpec((None, part, model_width), lambda s, i, _: (s, i, 0))
    return staged(
        partial(input_grad_kernel, ranks),
        after,
        rank,
        [tokens, cot_rows, norm_params, grads],
        jax.ShapeDtypeStruct(tokens.shape, bf16),
        "input_grad",
        grid=(count, rows // part),
        in_specs=[block, block, resident(norm_params), block],
        out_specs=block,
    )


def output_kernel(ranks, rank_ref, x_ref, bias_ref, o_ref, out_ref):
    piece = x_ref.shape[1] // ranks
    branches = from_relative(o_ref, rank_ref[0], ranks, piece).astype(f32)
    total = x_ref[...].astype(f32) + branches + bias_ref[0:1, :] + bias_ref[1:2, :]
    out_ref[...] = total.astype(bf16)


def layer_output(after, rank, tokens, output_bias, outs, ranks):
    count, rows, model_width = tokens.shape
    block = pl.BlockSpec((None, rows, model_width), lambda s, _: (s, 0, 0))
    return staged(
        partial(output_kernel, ranks),
        after,
        rank,
        [tokens, output_bias, outs],
        jax.ShapeDtypeStruct(tokens.shape, bf16),
        "layer_output",
        grid=(count,),
        in_specs=[block, resident(output_bias), block],
        out_specs=block,
    )


def swap(array, distance):
    size = lax.axis_size("dp")
    return lax.ppermute(array, "dp", [(i, i ^ distance) for i in range(size)])


def plus(left, right):
    return (left.astype(f32) + right.astype(f32)).astype(bf16)


class Line:
    def __init__(self, tick):
        self.tick, self.pending = tick, []

    def wait(self, *arrays):
        self.pending += arrays

    def run(self, stage, *arguments):
        result = stage(self.pending, *arguments)
        self.pending = [jax.tree.leaves(result)[-1]]
        return result


def add_halves_kernel(axis, count, near_ref, far_ref, top_ref, bottom_ref, *refs):
    near_out, far_out = refs[count:]
    half = near_ref.shape[axis] // 2
    first = (slice(0, half), slice(None)) if axis == 0 else (slice(None), slice(0, half))
    second = (slice(half, None), slice(None)) if axis == 0 else (slice(None), slice(half, None))
    near_out[first] = near_ref[first]
    near_out[second] = plus(near_ref[second], bottom_ref[...])
    far_out[first] = plus(far_ref[first], top_ref[...])
    far_out[second] = far_ref[second]


def add_halves(after, near, far, top, bottom, axis):
    anywhere = pl.BlockSpec(memory_space=pl.ANY)
    shape = jax.ShapeDtypeStruct(near.shape, near.dtype)
    columns = near.shape[1]
    blocks = 1 if axis == 0 else 2
    rows = near.shape[0] // blocks
    whole = pl.BlockSpec((rows, columns), lambda i: (i, 0))
    part = pl.BlockSpec((top.shape[0] // blocks, top.shape[1]), lambda i: (i, 0))
    return pl.pallas_call(
        partial(add_halves_kernel, axis, len(after)),
        grid=(blocks,),
        in_specs=[whole, whole, part, part, *[anywhere] * len(after)],
        out_specs=[whole, whole],
        out_shape=[shape, shape],
        compiler_params=pltpu.CompilerParams(vmem_limit_bytes=VMEM * 1024 * 1024),
        cost_estimate=pl.CostEstimate(flops=10**6, bytes_accessed=10**6, transcendentals=0),
        name="add_halves",
    )(near, far, top, bottom, *after)


class Gather:
    def __init__(self, own, axis):
        self.size = lax.axis_size("dp")
        self.own, self.axis = own, axis
        self.sent = [swap(own, j) for j in ((1, 2) if self.size == 4 else range(1, self.size))]
        self.rest = []

    def forward(self, after):
        if self.size == 4:
            if after:
                self.sent = hold(self.sent, after)
            half = self.own.shape[self.axis] // 2
            near, far = self.sent
            top = lax.slice_in_dim(near, 0, half, axis=self.axis)
            bottom = lax.slice_in_dim(far, half, 2 * half, axis=self.axis)
            self.rest = [swap(top, 2), swap(bottom, 1)]

    def pieces(self):
        pieces = [self.own, *self.sent, *self.rest]
        lows, low = [], 0
        for piece in pieces:
            lows.append(low)
            low += piece.shape[self.axis]
        return pieces, tuple(lows)


class Scatter:
    def __init__(self, pieces, axis, after=()):
        self.size = lax.axis_size("dp")
        self.axis = axis
        if self.size == 4:
            *ends, self.far, self.near, self.own = pieces
            top, bottom = hold(ends, after) if after else ends
            self.ends = [top, bottom]
            self.first = [swap(top, 1), swap(bottom, 2)]
        else:
            self.ends = []
            self.own = pieces[-1]
            self.first = [swap(piece, self.size - 1 - at) for at, piece in enumerate(pieces[:-1])]

    def forward(self, after=()):
        self.sums = []
        if self.size != 4:
            return [self.own, *self.first]
        if after:
            near, far = add_halves(after, self.near, self.far, *self.first, self.axis)
        else:
            top, bottom = self.first
            half = self.near.shape[self.axis] // 2

            def halves(array):
                return [lax.slice_in_dim(array, at, at + half, axis=self.axis) for at in (0, half)]

            near, far = halves(self.near), halves(self.far)
            near = jnp.concatenate([near[0], plus(near[1], bottom)], axis=self.axis)
            far = jnp.concatenate([plus(far[0], top), far[1]], axis=self.axis)
        self.sums = [near, far]
        return [self.own, swap(near, 1), swap(far, 2)]


def sum_axis(array, axis, distances):
    size = lax.axis_size(axis)
    offsets = [0]
    for distance in distances:
        offsets += [offset + distance for offset in offsets]
    terms = [lax.ppermute(array, axis, [(i, i ^ offset) for i in range(size)]) for offset in offsets[1:]]
    terms = [array, *terms]
    while len(terms) > 1:
        terms = [left + right for left, right in zip(terms[::2], terms[1::2])]
    return terms[0]


def sum_rounds(axis):
    distances = [1 << bit for bit in range((lax.axis_size(axis) - 1).bit_length())]
    odd = len(distances) % 2
    rounds = [distances[:1]] if odd else []
    return rounds + [distances[at : at + 2] for at in range(odd, len(distances), 2)]


def body(
    tokens,
    cotangent,
    segments,
    valid_mask,
    norm_params,
    norm_moments,
    heads_weight,
    heads_moments,
    heads_bias,
    heads_bias_moments,
    merge_weight,
    merge_moments,
    expand_weight,
    expand_moments,
    expand_bias,
    expand_bias_moments,
    shrink_weight,
    shrink_moments,
    output_bias,
    output_bias_moments,
):
    ranks = lax.axis_size("dp")
    rank = lax.axis_index("dp")
    count, _, model_width = tokens.shape
    seq_len = segments.shape[1]
    width = heads_weight.shape[2]
    piece = model_width // ranks
    rows = min(256, seq_len)

    def relative(array):
        parts = [
            lax.dynamic_slice_in_dim(array, (rank ^ j) * piece, piece, array.ndim - 1) for j in range(ranks)
        ]
        return jnp.concatenate(parts, axis=-1)

    norm_rel = relative(norm_params)
    norm_gain, norm_shift = norm_rel[0], norm_rel[1]
    inputs = relative(tokens).astype(f32)
    cot_rows = relative(cotangent)
    row_mean = jnp.mean(inputs, axis=-1, keepdims=True)
    centred = inputs - row_mean
    variance = jnp.mean(centred * centred, axis=-1, keepdims=True)
    inv_std = lax.rsqrt(variance + norm_eps)
    unit = centred * inv_std
    normed_rows = (unit * norm_gain + norm_shift).astype(bf16)

    def gather_rows(array):
        return lax.all_gather(array, "tensor", axis=1, tiled=True)

    def scatter_rows(array):
        return lax.psum_scatter(array, "tensor", scatter_dimension=1, tiled=True)

    tick = segments[0, :1]
    line = Line(tick)
    rank_here = rank.reshape(1).astype(jnp.int32)
    normed = gather_rows(normed_rows)
    cot = gather_rows(cot_rows)

    entry_own = jnp.concatenate([expand_weight, *[heads_weight[c] for c in range(3)]], axis=1).astype(bf16)
    entry_gather = Gather(entry_own, 0)
    entry_gather.forward(())
    entry = entry_gather.pieces()
    exit_own = jnp.concatenate([shrink_weight, merge_weight], axis=0).astype(bf16)
    exit_gather = Gather(hold([exit_own], entry_gather.rest or entry_gather.sent)[0], 1)
    starts = jnp.stack([document_starts(segments[s]) for s in range(count)])
    cosine, sine = jax.vmap(rotary_tables)(starts)
    mask_rows, mask_columns = jax.vmap(masks)(starts, valid_mask)
    lows = starts[:, ::rows] // rows
    expand_row = expand_bias.reshape(1, -1)
    big = min(512, seq_len)
    units_local = expand_weight.shape[1]

    line.wait(mask_columns)
    qkv, attended, rest, lse = line.run(
        attend, normed, 0, count, entry, heads_bias, cosine, sine, mask_rows, lows, rows
    )
    exit_gather.forward([attended])
    exits = exit_gather.pieces()
    hidden, slope = line.run(gelu_units, tick, normed, entry, expand_row, big)
    partials = line.run(out_sums, tick, attended, hidden, exits, big)

    outs = scatter_rows(partials)

    def tokens_of(array):
        return array.reshape(-1, array.shape[-1])

    def adam(moments, terms, row=0, column=0, parts=0):
        return line.run(adam_sum, tick, moments, terms, 1.0 / seq_len, row, column, parts)

    normed_turned, exit_turned = line.run(
        turn, tick, tokens_of(normed), tokens_of(hidden), tokens_of(attended), rows
    )
    exit_parts = line.run(columns_grad, tick, exit_turned, tokens_of(cot), ranks, "exit_grad")
    exit_scatter = Scatter(exit_parts, 1)
    d_cat, bias_sums = line.run(
        attend_back, qkv, attended, rest, cot, 0, count, exits, lse, mask_columns, cosine, sine, lows, rows
    )
    exit_terms = exit_scatter.forward([d_cat])
    d_hidden, sums, hidden_sums, norm_part = line.run(
        back_rows, rank_here, cot, slope, d_cat, normed, norm_rel, entry, exits, ranks, big
    )
    sums = hold([sums], exit_terms[1:])[0]
    grads = scatter_rows(sums)
    line.wait(outs)
    column_sums = jnp.concatenate([norm_part[:2].reshape(-1), jnp.sum(cotangent.astype(f32), axis=(0, 1))])
    earlier, *later = sum_rounds("tensor")
    column_sums = sum_axis(column_sums, "tensor", earlier)
    expand_parts = line.run(rows_grad, tick, normed_turned, tokens_of(d_hidden), ranks, "expand_grad")
    expand_scatter = Scatter(expand_parts, 0)
    expand_terms = expand_scatter.forward()
    line.wait(column_sums)
    heads_parts = line.run(rows_grad, tick, normed_turned, tokens_of(d_cat), ranks, "heads_grad")
    heads_scatter = Scatter(heads_parts, 0, expand_scatter.first)
    heads_terms = heads_scatter.forward()
    line.wait(*heads_scatter.ends)
    shrink_upd, shrink_mom = adam(shrink_moments, exit_terms)
    merge_upd, merge_mom = adam(merge_moments, exit_terms, row=units_local)
    line.wait(*heads_scatter.first)
    output = line.run(layer_output, rank_here, tokens, output_bias, outs, ranks)
    expand_upd, expand_mom = adam(expand_moments, expand_terms)
    for distances in later:
        column_sums = hold([column_sums], [*heads_terms[1:], expand_upd])[0]
        column_sums = sum_axis(column_sums, "tensor", distances)
    input_grad = line.run(input_gradient, rank_here, tokens, cotangent, norm_params, grads, ranks)
    line.wait(column_sums)
    totals = jnp.concatenate([column_sums, bias_sums[:3].reshape(-1), hidden_sums[0]])
    totals = hold([totals], [input_grad])[0]
    for distances in sum_rounds("dp"):
        totals = sum_axis(totals, "dp", distances)
    heads_upd, heads_mom = adam(heads_moments, heads_terms, parts=3)
    norm_total = totals[: 2 * model_width].reshape(2, model_width)
    output_bias_total = totals[2 * model_width : 3 * model_width]
    bias_total = totals[3 * model_width :]
    heads_bias_total = bias_total[: 3 * width].reshape(3, width)
    expand_bias_total = bias_total[3 * width :]

    scale_back = 1.0 / seq_len
    norm_upd, norm_mom = adam_update(norm_moments, norm_total * scale_back)
    hbias_upd, hbias_mom = adam_update(heads_bias_moments, heads_bias_total * scale_back)
    ebias_upd, ebias_mom = adam_update(expand_bias_moments, expand_bias_total * scale_back)
    output_bias_grad = jnp.stack([output_bias_total, output_bias_total]) * scale_back
    obias_upd, obias_mom = adam_update(output_bias_moments, output_bias_grad)
    return (
        output,
        input_grad,
        norm_upd,
        norm_mom,
        heads_upd,
        heads_mom,
        hbias_upd,
        hbias_mom,
        merge_upd,
        merge_mom,
        expand_upd,
        expand_mom,
        ebias_upd,
        ebias_mom,
        shrink_upd,
        shrink_mom,
        obias_upd,
        obias_mom,
    )


def solution(mesh):
    placed = (
        P("dp", "tensor", None),
        P("dp", "tensor", None),
        P("dp", None),
        P("dp", None),
        P(),
        P(),
        P(None, "dp", "tensor"),
        P(None, None, "dp", "tensor"),
        P(None, "tensor"),
        P(None, None, "tensor"),
        P("tensor", "dp"),
        P(None, "tensor", "dp"),
        P("dp", "tensor"),
        P(None, "dp", "tensor"),
        P("tensor"),
        P(None, "tensor"),
        P("tensor", "dp"),
        P(None, "tensor", "dp"),
        P(),
        P(),
    )
    return jax.shard_map(
        body,
        mesh=mesh,
        in_specs=placed,
        out_specs=(placed[0], placed[0], P(), P(), *placed[6:18], P(), P()),
        check_vma=False,
    )
```

```python
import math
from functools import partial

import jax
import jax.numpy as jnp
from jax import lax
from jax.experimental import pallas as pl
from jax.experimental.pallas import tpu as pltpu
from jax.sharding import PartitionSpec as P

HEAD_DIM = 64
ROT = 32
STEP = 5
LANES = 128

norm_eps = 1e-05
beta_first = 0.9
beta_second = 0.95
adam_eps = 1e-08
masked_score = -1000000000.0
score_scale = HEAD_DIM ** (-0.5)
VMEM = 60

f32 = jnp.float32
bf16 = jnp.bfloat16


def document_starts(segment):
    token_index = jnp.arange(segment.shape[0], dtype=jnp.int32)
    doc_begins = jnp.concatenate([jnp.ones((1,), dtype=jnp.bool_), segment[1:] != segment[:-1]])
    return lax.cummax(jnp.where(doc_begins, token_index, 0), axis=0)


def rotary_tables(doc_start):
    seq_len = doc_start.shape[0]
    positions = (jnp.arange(seq_len, dtype=jnp.int32) - doc_start).astype(f32)
    half_rot = ROT // 2
    frequency = jnp.power(10000.0, -2.0 * jnp.arange(half_rot, dtype=f32) / ROT)
    flat = jnp.zeros((HEAD_DIM - ROT,), f32)
    copies = LANES // HEAD_DIM
    by_lane = jnp.tile(jnp.concatenate([frequency, frequency, flat]), copies)
    sign = jnp.where(jnp.arange(LANES) % HEAD_DIM < half_rot, -1.0, 1.0)
    angles = positions[:, None] * by_lane[None, :]
    return jnp.cos(angles), jnp.sin(angles) * sign[None, :]


def masks(doc_start, valid):
    index = jnp.arange(doc_start.shape[0], dtype=jnp.int32)

    def build(query, start, key, key_valid):
        allowed = (key >= start) & (key <= query) & ((key_valid > 0) | (key == query))
        return jnp.where(allowed, 0.0, masked_score).astype(bf16)

    rows = build(index[:, None], doc_start[:, None], index[None, :], valid[None, :])
    columns = build(index[None, :], doc_start[None, :], index[:, None], valid[:, None])
    return rows, columns


def rotate(values, cosine, sine):
    half_rot = ROT // 2
    width = values.shape[1]
    lane = lax.broadcasted_iota(jnp.int32, values.shape, 1) % HEAD_DIM
    ahead = pltpu.roll(values, width - half_rot, 1)
    behind = pltpu.roll(values, half_rot, 1)
    partner = jnp.where(lane < half_rot, ahead, behind)
    return values * cosine + partner * sine


def nt(left, right):
    return lax.dot_general(left, right, (((1,), (1,)), ((), ())), preferred_element_type=f32)


def nn(left, right):
    return lax.dot_general(left, right, (((1,), (0,)), ((), ())), preferred_element_type=f32)


def tn(left, right):
    return lax.dot_general(left, right, (((0,), (0,)), ((), ())), preferred_element_type=f32)


def widen(table, width):
    return jnp.concatenate([table] * (width // LANES), axis=1)


one = pl.Buffered(1)


def resident(array):
    zeros = (0,) * array.ndim
    return pl.BlockSpec(array.shape, lambda *_: zeros, pipeline_mode=one)


def block_of(array, shape, place):
    return pl.BlockSpec(shape, lambda *_: place, pipeline_mode=one)


def staged(
    kernel, after, first, inputs, out_shape, name, grid, in_specs, out_specs, scratch_shapes=(), flops=10**10
):
    def without(first_ref, *refs):
        kernel(first_ref, *refs[len(after) :])

    return pl.pallas_call(
        without,
        grid_spec=pltpu.PrefetchScalarGridSpec(
            num_scalar_prefetch=1,
            grid=grid,
            in_specs=[*[pl.BlockSpec(memory_space=pl.ANY)] * len(after), *in_specs],
            out_specs=out_specs,
            scratch_shapes=scratch_shapes,
        ),
        out_shape=out_shape,
        compiler_params=pltpu.CompilerParams(vmem_limit_bytes=VMEM * 1024 * 1024),
        cost_estimate=pl.CostEstimate(flops=flops, bytes_accessed=flops // 1000, transcendentals=0),
        name=name,
    )(first, *after, *inputs)


def hold(arrays, after):
    def kernel(*refs):
        pass

    anywhere = pl.BlockSpec(memory_space=pl.ANY)
    return pl.pallas_call(
        kernel,
        in_specs=[anywhere] * (len(arrays) + len(after)),
        out_specs=[anywhere] * len(arrays),
        out_shape=[jax.ShapeDtypeStruct(array.shape, array.dtype) for array in arrays],
        input_output_aliases={at: at for at in range(len(arrays))},
        cost_estimate=pl.CostEstimate(flops=1000, bytes_accessed=1000, transcendentals=0),
        name="hold",
    )(*arrays, *after)


def attend_kernel(lows, first, low_ref, x_ref, bias_ref, cos_ref, sin_ref, mask_ref, *refs):
    *weights, qkv_ref, out_ref, rest_ref, lse_ref, k_all, v_all = refs
    seq, step = pl.program_id(0), pl.program_id(1)
    rows, width = out_ref.shape
    heads = width // HEAD_DIM
    blocks = k_all.shape[0] // rows
    cosine = widen(cos_ref[...], width)
    sine = widen(sin_ref[...], width)
    triple = []
    for which in range(3):
        total = None
        for low, ref in zip(lows, weights[which::3]):
            term = nn(x_ref[:, low : low + ref.shape[0]], ref[...])
            total = term if total is None else total + term
        triple.append(total + bias_ref[which : which + 1, :])
    query = rotate(triple[0], cosine, sine).astype(bf16)
    key = rotate(triple[1], cosine, sine).astype(bf16)
    value = triple[2].astype(bf16)
    qkv_ref[0] = query
    qkv_ref[1] = key
    qkv_ref[2] = value
    own = pl.ds(pl.multiple_of(step * rows, rows), rows)
    k_all[own, :] = key
    v_all[own, :] = value
    scaled = query * jnp.asarray(score_scale, bf16)
    head_of = lax.broadcasted_iota(jnp.int32, (rows, width), 1) // HEAD_DIM
    lane = lax.broadcasted_iota(jnp.int32, (rows, LANES), 1)
    span = step - low_ref[first + seq, step] + 1
    for count in range(1, blocks + 1):

        @pl.when(span == count)
        def _(count=count):
            begin = pl.multiple_of((step - (count - 1)) * rows, rows)
            keys = k_all[pl.ds(begin, count * rows), :]
            values = v_all[pl.ds(begin, count * rows), :]
            mask = mask_ref[:, pl.ds(begin, count * rows)].astype(f32)
            result = jnp.zeros((rows, width), f32)
            stats = jnp.zeros((rows, LANES), f32)
            for head in range(heads):
                mine = head_of == head
                scores = nt(jnp.where(mine, scaled, jnp.zeros_like(scaled)), keys) + mask
                top = jnp.max(scores, axis=1, keepdims=True)
                weights = jnp.exp(scores - top)
                total = jnp.sum(weights, axis=1, keepdims=True)
                mixed = nn(weights.astype(bf16), values) * (1.0 / total)
                result = jnp.where(mine, mixed, result)
                stats = jnp.where(lane == head, top + jnp.log(total), stats)
            low_result = result.astype(bf16)
            out_ref[...] = low_result
            rest_ref[...] = (result - low_result.astype(f32)).astype(bf16)
            lse_ref[...] = jnp.transpose(stats)[: lse_ref.shape[0], :]


def attend(after, normed, first, count, entry, bias, cosine, sine, mask, low, rows):
    pieces, lows = entry
    _, seq_len, model_width = normed.shape
    width = bias.shape[1]
    blocks = seq_len // rows
    stat_rows = 8
    side = (pieces[0].shape[1] - 3 * width) // width

    def rows_of(columns):
        return pl.BlockSpec((None, rows, columns), lambda s, i, low: (first + s, i, 0))

    return staged(
        partial(attend_kernel, lows, first),
        after,
        low,
        [normed, bias, cosine, sine, mask, *[piece for piece in pieces for _ in range(3)]],
        [
            jax.ShapeDtypeStruct((3, count, seq_len, width), bf16),
            jax.ShapeDtypeStruct((count, seq_len, width), bf16),
            jax.ShapeDtypeStruct((count, seq_len, width), bf16),
            jax.ShapeDtypeStruct((count, stat_rows, seq_len), f32),
        ],
        "attend",
        grid=(count, blocks),
        in_specs=[
            rows_of(model_width),
            resident(bias),
            rows_of(LANES),
            rows_of(LANES),
            rows_of(seq_len),
            *[
                block_of(piece, (piece.shape[0], width), (0, side + which))
                for piece in pieces
                for which in range(3)
            ],
        ],
        out_specs=[
            pl.BlockSpec((3, None, rows, width), lambda s, i, low: (0, s, i, 0)),
            pl.BlockSpec((None, rows, width), lambda s, i, low: (s, i, 0)),
            pl.BlockSpec((None, rows, width), lambda s, i, low: (s, i, 0)),
            pl.BlockSpec((None, stat_rows, rows), lambda s, i, low: (s, 0, i)),
        ],
        scratch_shapes=[pltpu.VMEM((seq_len, width), bf16), pltpu.VMEM((seq_len, width), bf16)],
    )


def attend_back_kernel(
    lows, first, low_ref, q_ref, k_ref, v_ref, o_ref, rest_ref, g_ref, lse_ref, mask_ref, cos_ref, sin_ref, *refs
):
    *weights, out_ref, sum_ref, dk_all, dv_all, k_turned = refs
    seq, step = pl.program_id(0), pl.program_id(1)
    rows, width = q_ref.shape
    heads = width // HEAD_DIM
    seq_len = dk_all.shape[0]
    blocks = seq_len // rows

    @pl.when(step == 0)
    def _():
        dk_all[...] = jnp.zeros_like(dk_all)
        dv_all[...] = jnp.zeros_like(dv_all)
        k_turned[...] = jnp.transpose(k_ref[...])

    @pl.when((step == 0) & (seq == 0))
    def _():
        sum_ref[...] = jnp.zeros_like(sum_ref)

    scaled = q_ref[...] * jnp.asarray(score_scale, bf16)
    d_out = None
    for low, ref in zip(lows, weights):
        term = nt(g_ref[:, low : low + ref.shape[1]], ref[...])
        d_out = term if d_out is None else d_out + term
    d_out = d_out.astype(bf16)
    zero = jnp.zeros_like(d_out)
    head_of = lax.broadcasted_iota(jnp.int32, (rows, width), 1) // HEAD_DIM
    product = d_out.astype(f32) * (o_ref[...].astype(f32) + rest_ref[...].astype(f32))
    high = product.astype(bf16)
    rest = (product - high.astype(f32)).astype(bf16)
    row_of = lax.broadcasted_iota(jnp.int32, (8, width), 0)
    by_head = (lax.broadcasted_iota(jnp.int32, (8, width), 1) // HEAD_DIM == row_of).astype(bf16)
    delta = nt(by_head, high) + nt(by_head, rest)
    own = pl.ds(pl.multiple_of(step * rows, rows), rows)
    span = step - low_ref[first + seq, step] + 1
    for count in range(1, blocks + 1):

        @pl.when(span == count)
        def _(count=count):
            begin = pl.multiple_of((step - (count - 1)) * rows, rows)
            reach = pl.ds(begin, count * rows)
            keys = k_ref[reach, :]
            values = v_ref[reach, :]
            mask = mask_ref[reach, :].astype(f32)
            probs_side, scores_side, queries_down, d_outs_down, d_query = [], [], [], [], []
            for head in range(heads):
                mine = head_of == head
                query = jnp.where(mine, scaled, zero)
                d_mine = jnp.where(mine, d_out, zero)
                scores = nt(keys, query) + mask
                probs = jnp.exp(scores - lse_ref[head : head + 1, :])
                d_probs = nt(values, d_mine)
                d_scores = (probs * (d_probs - delta[head : head + 1, :])).astype(bf16)
                d_query.append(nn(k_turned[head * HEAD_DIM : (head + 1) * HEAD_DIM, reach], d_scores))
                probs_side.append(probs.astype(bf16))
                scores_side.append(d_scores)
                queries_down.append(query)
                d_outs_down.append(d_mine)
            dv_all[reach, :] += nn(
                jnp.concatenate(probs_side, axis=1), jnp.concatenate(d_outs_down, axis=0)
            )
            dk_all[reach, :] += nn(
                jnp.concatenate(scores_side, axis=1), jnp.concatenate(queries_down, axis=0)
            )
            cosine = widen(cos_ref[own, :], width)
            sine = widen(sin_ref[own, :], width)
            d_rot = jnp.transpose(jnp.concatenate(d_query, axis=0)) * score_scale
            low_query = rotate(d_rot, cosine, -sine).astype(bf16)
            out_ref[own, :width] = low_query
            sum_ref[0:1, :] += jnp.sum(low_query.astype(f32), axis=0, keepdims=True)

    @pl.when(step == blocks - 1)
    def _():
        cosine = widen(cos_ref[...], width)
        sine = widen(sin_ref[...], width)
        low_key = rotate(dk_all[...], cosine, -sine).astype(bf16)
        low_value = dv_all[...].astype(bf16)
        out_ref[:, width : 2 * width] = low_key
        out_ref[:, 2 * width :] = low_value
        sum_ref[1:2, :] += jnp.sum(low_key.astype(f32), axis=0, keepdims=True)
        sum_ref[2:3, :] += jnp.sum(low_value.astype(f32), axis=0, keepdims=True)


def attend_back(after, qkv, attended, rest, cot, first, count, exits, lse, mask, cosine, sine, low, rows):
    pieces, lows = exits
    _, seq_len, model_width = cot.shape
    width = qkv.shape[3]
    blocks = seq_len // rows
    stat_rows = lse.shape[1]
    units = pieces[0].shape[0] - width

    def whole_of(columns):
        return pl.BlockSpec((None, seq_len, columns), lambda s, i, low: (first + s, 0, 0))

    def rows_of(columns):
        return pl.BlockSpec((None, rows, columns), lambda s, i, low: (first + s, i, 0))

    return staged(
        partial(attend_back_kernel, lows, first),
        after,
        low,
        [qkv, qkv, qkv, attended, rest, cot, lse, mask, cosine, sine, *pieces],
        [
            jax.ShapeDtypeStruct((count, seq_len, 3 * width), bf16),
            jax.ShapeDtypeStruct((8, width), f32),
        ],
        "attend_back",
        grid=(count, blocks),
        in_specs=[
            pl.BlockSpec((None, None, rows, width), lambda s, i, low: (0, first + s, i, 0)),
            pl.BlockSpec((None, None, seq_len, width), lambda s, i, low: (1, first + s, 0, 0)),
            pl.BlockSpec((None, None, seq_len, width), lambda s, i, low: (2, first + s, 0, 0)),
            rows_of(width),
            rows_of(width),
            rows_of(model_width),
            pl.BlockSpec((None, stat_rows, rows), lambda s, i, low: (first + s, 0, i)),
            pl.BlockSpec((None, seq_len, rows), lambda s, i, low: (first + s, 0, i)),
            whole_of(LANES),
            whole_of(LANES),
            *[block_of(piece, (width, piece.shape[1]), (units // width, 0)) for piece in pieces],
        ],
        out_specs=[
            pl.BlockSpec((None, seq_len, 3 * width), lambda s, i, low: (s, 0, 0)),
            pl.BlockSpec((8, width), lambda s, i, low: (0, 0)),
        ],
        scratch_shapes=[
            pltpu.VMEM((seq_len, width), f32),
            pltpu.VMEM((seq_len, width), f32),
            pltpu.VMEM((width, seq_len), bf16),
        ],
    )


def gelu_kernel(lows, tick_ref, x_ref, bias_ref, *refs):
    *weights, hidden_ref, slope_ref = refs
    pre = bias_ref[...]
    for low, ref in zip(lows, weights):
        pre = pre + nn(x_ref[:, low : low + ref.shape[0]], ref[...])
    scale = (2.0 / math.pi) ** 0.5
    square = pre * pre
    half = 0.5 + 0.5 * jnp.tanh(pre * (scale + (scale * 0.044715) * square))
    hidden = pre * half
    hidden_ref[...] = hidden.astype(bf16)
    slope = half + hidden * (1.0 - half) * (2.0 * scale + (6.0 * scale * 0.044715) * square)
    slope_ref[...] = slope.astype(bf16)


def gelu_units(after, tick, normed, entry, bias, rows):
    pieces, lows = entry
    count, seq_len, model_width = normed.shape
    units = bias.shape[1]
    block = pl.BlockSpec((None, rows, units), lambda s, i, _: (s, i, 0))
    return staged(
        partial(gelu_kernel, lows),
        after,
        tick,
        [normed, bias, *pieces],
        [jax.ShapeDtypeStruct((count, seq_len, units), bf16)] * 2,
        "gelu_units",
        grid=(count, seq_len // rows),
        in_specs=[
                pl.BlockSpec((None, rows, model_width), lambda s, i, _: (s, i, 0)),
                resident(bias),
                *[block_of(piece, (piece.shape[0], units), (0, 0)) for piece in pieces],
            ],
        out_specs=[block, block],
    )


def out_kernel(lows, tick_ref, a_ref, h_ref, *refs):
    *weights, out_ref = refs
    units = h_ref.shape[1]
    for low, ref in zip(lows, weights):
        term = nn(h_ref[...], ref[:units, :]) + nn(a_ref[...], ref[units:, :])
        out_ref[:, low : low + ref.shape[1]] = term.astype(bf16)


def out_sums(after, tick, attended, hidden, exits, rows):
    pieces, lows = exits
    count, seq_len, width = attended.shape
    units = hidden.shape[2]
    model_width = sum(piece.shape[1] for piece in pieces)

    def rows_of(columns):
        return pl.BlockSpec((None, rows, columns), lambda s, i, _: (s, i, 0))

    return staged(
        partial(out_kernel, lows),
        after,
        tick,
        [attended, hidden, *pieces],
        jax.ShapeDtypeStruct((count, seq_len, model_width), bf16),
        "out_sums",
        grid=(count, seq_len // rows),
        in_specs=[rows_of(width), rows_of(units), *[resident(piece) for piece in pieces]],
        out_specs=rows_of(model_width),
    )


def from_relative(ref, rank, ranks, piece):
    return jnp.concatenate(
        [ref[:, pl.ds(pl.multiple_of((rank ^ j) * piece, piece), piece)] for j in range(ranks)], axis=1
    )


def back_rows_kernel(
    entry_lows, exit_lows, ranks, rank_ref, g_ref, slope_ref, c_ref, x_ref, norm_ref, *refs
):
    entry, exits = refs[: len(entry_lows)], refs[len(entry_lows) : len(entry_lows) + len(exit_lows)]
    hidden_ref, normed_ref, sum_ref, norm_sum_ref, norm_total = refs[-5:]
    units = slope_ref.shape[1]
    first = (pl.program_id(0) == 0) & (pl.program_id(1) == 0)
    final = (pl.program_id(0) == pl.num_programs(0) - 1) & (pl.program_id(1) == pl.num_programs(1) - 1)

    @pl.when(first)
    def _():
        sum_ref[...] = jnp.zeros_like(sum_ref)
        norm_total[...] = jnp.zeros_like(norm_total)

    total = None
    for low, ref in zip(exit_lows, exits):
        term = nt(g_ref[:, low : low + ref.shape[1]], ref[...])
        total = term if total is None else total + term
    d_hidden = (total * slope_ref[...].astype(f32)).astype(bf16)
    hidden_ref[...] = d_hidden
    sum_ref[0:1, :] += jnp.sum(d_hidden.astype(f32), axis=0, keepdims=True)
    for low, ref in zip(entry_lows, entry):
        here = slice(low, low + ref.shape[0])
        term = nt(d_hidden, ref[:, :units]) + nt(c_ref[...], ref[:, units:])
        normed_ref[:, here] = term.astype(bf16)
        unit = (x_ref[:, here].astype(f32) - norm_ref[1:2, here]) * (1.0 / norm_ref[0:1, here])
        norm_total[0:1, here] += jnp.sum(term * unit, axis=0, keepdims=True)
        norm_total[1:2, here] += jnp.sum(term, axis=0, keepdims=True)

    @pl.when(final)
    def _():
        norm_sum_ref[...] = from_relative(norm_total, rank_ref[0], ranks, norm_total.shape[1] // ranks)


def back_rows(after, rank, cot, slope, d_cat, normed, norm_rel, entry, exits, ranks, rows):
    pieces, lows = entry
    exit_pieces, exit_lows = exits
    count, seq_len, model_width = cot.shape
    units = slope.shape[2]

    def rows_of(columns):
        return pl.BlockSpec((None, rows, columns), lambda s, i, _: (s, i, 0))

    return staged(
        partial(back_rows_kernel, lows, exit_lows, ranks),
        after,
        rank,
        [cot, slope, d_cat, normed, norm_rel, *pieces, *exit_pieces],
        [
            jax.ShapeDtypeStruct((count, seq_len, units), bf16),
            jax.ShapeDtypeStruct((count, seq_len, model_width), bf16),
            jax.ShapeDtypeStruct((8, units), f32),
            jax.ShapeDtypeStruct((8, model_width), f32),
        ],
        "back_rows",
        grid=(count, seq_len // rows),
        in_specs=[
            rows_of(model_width),
            rows_of(units),
            rows_of(d_cat.shape[2]),
            rows_of(model_width),
            resident(norm_rel),
            *[resident(piece) for piece in pieces],
            *[block_of(piece, (units, piece.shape[1]), (0, 0)) for piece in exit_pieces],
        ],
        out_specs=[
            rows_of(units),
            rows_of(model_width),
            pl.BlockSpec((8, units), lambda s, i, _: (0, 0)),
            pl.BlockSpec((8, model_width), lambda s, i, _: (0, 0)),
        ],
        scratch_shapes=[pltpu.VMEM((8, model_width), f32)],
    )


def targets(ranks, parts):
    if ranks == 4:
        half = parts // 2
        return [(0, half), (half, parts)] + [(at * parts, (at + 1) * parts) for at in range(1, ranks)]
    return [(at * parts, (at + 1) * parts) for at in range(ranks)]


def turn_kernel(tick_ref, x_ref, h_ref, a_ref, normed_ref, exit_ref):
    units = h_ref.shape[1]
    normed_ref[...] = jnp.transpose(x_ref[...])
    exit_ref[:units, :] = jnp.transpose(h_ref[...])
    exit_ref[units:, :] = jnp.transpose(a_ref[...])


def turn(after, tick, normed, hidden, attended, rows):
    tokens, model_width = normed.shape
    units, width = hidden.shape[1], attended.shape[1]

    def rows_of(columns):
        return pl.BlockSpec((rows, columns), lambda i, _: (i, 0))

    def columns_of(height):
        return pl.BlockSpec((height, rows), lambda i, _: (0, i))

    return staged(
        turn_kernel,
        after,
        tick,
        [normed, hidden, attended],
        [
            jax.ShapeDtypeStruct((model_width, tokens), bf16),
            jax.ShapeDtypeStruct((units + width, tokens), bf16),
        ],
        "turn",
        grid=(tokens // rows,),
        in_specs=[rows_of(model_width), rows_of(units), rows_of(width)],
        out_specs=[columns_of(model_width), columns_of(units + width)],
    )


def grad_kernel(spans, tick_ref, left, right, *outs):
    step = pl.program_id(0)
    for (begin, end), out_ref in zip(spans, outs):

        @pl.when((step >= begin) & (step < end))
        def _(out_ref=out_ref):
            out_ref[...] = nn(left[...], right[...]).astype(bf16)


def rows_grad(after, tick, left, right, ranks, name):
    model_width, tokens = left.shape
    columns = right.shape[1]
    piece = model_width // ranks
    parts = max(2, piece // 256)
    block = piece // parts
    spans = targets(ranks, parts)

    def row_block(i, _):
        return ((ranks - 1 - i // parts) * parts + i % parts, 0)

    def target_block(begin, end):
        return lambda i, _: (jnp.clip(i - begin, 0, end - begin - 1), 0)

    return staged(
        partial(grad_kernel, spans),
        after,
        tick,
        [left, right],
        [jax.ShapeDtypeStruct(((end - begin) * block, columns), bf16) for begin, end in spans],
        name,
        grid=(ranks * parts,),
        in_specs=[pl.BlockSpec((block, tokens), row_block), resident(right)],
        out_specs=[pl.BlockSpec((block, columns), target_block(*span)) for span in spans],
    )


def columns_grad(after, tick, left, right, ranks, name):
    height = left.shape[0]
    tokens, model_width = right.shape
    piece = model_width // ranks
    parts = 2
    block = piece // parts
    spans = targets(ranks, parts)

    def column_block(i, _):
        return (0, (ranks - 1 - i // parts) * parts + i % parts)

    def target_block(begin, end):
        return lambda i, _: (0, jnp.clip(i - begin, 0, end - begin - 1))

    return staged(
        partial(grad_kernel, spans),
        after,
        tick,
        [left, right],
        [jax.ShapeDtypeStruct((height, (end - begin) * block), bf16) for begin, end in spans],
        name,
        grid=(ranks * parts,),
        in_specs=[resident(left), pl.BlockSpec((tokens, block), column_block)],
        out_specs=[pl.BlockSpec((height, block), target_block(*span)) for span in spans],
    )


def adam_step(moment_one, moment_two, gradient):
    moment_one = beta_first * moment_one + (1.0 - beta_first) * gradient
    moment_two = beta_second * moment_two + (1.0 - beta_second) * gradient * gradient
    first_fix = 1.0 - beta_first**STEP
    second_fix = 1.0 - beta_second**STEP
    update = moment_one / first_fix / (jnp.sqrt(moment_two / second_fix) + adam_eps)
    return update, moment_one, moment_two


def adam_update(moments, gradient):
    update, moment_one, moment_two = adam_step(moments[0], moments[1], gradient)
    return update, jnp.stack([moment_one, moment_two])


def adam_kernel(scale, tick_ref, moments_ref, *refs):
    *terms, update_ref, new_ref = refs
    gradient = terms[0][...].astype(f32)
    for term in terms[1:]:
        gradient = gradient + term[...].astype(f32)
    update, moment_one, moment_two = adam_step(moments_ref[0], moments_ref[1], gradient * scale)
    update_ref[...] = update
    new_ref[0] = moment_one
    new_ref[1] = moment_two


def adam_sum(after, tick, moments, terms, scale, row, column, parts):
    groups = parts if parts else 1
    height, width = moments.shape[-2:]
    rows = min(256, height)
    steps = height // rows
    if parts:
        moment_block = pl.BlockSpec((2, None, rows, width), lambda p, i, _: (0, p, i, 0))
        update_block = pl.BlockSpec((None, rows, width), lambda p, i, _: (p, i, 0))
    else:
        moment_block = pl.BlockSpec((2, rows, width), lambda p, i, _: (0, i, 0))
        update_block = pl.BlockSpec((rows, width), lambda p, i, _: (i, 0))
    term_block = pl.BlockSpec((rows, width), lambda p, i, _: (row // rows + i, column // width + p))
    return staged(
        partial(adam_kernel, scale),
        after,
        tick,
        [moments, *terms],
        [
            jax.ShapeDtypeStruct(moments.shape[1:], f32),
            jax.ShapeDtypeStruct(moments.shape, f32),
        ],
        "adam_sum",
        grid=(groups, steps),
        in_specs=[moment_block, *[term_block] * len(terms)],
        out_specs=[update_block, moment_block],
    )


def input_grad_kernel(ranks, rank_ref, x_ref, g_ref, norm_ref, d_ref, out_ref):
    piece = x_ref.shape[1] // ranks
    inputs = x_ref[...].astype(f32)
    centred = inputs - jnp.mean(inputs, axis=1, keepdims=True)
    variance = jnp.mean(centred * centred, axis=1, keepdims=True)
    inv_std = lax.rsqrt(variance + norm_eps)
    unit = centred * inv_std
    d_unit = from_relative(d_ref, rank_ref[0], ranks, piece).astype(f32) * norm_ref[0:1, :]
    mean_unit = jnp.mean(d_unit, axis=1, keepdims=True)
    mean_cross = jnp.mean(d_unit * unit, axis=1, keepdims=True)
    cot = g_ref[...].astype(f32)
    out_ref[...] = (cot + inv_std * (d_unit - mean_unit - unit * mean_cross)).astype(bf16)


def input_gradient(after, rank, tokens, cot_rows, norm_params, grads, ranks):
    count, rows, model_width = tokens.shape
    part = rows // 2
    block = pl.BlockSpec((None, part, model_width), lambda s, i, _: (s, i, 0))
    return staged(
        partial(input_grad_kernel, ranks),
        after,
        rank,
        [tokens, cot_rows, norm_params, grads],
        jax.ShapeDtypeStruct(tokens.shape, bf16),
        "input_grad",
        grid=(count, rows // part),
        in_specs=[block, block, resident(norm_params), block],
        out_specs=block,
    )


def output_kernel(ranks, rank_ref, x_ref, bias_ref, o_ref, out_ref):
    piece = x_ref.shape[1] // ranks
    branches = from_relative(o_ref, rank_ref[0], ranks, piece).astype(f32)
    total = x_ref[...].astype(f32) + branches + bias_ref[0:1, :] + bias_ref[1:2, :]
    out_ref[...] = total.astype(bf16)


def layer_output(after, rank, tokens, output_bias, outs, ranks):
    count, rows, model_width = tokens.shape
    block = pl.BlockSpec((None, rows, model_width), lambda s, _: (s, 0, 0))
    return staged(
        partial(output_kernel, ranks),
        after,
        rank,
        [tokens, output_bias, outs],
        jax.ShapeDtypeStruct(tokens.shape, bf16),
        "layer_output",
        grid=(count,),
        in_specs=[block, resident(output_bias), block],
        out_specs=block,
    )


def swap(array, distance):
    size = lax.axis_size("dp")
    return lax.ppermute(array, "dp", [(i, i ^ distance) for i in range(size)])


def plus(left, right):
    return (left.astype(f32) + right.astype(f32)).astype(bf16)


class Line:
    def __init__(self, tick):
        self.tick, self.pending = tick, []

    def wait(self, *arrays):
        self.pending += arrays

    def run(self, stage, *arguments):
        result = stage(self.pending, *arguments)
        self.pending = [jax.tree.leaves(result)[-1]]
        return result


def add_halves_kernel(axis, count, near_ref, far_ref, top_ref, bottom_ref, *refs):
    near_out, far_out = refs[count:]
    half = near_ref.shape[axis] // 2
    first = (slice(0, half), slice(None)) if axis == 0 else (slice(None), slice(0, half))
    second = (slice(half, None), slice(None)) if axis == 0 else (slice(None), slice(half, None))
    near_out[first] = near_ref[first]
    near_out[second] = plus(near_ref[second], bottom_ref[...])
    far_out[first] = plus(far_ref[first], top_ref[...])
    far_out[second] = far_ref[second]


def add_halves(after, near, far, top, bottom, axis):
    anywhere = pl.BlockSpec(memory_space=pl.ANY)
    shape = jax.ShapeDtypeStruct(near.shape, near.dtype)
    columns = near.shape[1]
    blocks = 1 if axis == 0 else 2
    rows = near.shape[0] // blocks
    whole = pl.BlockSpec((rows, columns), lambda i: (i, 0))
    part = pl.BlockSpec((top.shape[0] // blocks, top.shape[1]), lambda i: (i, 0))
    return pl.pallas_call(
        partial(add_halves_kernel, axis, len(after)),
        grid=(blocks,),
        in_specs=[whole, whole, part, part, *[anywhere] * len(after)],
        out_specs=[whole, whole],
        out_shape=[shape, shape],
        compiler_params=pltpu.CompilerParams(vmem_limit_bytes=VMEM * 1024 * 1024),
        cost_estimate=pl.CostEstimate(flops=10**6, bytes_accessed=10**6, transcendentals=0),
        name="add_halves",
    )(near, far, top, bottom, *after)


class Gather:
    def __init__(self, own, axis):
        self.size = lax.axis_size("dp")
        self.own, self.axis = own, axis
        self.sent = [swap(own, j) for j in ((1, 2) if self.size == 4 else range(1, self.size))]
        self.rest = []

    def forward(self, after):
        if self.size == 4:
            if after:
                self.sent = hold(self.sent, after)
            half = self.own.shape[self.axis] // 2
            near, far = self.sent
            top = lax.slice_in_dim(near, 0, half, axis=self.axis)
            bottom = lax.slice_in_dim(far, half, 2 * half, axis=self.axis)
            self.rest = [swap(top, 2), swap(bottom, 1)]

    def pieces(self):
        pieces = [self.own, *self.sent, *self.rest]
        lows, low = [], 0
        for piece in pieces:
            lows.append(low)
            low += piece.shape[self.axis]
        return pieces, tuple(lows)


class Scatter:
    def __init__(self, pieces, axis, after=()):
        self.size = lax.axis_size("dp")
        self.axis = axis
        if self.size == 4:
            *ends, self.far, self.near, self.own = pieces
            top, bottom = hold(ends, after) if after else ends
            self.ends = [top, bottom]
            self.first = [swap(top, 1), swap(bottom, 2)]
        else:
            self.ends = []
            self.own = pieces[-1]
            self.first = [swap(piece, self.size - 1 - at) for at, piece in enumerate(pieces[:-1])]

    def forward(self, after=()):
        self.sums = []
        if self.size != 4:
            return [self.own, *self.first]
        if after:
            near, far = add_halves(after, self.near, self.far, *self.first, self.axis)
        else:
            top, bottom = self.first
            half = self.near.shape[self.axis] // 2

            def halves(array):
                return [lax.slice_in_dim(array, at, at + half, axis=self.axis) for at in (0, half)]

            near, far = halves(self.near), halves(self.far)
            near = jnp.concatenate([near[0], plus(near[1], bottom)], axis=self.axis)
            far = jnp.concatenate([plus(far[0], top), far[1]], axis=self.axis)
        self.sums = [near, far]
        return [self.own, swap(near, 1), swap(far, 2)]


def sum_axis(array, axis, distances):
    size = lax.axis_size(axis)
    offsets = [0]
    for distance in distances:
        offsets += [offset + distance for offset in offsets]
    terms = [lax.ppermute(array, axis, [(i, i ^ offset) for i in range(size)]) for offset in offsets[1:]]
    terms = [array, *terms]
    while len(terms) > 1:
        terms = [left + right for left, right in zip(terms[::2], terms[1::2])]
    return terms[0]


def sum_rounds(axis):
    distances = [1 << bit for bit in range((lax.axis_size(axis) - 1).bit_length())]
    odd = len(distances) % 2
    rounds = [distances[:1]] if odd else []
    return rounds + [distances[at : at + 2] for at in range(odd, len(distances), 2)]


def body(
    tokens,
    cotangent,
    segments,
    valid_mask,
    norm_params,
    norm_moments,
    heads_weight,
    heads_moments,
    heads_bias,
    heads_bias_moments,
    merge_weight,
    merge_moments,
    expand_weight,
    expand_moments,
    expand_bias,
    expand_bias_moments,
    shrink_weight,
    shrink_moments,
    output_bias,
    output_bias_moments,
):
    ranks = lax.axis_size("dp")
    rank = lax.axis_index("dp")
    count, _, model_width = tokens.shape
    seq_len = segments.shape[1]
    width = heads_weight.shape[2]
    piece = model_width // ranks
    rows = min(256, seq_len)

    def relative(array):
        parts = [
            lax.dynamic_slice_in_dim(array, (rank ^ j) * piece, piece, array.ndim - 1) for j in range(ranks)
        ]
        return jnp.concatenate(parts, axis=-1)

    norm_rel = relative(norm_params)
    norm_gain, norm_shift = norm_rel[0], norm_rel[1]
    inputs = relative(tokens).astype(f32)
    cot_rows = relative(cotangent)
    row_mean = jnp.mean(inputs, axis=-1, keepdims=True)
    centred = inputs - row_mean
    variance = jnp.mean(centred * centred, axis=-1, keepdims=True)
    inv_std = lax.rsqrt(variance + norm_eps)
    unit = centred * inv_std
    normed_rows = (unit * norm_gain + norm_shift).astype(bf16)

    def gather_rows(array):
        return lax.all_gather(array, "tensor", axis=1, tiled=True)

    def scatter_rows(array):
        return lax.psum_scatter(array, "tensor", scatter_dimension=1, tiled=True)

    tick = segments[0, :1]
    line = Line(tick)
    rank_here = rank.reshape(1).astype(jnp.int32)
    normed = gather_rows(normed_rows)
    cot = gather_rows(cot_rows)

    entry_own = jnp.concatenate([expand_weight, *[heads_weight[c] for c in range(3)]], axis=1).astype(bf16)
    entry_gather = Gather(entry_own, 0)
    entry_gather.forward(())
    entry = entry_gather.pieces()
    exit_own = jnp.concatenate([shrink_weight, merge_weight], axis=0).astype(bf16)
    exit_gather = Gather(hold([exit_own], entry_gather.rest or entry_gather.sent)[0], 1)
    starts = jnp.stack([document_starts(segments[s]) for s in range(count)])
    cosine, sine = jax.vmap(rotary_tables)(starts)
    mask_rows, mask_columns = jax.vmap(masks)(starts, valid_mask)
    lows = starts[:, ::rows] // rows
    expand_row = expand_bias.reshape(1, -1)
    big = min(512, seq_len)
    units_local = expand_weight.shape[1]

    line.wait(mask_columns)
    qkv, attended, rest, lse = line.run(
        attend, normed, 0, count, entry, heads_bias, cosine, sine, mask_rows, lows, rows
    )
    exit_gather.forward([attended])
    exits = exit_gather.pieces()
    hidden, slope = line.run(gelu_units, tick, normed, entry, expand_row, big)
    partials = line.run(out_sums, tick, attended, hidden, exits, big)

    outs = scatter_rows(partials)

    def tokens_of(array):
        return array.reshape(-1, array.shape[-1])

    def adam(moments, terms, row=0, column=0, parts=0):
        return line.run(adam_sum, tick, moments, terms, 1.0 / seq_len, row, column, parts)

    normed_turned, exit_turned = line.run(
        turn, tick, tokens_of(normed), tokens_of(hidden), tokens_of(attended), rows
    )
    exit_parts = line.run(columns_grad, tick, exit_turned, tokens_of(cot), ranks, "exit_grad")
    exit_scatter = Scatter(exit_parts, 1)
    d_cat, bias_sums = line.run(
        attend_back, qkv, attended, rest, cot, 0, count, exits, lse, mask_columns, cosine, sine, lows, rows
    )
    exit_terms = exit_scatter.forward([d_cat])
    d_hidden, sums, hidden_sums, norm_part = line.run(
        back_rows, rank_here, cot, slope, d_cat, normed, norm_rel, entry, exits, ranks, big
    )
    sums = hold([sums], exit_terms[1:])[0]
    grads = scatter_rows(sums)
    line.wait(outs)
    column_sums = jnp.concatenate([norm_part[:2].reshape(-1), jnp.sum(cotangent.astype(f32), axis=(0, 1))])
    earlier, *later = sum_rounds("tensor")
    column_sums = sum_axis(column_sums, "tensor", earlier)
    expand_parts = line.run(rows_grad, tick, normed_turned, tokens_of(d_hidden), ranks, "expand_grad")
    expand_scatter = Scatter(expand_parts, 0)
    expand_terms = expand_scatter.forward()
    line.wait(column_sums)
    heads_parts = line.run(rows_grad, tick, normed_turned, tokens_of(d_cat), ranks, "heads_grad")
    heads_scatter = Scatter(heads_parts, 0, expand_scatter.first)
    heads_terms = heads_scatter.forward()
    line.wait(*heads_scatter.ends)
    shrink_upd, shrink_mom = adam(shrink_moments, exit_terms)
    merge_upd, merge_mom = adam(merge_moments, exit_terms, row=units_local)
    line.wait(*heads_scatter.first)
    output = line.run(layer_output, rank_here, tokens, output_bias, outs, ranks)
    expand_upd, expand_mom = adam(expand_moments, expand_terms)
    input_grad = line.run(input_gradient, rank_here, tokens, cotangent, norm_params, grads, ranks)
    (column_sums,) = hold([column_sums], [input_grad])
    for distances in later:
        column_sums = sum_axis(column_sums, "tensor", distances)
    totals = jnp.concatenate([column_sums, bias_sums[:3].reshape(-1), hidden_sums[0]])
    for distances in sum_rounds("dp"):
        totals = sum_axis(totals, "dp", distances)
    heads_upd, heads_mom = adam(heads_moments, heads_terms, parts=3)
    norm_total = totals[: 2 * model_width].reshape(2, model_width)
    output_bias_total = totals[2 * model_width : 3 * model_width]
    bias_total = totals[3 * model_width :]
    heads_bias_total = bias_total[: 3 * width].reshape(3, width)
    expand_bias_total = bias_total[3 * width :]

    scale_back = 1.0 / seq_len
    norm_upd, norm_mom = adam_update(norm_moments, norm_total * scale_back)
    hbias_upd, hbias_mom = adam_update(heads_bias_moments, heads_bias_total * scale_back)
    ebias_upd, ebias_mom = adam_update(expand_bias_moments, expand_bias_total * scale_back)
    output_bias_grad = jnp.stack([output_bias_total, output_bias_total]) * scale_back
    obias_upd, obias_mom = adam_update(output_bias_moments, output_bias_grad)
    return (
        output,
        input_grad,
        norm_upd,
        norm_mom,
        heads_upd,
        heads_mom,
        hbias_upd,
        hbias_mom,
        merge_upd,
        merge_mom,
        expand_upd,
        expand_mom,
        ebias_upd,
        ebias_mom,
        shrink_upd,
        shrink_mom,
        obias_upd,
        obias_mom,
    )


def solution(mesh):
    placed = (
        P("dp", "tensor", None),
        P("dp", "tensor", None),
        P("dp", None),
        P("dp", None),
        P(),
        P(),
        P(None, "dp", "tensor"),
        P(None, None, "dp", "tensor"),
        P(None, "tensor"),
        P(None, None, "tensor"),
        P("tensor", "dp"),
        P(None, "tensor", "dp"),
        P("dp", "tensor"),
        P(None, "dp", "tensor"),
        P("tensor"),
        P(None, "tensor"),
        P("tensor", "dp"),
        P(None, "tensor", "dp"),
        P(),
        P(),
    )
    return jax.shard_map(
        body,
        mesh=mesh,
        in_specs=placed,
        out_specs=(placed[0], placed[0], P(), P(), *placed[6:18], P(), P()),
        check_vma=False,
    )
```
